32 devices in a mesh: seq: 8 (over y, x, core), rows: 4 (over z).
Axes of the slice: x: 2, y: 2, z: 4, core: 2. Of those that a mesh axis runs over, the one named last changes fastest.
Arguments:
- tokens: bfloat16 [4, 3072, 768], P('rows', 'seq'), may hold values from -6 to 6
- segment_ids: int32 [4, 3072], P('rows', 'seq'), may hold values from 0 to 8, as said below
- valid_tokens: int32 [4, 3072], P('rows', 'seq'), may hold values from 0 to 1, as said below
- q_weight: bfloat16 [4, 192, 192], replicated, may hold values from -0.625 to 0.625
- k_weight: bfloat16 [4, 192, 192], replicated, may hold values from -0.625 to 0.625
- v_weight: bfloat16 [4, 192, 192], replicated, may hold values from -0.4375 to 0.4375
- out_weight: bfloat16 [768, 768], replicated, may hold values from -0.625 to 0.625
- gain_one: float32 [768], replicated, may hold values from 0.5 to 1.5
- bias_one: float32 [768], replicated, may hold values from -1.2 to 1.2
- ffn_in: bfloat16 [4, 192, 768], replicated, may hold values from -0.4375 to 0.4375
- ffn_out: bfloat16 [4, 768, 192], replicated, may hold values from -0.21875 to 0.21875
- gain_two: float32 [768], replicated, may hold values from 0.5 to 1.5
- bias_two: float32 [768], replicated, may hold values from -1.2 to 1.2
- cotangent: float32 [4, 3072, 768], P('rows', 'seq'), may hold values from -6 to 6
Outputs:
- mixed: float32 [4, 3072, 768], P('rows', 'seq')
- grad_tokens: float32 [4, 3072, 768], P('rows', 'seq')
- grad_q_weight: float32 [4, 192, 192], replicated
- grad_k_weight: float32 [4, 192, 192], replicated
- grad_v_weight: float32 [4, 192, 192], replicated
- grad_out_weight: float32 [768, 768], replicated
- grad_gain_one: float32 [768], replicated
- grad_bias_one: float32 [768], replicated
- grad_ffn_in: float32 [4, 192, 768], replicated
- grad_ffn_out: float32 [4, 768, 192], replicated
- grad_gain_two: float32 [768], replicated
- grad_bias_two: float32 [768], replicated
The draws below stay inside these ranges and needn't reach their ends.
Inputs may be any that keep to these rules, and one draw needn't show every extreme that they name: `segment_ids`: segment numbers never fall along a row. `valid_tokens`: padding (0) stands only at the end of a row, and every row has some.
All inputs are finite; a program needn't handle non-finite values.
Results may differ from the reference program's by a relative error of at most 0.018.
The reference program's roundings to bfloat16 on the way count: a program that leaves them out, or rounds other values in their place, can miss the bound.
Values may be sent and summed in bfloat16 or wider, within the bound.
No kernel may reach another device: no remote copies, remote signals or barrier semaphores. Data moves between devices by JAX's collectives and lax.ppermute only.
A program may use at most 192 MiB of HBM per device.

```python
import math
import jax
import jax.numpy as jnp
from jax import lax

D = 768
HEADS = 12
GROUPS = 4
SEG_DEV = 384
DG = 192
FG = 768
LENGTH = 3072
ROWS = 4


def draw_segment_ids(key, part):
    key = jax.random.fold_in(key, 11)
    key_start, key_end, key_front, key_back = jax.random.split(key, 4)
    long_start = jax.random.randint(key_start, (ROWS, 1), SEG_DEV // 4, SEG_DEV)
    long_end = LENGTH - jax.random.randint(key_end, (ROWS, 1), SEG_DEV // 4, SEG_DEV)
    front_cuts = jax.random.randint(key_front, (ROWS, 3), 1, SEG_DEV // 4)
    back_cuts = long_end + jax.random.randint(key_back, (ROWS, 3), 1, SEG_DEV // 4)
    bounds = jnp.concatenate([front_cuts, long_start, long_end, back_cuts], axis=1)
    positions = jnp.arange(LENGTH, dtype=jnp.int32)
    above = positions[None, :, None] >= bounds[:, None, :]
    return jnp.sum(above.astype(jnp.int32), axis=2).astype(jnp.int32)


def draw_valid_tokens(key, part):
    key = jax.random.fold_in(key, 12)
    padding = jax.random.randint(key, (ROWS, 1), 1, SEG_DEV // 2)
    positions = jnp.arange(LENGTH, dtype=jnp.int32)[None, :]
    return (positions < LENGTH - padding).astype(jnp.int32)


def block_levels(own_key, shape, cuts, least, top_value):
    def one(dim, shards_of):
        steps = jax.random.uniform(jax.random.fold_in(jax.random.fold_in(own_key, 6), dim), (shards_of,), jnp.float32, least / len(cuts), top_value / len(cuts))
        return jnp.repeat(jnp.exp(steps), shape[dim] // shards_of).reshape((-1,) + (1,) * (len(shape) - dim - 1))

    level = one(*cuts[0])
    for cut in cuts[1:]:
        level = level * one(*cut)
    return level


def gaussian(rng, shape, scale, limit, shards=(), held_as=jnp.bfloat16):
    level = block_levels(rng, shape, shards, -0.22, 0.18) if shards else 1.0
    drawn = jax.random.normal(rng, shape, jnp.float32) * scale * level
    return jnp.minimum(jnp.maximum(drawn, -limit), limit).astype(held_as)


def setup_inputs(seed: int = 0) -> dict:
    seeds = jax.random.split(jax.random.key(seed), 15)
    return {
        "tokens": gaussian(seeds[0], (ROWS, LENGTH, D), 1.0, 6.0, ((0, 4), (1, 8))),
        "segment_ids": draw_segment_ids(jax.random.fold_in(seeds[14], 71), 0),
        "valid_tokens": draw_valid_tokens(jax.random.fold_in(seeds[14], 71), 0),
        "q_weight": gaussian(seeds[3], (GROUPS, DG, DG), (DG * 2 // 5) ** -0.5, 0.625),
        "k_weight": gaussian(seeds[4], (GROUPS, DG, DG), (DG * 2 // 5) ** -0.5, 0.625),
        "v_weight": gaussian(seeds[5], (GROUPS, DG, DG), DG ** -0.5, 0.4375),
        "out_weight": gaussian(seeds[6], (D, D), (D // 8) ** -0.5, 0.625),
        "gain_one": jnp.clip(1.0 + 0.1 * jax.random.normal(seeds[7], (D,), jnp.float32), 0.5, 1.5),
        "bias_one": gaussian(seeds[8], (D,), 0.3, 1.2, (), jnp.float32),
        "ffn_in": gaussian(seeds[9], (GROUPS, DG, FG), DG ** -0.5, 0.4375),
        "ffn_out": gaussian(seeds[10], (GROUPS, FG, DG), FG ** -0.5, 0.21875),
        "gain_two": jnp.clip(1.0 + 0.1 * jax.random.normal(seeds[11], (D,), jnp.float32), 0.5, 1.5),
        "bias_two": gaussian(seeds[12], (D,), 0.3, 1.2, (), jnp.float32),
        "cotangent": gaussian(seeds[13], (ROWS, LENGTH, D), 1.0, 6.0, ((0, 4), (1, 8)), jnp.float32),
    }


masked_score = -1000000000.0
highest = lax.Precision.HIGHEST

@jax.custom_vjp
def low(v):
    return lax.optimization_barrier(v.astype(jnp.bfloat16)).astype(jnp.float32)

@jax.custom_vjp
def low_back(v):
    return v

def low_keep(v):
    return (low(v), None)

def low_pass(kept, grad):
    return (grad,)

def back_keep(v):
    return (v, None)

def back_low(kept, grad):
    return (low(grad),)
low.defvjp(low_keep, low_pass)
low_back.defvjp(back_keep, back_low)

def grouped(inputs, weight):
    groups, width_in, width_out = weight.shape
    leading = inputs.shape[:-1]
    split = inputs.reshape(leading + (groups, width_in))
    output = jnp.einsum('...gi,gio->...go', split, weight, precision=highest)
    return output.reshape(leading + (groups * width_out,))

def layer_norm(values, gain, shift):
    center = values - lax.optimization_barrier(jnp.mean(values, axis=-1, keepdims=True))
    spread = lax.optimization_barrier(jnp.mean(center * center, axis=-1, keepdims=True))
    return center * lax.rsqrt(spread + 1e-06) * gain + shift

def attend_row(row_inputs):
    query_row, key_row, value_row, query_code, key_code = row_inputs
    head_size = D // HEADS
    block_rows = math.gcd(LENGTH, 512)
    query_blocks = query_row.reshape(LENGTH // block_rows, block_rows, HEADS, head_size)
    code_blocks = query_code.reshape(LENGTH // block_rows, block_rows)

    def one_block(block_inputs):
        query_blk, code_blk = block_inputs
        scores = jnp.einsum('qhd,khd->qhk', query_blk, key_row, precision=highest) * head_size ** (-0.5)
        scores = low_back(scores)
        allowed = code_blk[:, None, None] == key_code[None, None, :]
        scores = jnp.where(allowed, scores, masked_score)
        log_total = jax.nn.logsumexp(scores, axis=-1, keepdims=True)
        probs = low(jnp.exp(scores - log_total))
        return jnp.einsum('qhk,khd->qhd', probs, value_row, precision=highest)
    attended = lax.map(jax.checkpoint(one_block), (query_blocks, code_blocks))
    return attended.reshape(LENGTH, D)

def reference(tokens, segment_ids, valid_tokens, q_weight, k_weight, v_weight, out_weight, gain_one, bias_one, ffn_in, ffn_out, gain_two, bias_two, cotangent):
    valid_float = valid_tokens.astype(jnp.float32)
    key_code = jnp.where(valid_tokens == 1, segment_ids, -1).astype(jnp.int32)
    query_code = segment_ids.astype(jnp.int32)
    head_shape = (ROWS, LENGTH, HEADS, D // HEADS)

    def forward(token_vals, q_vals, k_vals, v_vals, out_vals, gain_a, bias_a, ffn_in_vals, ffn_out_vals, gain_b, bias_b):
        queries = low_back(low(grouped(token_vals, q_vals)))
        key_vals = low_back(low(grouped(token_vals, k_vals)))
        value_vals = low_back(low(grouped(token_vals, v_vals)))
        attended = lax.map(attend_row, (queries.reshape(head_shape), key_vals.reshape(head_shape), value_vals.reshape(head_shape), query_code, key_code))
        attended = low_back(low(attended * valid_float[..., None]))
        branch_one = low_back(jnp.einsum('rld,de->rle', attended, out_vals, precision=highest))
        first = layer_norm(token_vals + branch_one, gain_a, bias_a)
        hidden_pre = low_back(grouped(low(first), ffn_in_vals))
        hidden = low(jax.nn.gelu(hidden_pre, approximate=False))
        branch_two = low_back(grouped(hidden, ffn_out_vals))
        return layer_norm(first + branch_two, gain_b, bias_b)
    floats = (tokens.astype(jnp.float32), q_weight.astype(jnp.float32), k_weight.astype(jnp.float32), v_weight.astype(jnp.float32), out_weight.astype(jnp.float32), gain_one.astype(jnp.float32), bias_one.astype(jnp.float32), ffn_in.astype(jnp.float32), ffn_out.astype(jnp.float32), gain_two.astype(jnp.float32), bias_two.astype(jnp.float32))
    output, pullback = jax.vjp(forward, *floats)
    grads = pullback(cotangent.astype(jnp.float32))
    return (output, grads[0], grads[1], grads[2], grads[3], grads[4], grads[5], grads[6], grads[7], grads[8], grads[9], grads[10])
```

```python
import functools

import jax
import jax.numpy as jnp
from jax import lax
from jax.experimental import pallas as pl
from jax.experimental.pallas import tpu as pltpu
from jax.sharding import PartitionSpec as P

HEADS = 12
GROUPS = 4
PENALTY = 2.0**30
VMEM_BYTES = 56 * 2**20
bf16 = jnp.bfloat16
f32 = jnp.float32


def dot(a, b, dims):
    return lax.dot_general(a, b, (dims, ((), ())), preferred_element_type=f32)


NN = ((1,), (0,))
TN = ((0,), (0,))
NT = ((1,), (1,))


def pieces(row):
    high = row.astype(bf16)
    rest = row - high.astype(f32)
    middle = rest.astype(bf16)
    low = (rest - middle.astype(f32)).astype(bf16)
    count = row.shape[-1]
    index = lax.broadcasted_iota(jnp.int32, (16, count), 0)
    out = jnp.where(index == 0, high.astype(f32), 0.0)
    out = jnp.where(index == 1, middle.astype(f32), out)
    out = jnp.where(index == 2, low.astype(f32), out)
    return out.astype(bf16)


def minus_rows(count):
    index = lax.broadcasted_iota(jnp.int32, (16, count), 0)
    return jnp.where(index < 3, -1.0, 0.0).astype(bf16)


def forward_kernel(parts, width, heads, where_ref, *refs):
    blocks = refs[:parts]
    wq_ref, wk_ref, wv_ref = refs[parts : parts + 3]
    qx_ref, kx_ref, vx_ref, full_ref, att_ref = refs[parts + 3 : parts + 8]
    wqt, wkt, wvt = refs[parts + 8 :]
    head = pl.program_id(0)
    size = width // heads
    toks = blocks[0].shape[2]

    @pl.when(head == 0)
    def _():
        wqt[...] = (wq_ref[0].astype(f32) * size**-0.5).T.astype(bf16)
        wkt[...] = wk_ref[0].astype(f32).T.astype(bf16)
        wvt[...] = wv_ref[0].astype(f32).T.astype(bf16)

    rows = pl.ds(pl.multiple_of(head * size, size), size)
    code_index = lax.broadcasted_iota(jnp.int32, (16, toks), 0).astype(f32)
    for p in range(parts):
        for j in range(GROUPS):
            b = p * GROUPS + j
            span = slice(b * toks, (b + 1) * toks)
            tok = blocks[p][j, :width, :]
            codes = blocks[p][j, width : width + 16, :].astype(f32)
            kx_ref[0, :size, span] = dot(wkt[rows, :], tok, NN).astype(bf16)
            kx_ref[0, size : size + 16, span] = jnp.where(
                code_index == codes[1:2], 0.0, -PENALTY
            ).astype(bf16)
            kx_ref[0, size + 16 :, span] = minus_rows(toks)
            vx_ref[0, :size, span] = dot(wvt[rows, :], tok, NN).astype(bf16)
            vx_ref[0, size:, span] = minus_rows(toks)
            if p == 0:
                qx_ref[0, :size, span] = dot(wqt[rows, :], tok, NN).astype(bf16)
                qx_ref[0, size : size + 16, span] = jnp.where(code_index == codes[0:1], 1.0, 0.0).astype(bf16)

    tile = 2 * toks
    keys = parts * GROUPS * toks
    ext = size + 16

    for qt in range(GROUPS // 2):
        qspan = slice(qt * tile, (qt + 1) * tile)

        def scores(kt):
            return dot(kx_ref[0, :ext, kt * tile : (kt + 1) * tile], qx_ref[0, :ext, qspan], TN)

        peak = None
        total = None
        upcoming = scores(0)
        for kt in range(keys // tile):
            now = upcoming
            if (kt + 1) * tile < keys:
                upcoming = scores(kt + 1)
            top = jnp.max(now, axis=0, keepdims=True)
            new_peak = top if peak is None else jnp.maximum(peak, top)
            weights = jnp.exp(now - new_peak).astype(bf16)
            mixed = dot(vx_ref[0, :, kt * tile : (kt + 1) * tile], weights, NN)
            if peak is None:
                total = mixed
            else:
                total = total * jnp.exp(peak - new_peak) + mixed
            peak = new_peak
        row_sum = -total[size : size + 1]
        attended = total[:size] / row_sum
        log_total = peak + jnp.log(row_sum)
        full_ref[:, qspan] = attended
        for half in range(2):
            j = 2 * qt + half
            sub = slice(half * toks, (half + 1) * toks)
            valid = blocks[0][j, width : width + 16, :].astype(f32)[1:2] >= 0.0
            att_ref[j] = jnp.where(valid, attended[:, sub], 0.0).astype(bf16)
            qx_ref[0, ext:, qt * tile + half * toks : qt * tile + (half + 1) * toks] = pieces(
                jnp.where(valid, log_total[:, sub], PENALTY)
            )


def forward_attention(where, blocks, q_weight, k_weight, v_weight):
    parts = len(blocks)
    _, rows, toks = blocks[0].shape
    width = q_weight.shape[1]
    heads = HEADS // GROUPS
    size = width // heads
    own, keys = GROUPS * toks, parts * GROUPS * toks
    weight_spec = pl.BlockSpec((1, width, width), lambda h, w: (w[0], 0, 0))
    return pl.pallas_call(
        functools.partial(forward_kernel, parts, width, heads),
        name="attention_forward",
        grid_spec=pltpu.PrefetchScalarGridSpec(
            num_scalar_prefetch=1,
            grid=(heads,),
            in_specs=[pl.BlockSpec((GROUPS, rows, toks), lambda h, w: (0, 0, 0))] * parts + [weight_spec] * 3,
            out_specs=[
                pl.BlockSpec((1, size + 32, own), lambda h, w: (h, 0, 0)),
                pl.BlockSpec((1, size + 32, keys), lambda h, w: (h, 0, 0)),
                pl.BlockSpec((1, size + 16, keys), lambda h, w: (h, 0, 0)),
                pl.BlockSpec((size, own), lambda h, w: (h, 0)),
                pl.BlockSpec((GROUPS, size, toks), lambda h, w: (0, h, 0)),
            ],
            scratch_shapes=[pltpu.VMEM((width, width), bf16)] * 3,
        ),
        out_shape=[
            jax.ShapeDtypeStruct((heads, size + 32, own), bf16),
            jax.ShapeDtypeStruct((heads, size + 32, keys), bf16),
            jax.ShapeDtypeStruct((heads, size + 16, keys), bf16),
            jax.ShapeDtypeStruct((width, own), f32),
            jax.ShapeDtypeStruct((GROUPS, width, toks), bf16),
        ],
        compiler_params=pltpu.CompilerParams(vmem_limit_bytes=VMEM_BYTES),
    )(where, *blocks, q_weight, k_weight, v_weight)


def backward_kernel(parts, width, heads, where_ref, *refs):
    grads = refs[:GROUPS]
    blocks = refs[GROUPS : GROUPS + parts]
    qx_ref, kx_ref, vx_ref, full_ref, wq_ref, wk_ref, wv_ref = refs[GROUPS + parts : GROUPS + parts + 7]
    back_ref, wgrad_ref = refs[GROUPS + parts + 7 : GROUPS + parts + 9]
    gx, dk, dv, dq_low, dk_low, dv_low = refs[GROUPS + parts + 9 :]
    head = pl.program_id(0)
    size = width // heads
    toks = blocks[0].shape[2]
    own, keys = GROUPS * toks, parts * GROUPS * toks
    rows = pl.ds(pl.multiple_of(head * size, size), size)

    for j in range(GROUPS):
        span = slice(j * toks, (j + 1) * toks)
        grad = grads[j][...]
        gx[:size, span] = grad
        gx[size:, span] = pieces(jnp.sum(grad.astype(f32) * full_ref[:, span], axis=0, keepdims=True))

    tile = 2 * toks
    for qt in range(own // tile):
        qspan = slice(qt * tile, (qt + 1) * tile)
        dq = None
        for kt in range(keys // tile):
            kspan = slice(kt * tile, (kt + 1) * tile)
            probs = jnp.exp(dot(qx_ref[0, :, qspan], kx_ref[0, :, kspan], TN))
            slopes = dot(gx[:, qspan], vx_ref[0, :, kspan], TN)
            probs_low = probs.astype(bf16)
            grad_scores = (probs * slopes).astype(bf16)
            dv_new = dot(gx[:size, qspan], probs_low, NN)
            dk_new = dot(qx_ref[0, :size, qspan], grad_scores, NN)
            dq_new = dot(kx_ref[0, :size, kspan], grad_scores, NT)
            if qt == 0:
                dv[:, kspan] = dv_new
                dk[:, kspan] = dk_new
            else:
                dv[:, kspan] += dv_new
                dk[:, kspan] += dk_new
            dq = dq_new if dq is None else dq + dq_new
        dq_low[rows, qspan] = (dq * size**-0.5).astype(bf16)
    dk_low[rows, :] = dk[...].astype(bf16)
    dv_low[rows, :] = dv[...].astype(bf16)

    @pl.when(head == heads - 1)
    def _():
        sums = [jnp.zeros((width, width), f32) for _ in range(3)]
        for p in range(parts):
            for j in range(GROUPS):
                b = p * GROUPS + j
                span = slice(b * toks, (b + 1) * toks)
                tok = blocks[p][j, :width, :]
                back = dot(wk_ref[0], dk_low[:, span], NN) + dot(wv_ref[0], dv_low[:, span], NN)
                sums[1] += dot(tok, dk_low[:, span], NT)
                sums[2] += dot(tok, dv_low[:, span], NT)
                if p == 0:
                    back += dot(wq_ref[0], dq_low[:, span], NN)
                    sums[0] += dot(tok, dq_low[:, span], NT)
                back_ref[p, j] = back.astype(bf16)
        chunk = width // parts
        for c in range(parts):
            slot = jnp.bitwise_xor(where_ref[1], c)
            for which in range(3):
                wgrad_ref[slot, which] = sums[which][c * chunk : (c + 1) * chunk].astype(bf16)


def backward_attention(where, grads, blocks, qx, kx, vx, full, q_weight, k_weight, v_weight):
    parts = len(blocks)
    _, rows, toks = blocks[0].shape
    width = q_weight.shape[1]
    heads = HEADS // GROUPS
    size = width // heads
    own, keys = GROUPS * toks, parts * GROUPS * toks
    weight_spec = pl.BlockSpec((1, width, width), lambda h, w: (w[0], 0, 0))
    return pl.pallas_call(
        functools.partial(backward_kernel, parts, width, heads),
        name="attention_backward",
        grid_spec=pltpu.PrefetchScalarGridSpec(
            num_scalar_prefetch=1,
            grid=(heads,),
            in_specs=[pl.BlockSpec((size, toks), lambda h, w: (h, 0))] * GROUPS
            + [pl.BlockSpec((GROUPS, rows, toks), lambda h, w: (0, 0, 0))] * parts
            + [
                pl.BlockSpec((1, size + 32, own), lambda h, w: (h, 0, 0)),
                pl.BlockSpec((1, size + 32, keys), lambda h, w: (h, 0, 0)),
                pl.BlockSpec((1, size + 16, keys), lambda h, w: (h, 0, 0)),
                pl.BlockSpec((size, own), lambda h, w: (h, 0)),
            ]
            + [weight_spec] * 3,
            out_specs=[
                pl.BlockSpec((parts, GROUPS, width, toks), lambda h, w: (0, 0, 0, 0)),
                pl.BlockSpec((parts, 3, width // parts, width), lambda h, w: (0, 0, 0, 0)),
            ],
            scratch_shapes=[
                pltpu.VMEM((size + 16, own), bf16),
                pltpu.VMEM((size, keys), f32),
                pltpu.VMEM((size, keys), f32),
                pltpu.VMEM((width, own), bf16),
                pltpu.VMEM((width, keys), bf16),
                pltpu.VMEM((width, keys), bf16),
            ],
        ),
        out_shape=[
            jax.ShapeDtypeStruct((parts, GROUPS, width, toks), bf16),
            jax.ShapeDtypeStruct((parts, 3, width // parts, width), bf16),
        ],
        compiler_params=pltpu.CompilerParams(vmem_limit_bytes=VMEM_BYTES),
    )(where, *grads, *blocks, qx, kx, vx, full, q_weight, k_weight, v_weight)


def norm_parts(values):
    mean = jnp.mean(values, axis=0, keepdims=True)
    center = values - mean
    spread = jnp.mean(center * center, axis=0, keepdims=True)
    scale = lax.rsqrt(spread + 1e-06)
    return center * scale, scale


def norm_back(normal, scale, grad):
    mean = jnp.mean(grad, axis=0, keepdims=True)
    cross = jnp.mean(grad * normal, axis=0, keepdims=True)
    return (grad - mean - normal * cross) * scale


def middle_kernel(parts, where_ref, *refs):
    slots = refs[:GROUPS]
    tok_ref, cot_ref, valid_ref, vec_ref, w_ref, fi_ref, fo_ref = refs[GROUPS : GROUPS + 7]
    mixed_ref, first_grad_ref, send_ref, pay_ref = refs[GROUPS + 7 : GROUPS + 11]
    att, first_ref, low_ref, hid_ref, slope_ref, second_ref, ghp_ref, gfirst_ref = refs[GROUPS + 11 :]
    model, toks = tok_ref.shape
    width = model // GROUPS
    wide = fi_ref.shape[2]
    own_group, own_part = where_ref[0], where_ref[1]
    gain_one, bias_one = vec_ref[:, 0:1], vec_ref[:, 1:2]
    gain_two, bias_two = vec_ref[:, 2:3], vec_ref[:, 3:4]
    chunk = model // (parts * GROUPS)

    def store(first_tile, first_row, values):
        low = values.astype(bf16)
        for r in range(values.shape[0] // chunk):
            s = first_row // chunk + r
            p = jnp.bitwise_xor(own_part, s % parts)
            j = jnp.bitwise_xor(own_group, s // parts)
            for t in range(values.shape[1] // 128):
                pay_ref[p, j, first_tile + t] = low[r * chunk : (r + 1) * chunk, t * 128 : (t + 1) * 128]

    for j in range(GROUPS):
        start = pl.multiple_of(jnp.bitwise_xor(own_group, j) * width, width)
        att[pl.ds(start, width), :] = slots[j][...]
    first_pre = tok_ref[...].astype(f32) + dot(w_ref[...], att[...], TN)
    normal_one, scale_one = norm_parts(first_pre)
    first_ref[...] = normal_one
    first = normal_one * gain_one + bias_one
    low_ref[...] = first.astype(bf16)
    for g in range(GROUPS):
        mine = slice(g * width, (g + 1) * width)
        pre = dot(fi_ref[g], low_ref[mine, :], TN)
        phi = 0.5 * (1.0 + lax.erf(pre * 0.5**0.5))
        density = jnp.exp(-0.5 * pre * pre) * 0.3989422804014327
        hid_ref[g] = (pre * phi).astype(bf16)
        slope_ref[g] = phi + pre * density
        second_ref[mine, :] = (first_ref[mine, :] * gain_one[mine] + bias_one[mine]) + dot(fo_ref[g], hid_ref[g], TN)
    normal_two, scale_two = norm_parts(second_ref[...])
    mixed_ref[0] = (normal_two * gain_two + bias_two).T
    cot = cot_ref[0].T
    grad_gain_two = jnp.sum(cot * normal_two, axis=1, keepdims=True)
    grad_bias_two = jnp.sum(cot, axis=1, keepdims=True)
    grad_second = norm_back(normal_two, scale_two, cot * gain_two)
    second_ref[...] = grad_second
    grad_low = grad_second.astype(bf16)
    for g in range(GROUPS):
        mine = slice(g * width, (g + 1) * width)
        ghp = (dot(fo_ref[g], grad_low[mine, :], NN) * slope_ref[g]).astype(bf16)
        ghp_ref[g] = ghp
        gfirst_ref[mine, :] = second_ref[mine, :] + dot(fi_ref[g], ghp, NN)
    grad_first = gfirst_ref[...]
    normal_one = first_ref[...]
    grad_gain_one = jnp.sum(grad_first * normal_one, axis=1, keepdims=True)
    grad_bias_one = jnp.sum(grad_first, axis=1, keepdims=True)
    first_grad = norm_back(normal_one, scale_one, grad_first * gain_one)
    first_grad_ref[...] = first_grad
    first_grad_low = first_grad.astype(bf16)
    grad_att = jnp.where(valid_ref[...] == 1, dot(w_ref[...], first_grad_low, NN), 0.0).astype(bf16)
    for g in range(GROUPS):
        send_ref[jnp.bitwise_xor(own_group, g)] = grad_att[g * width : (g + 1) * width]

    tiles = model // 128
    store(0, 0, dot(att[...], first_grad_low, NT))
    for g in range(GROUPS):
        mine = slice(g * width, (g + 1) * width)
        store(tiles, g * width, dot(low_ref[mine, :], ghp_ref[g], NT))
        store(tiles + wide // 128, g * width, dot(grad_low[mine, :], hid_ref[g], NT))
    lane = lax.broadcasted_iota(jnp.int32, (model, 128), 1)
    vectors = jnp.where(lane == 0, grad_gain_one, 0.0)
    vectors = jnp.where(lane == 1, grad_bias_one, vectors)
    vectors = jnp.where(lane == 2, grad_gain_two, vectors)
    vectors = jnp.where(lane == 3, grad_bias_two, vectors)
    store(tiles + 2 * (wide // 128), 0, vectors)


def middle(where, parts, slots, tok_t, cotangent, valid, vecs, out_weight, ffn_in, ffn_out):
    model, toks = tok_t.shape
    width = model // GROUPS
    wide = ffn_in.shape[2]
    chunk = model // (parts * GROUPS)
    tiles = model // 128 + 2 * (wide // 128) + 1

    def whole(shape):
        return pl.BlockSpec(shape, lambda i, w: (0,) * len(shape))

    args = (*slots, tok_t, cotangent, valid, vecs, out_weight, ffn_in, ffn_out)
    outs = [
        jax.ShapeDtypeStruct((1, toks, model), f32),
        jax.ShapeDtypeStruct((model, toks), f32),
        jax.ShapeDtypeStruct((GROUPS, width, toks), bf16),
        jax.ShapeDtypeStruct((parts, GROUPS, tiles, chunk, 128), bf16),
    ]
    return pl.pallas_call(
        functools.partial(middle_kernel, parts),
        name="middle",
        grid_spec=pltpu.PrefetchScalarGridSpec(
            num_scalar_prefetch=1,
            grid=(1,),
            in_specs=[whole(a.shape) for a in args],
            out_specs=[whole(o.shape) for o in outs],
            scratch_shapes=[
                pltpu.VMEM((model, toks), bf16),
                pltpu.VMEM((model, toks), f32),
                pltpu.VMEM((model, toks), bf16),
                pltpu.VMEM((GROUPS, wide, toks), bf16),
                pltpu.VMEM((GROUPS, wide, toks), f32),
                pltpu.VMEM((model, toks), f32),
                pltpu.VMEM((GROUPS, wide, toks), bf16),
                pltpu.VMEM((model, toks), f32),
            ],
        ),
        out_shape=outs,
        compiler_params=pltpu.CompilerParams(vmem_limit_bytes=VMEM_BYTES),
    )(where, *args)


def token_grad_kernel(where_ref, *refs):
    slots = refs[:GROUPS]
    first_grad_ref, out_ref, scratch = refs[GROUPS:]
    width = slots[0].shape[0]
    for j in range(GROUPS):
        start = pl.multiple_of(jnp.bitwise_xor(where_ref[0], j) * width, width)
        mine = pl.ds(start, width)
        scratch[mine, :] = first_grad_ref[mine, :] + slots[j][...].astype(f32)
    out_ref[0] = scratch[...].T


def token_grad(where, slots, first_grad):
    model, toks = first_grad.shape

    def whole(shape):
        return pl.BlockSpec(shape, lambda i, w: (0,) * len(shape))

    return pl.pallas_call(
        token_grad_kernel,
        name="token_grad",
        grid_spec=pltpu.PrefetchScalarGridSpec(
            num_scalar_prefetch=1,
            grid=(1,),
            in_specs=[whole(s.shape) for s in slots] + [whole(first_grad.shape)],
            out_specs=whole((1, toks, model)),
            scratch_shapes=[pltpu.VMEM((model, toks), f32)],
        ),
        out_shape=jax.ShapeDtypeStruct((1, toks, model), f32),
        compiler_params=pltpu.CompilerParams(vmem_limit_bytes=VMEM_BYTES),
    )(where, *slots, first_grad)


def weight_grad_kernel(parts, tiles, wide, where_ref, *refs):
    slots = refs[:parts]
    out_ref, in_ref, ffn_out_ref, vec_ref, wide_scratch = refs[parts:]
    chunk = slots[0].shape[2]
    wide_tiles = wide // 128
    for p in range(parts):
        start = pl.multiple_of(jnp.bitwise_xor(where_ref[1], p) * chunk, chunk)
        mine = pl.ds(start, chunk)
        for t in range(tiles):
            out_ref[mine, t * 128 : (t + 1) * 128] = slots[p][0, t].astype(f32)
        for t in range(wide_tiles):
            in_ref[0, mine, t * 128 : (t + 1) * 128] = slots[p][0, tiles + t].astype(f32)
            wide_scratch[mine, t * 128 : (t + 1) * 128] = slots[p][0, tiles + wide_tiles + t].astype(f32)
        vec_ref[mine, :] = slots[p][0, tiles + 2 * wide_tiles].astype(f32)
    ffn_out_ref[0] = wide_scratch[...].T


def weight_grads(where, slots, model, wide):
    parts = len(slots)
    _, count, chunk, _ = slots[0].shape
    width = model // GROUPS
    return pl.pallas_call(
        functools.partial(weight_grad_kernel, parts, model // 128, wide),
        name="weight_grads",
        grid_spec=pltpu.PrefetchScalarGridSpec(
            num_scalar_prefetch=1,
            grid=(GROUPS,),
            in_specs=[pl.BlockSpec((1, count, chunk, 128), lambda j, w: (j, 0, 0, 0))] * parts,
            out_specs=[
                pl.BlockSpec((width, model), lambda j, w: (jnp.bitwise_xor(j, w[0]), 0)),
                pl.BlockSpec((1, width, wide), lambda j, w: (jnp.bitwise_xor(j, w[0]), 0, 0)),
                pl.BlockSpec((1, wide, width), lambda j, w: (jnp.bitwise_xor(j, w[0]), 0, 0)),
                pl.BlockSpec((width, 128), lambda j, w: (jnp.bitwise_xor(j, w[0]), 0)),
            ],
            scratch_shapes=[pltpu.VMEM((width, wide), f32)],
        ),
        out_shape=[
            jax.ShapeDtypeStruct((model, model), f32),
            jax.ShapeDtypeStruct((GROUPS, width, wide), f32),
            jax.ShapeDtypeStruct((GROUPS, wide, width), f32),
            jax.ShapeDtypeStruct((model, 128), f32),
        ],
        compiler_params=pltpu.CompilerParams(vmem_limit_bytes=VMEM_BYTES),
    )(where, *slots)


def qkv_grad_kernel(parts, where_ref, *refs):
    slots = refs[: parts * GROUPS]
    outs = refs[parts * GROUPS :]
    chunk = slots[0].shape[1]
    for p in range(parts):
        start = pl.multiple_of(jnp.bitwise_xor(where_ref[1], p) * chunk, chunk)
        for j in range(GROUPS):
            group = jnp.bitwise_xor(where_ref[0], j)
            for which in range(3):
                outs[which][group, pl.ds(start, chunk), :] = slots[p * GROUPS + j][which].astype(f32)


def qkv_grads(where, slots):
    parts = len(slots) // GROUPS
    _, chunk, width = slots[0].shape

    def whole(shape):
        return pl.BlockSpec(shape, lambda i, w: (0,) * len(shape))

    out = (GROUPS, width, width)
    return pl.pallas_call(
        functools.partial(qkv_grad_kernel, parts),
        name="qkv_grads",
        grid_spec=pltpu.PrefetchScalarGridSpec(
            num_scalar_prefetch=1,
            grid=(1,),
            in_specs=[whole(s.shape) for s in slots],
            out_specs=[whole(out)] * 3,
        ),
        out_shape=[jax.ShapeDtypeStruct(out, f32)] * 3,
        compiler_params=pltpu.CompilerParams(vmem_limit_bytes=VMEM_BYTES),
    )(where, *slots)


def add_low(terms):
    total = terms[0].astype(f32)
    for term in terms[1:]:
        total = total + term.astype(f32)
    return total.astype(bf16)


def shards(
    tokens,
    segment_ids,
    valid_tokens,
    q_weight,
    k_weight,
    v_weight,
    out_weight,
    gain_one,
    bias_one,
    ffn_in,
    ffn_out,
    gain_two,
    bias_two,
    cotangent,
):
    seq = lax.axis_size("seq")
    depth = lax.axis_size("rows")
    parts = seq // GROUPS
    _, toks, model = tokens.shape
    width = model // GROUPS
    wide = ffn_in.shape[2]
    place = lax.axis_index("seq")
    own_group, own_part = place // parts, place % parts
    where = jnp.stack([own_group, own_part]).astype(jnp.int32)

    def swap(value, distance):
        return lax.ppermute(value, "seq", [(k, k ^ distance) for k in range(seq)])

    def across(value):
        return [value[0]] + [swap(value[j], parts * j) for j in range(1, GROUPS)]

    def around(value):
        return [value] + [swap(value, parts * j) for j in range(1, GROUPS)]

    tok_t = tokens[0].T
    key_code = jnp.where(valid_tokens == 1, segment_ids, -1)
    codes = jnp.concatenate([segment_ids, key_code, jnp.zeros((14, toks), jnp.int32)]).astype(bf16)
    grouped = tok_t.reshape(GROUPS, width, toks)
    sends = [
        jnp.concatenate([lax.dynamic_index_in_dim(grouped, own_group ^ j, 0, False), codes])
        for j in range(GROUPS)
    ]
    mine = jnp.stack(across(sends))
    blocks = [mine] + [swap(mine, p) for p in range(1, parts)]

    qx, kx, vx, full, att = forward_attention(where, blocks, q_weight, k_weight, v_weight)
    vecs = jnp.stack([gain_one, bias_one, gain_two, bias_two], axis=1)
    mixed, first_grad, send, pay = middle(
        where, parts, across(att), tok_t, cotangent, valid_tokens, vecs, out_weight, ffn_in, ffn_out
    )
    back, wgrad = backward_attention(
        where, across(send), blocks, qx, kx, vx, full, q_weight, k_weight, v_weight
    )

    half = add_low([pay[0]] + [swap(pay[p], p) for p in range(1, parts)])
    piece = add_low(across(half))
    flat = piece.reshape(depth, -1, 128)
    split = lax.all_to_all(flat, "rows", 0, 0, tiled=True)
    total = add_low([split[z] for z in range(depth)])
    piece = lax.all_to_all(jnp.broadcast_to(total, flat.shape), "rows", 0, 0, tiled=True).reshape(piece.shape)
    half = jnp.stack(around(piece))
    grad_out_weight, grad_ffn_in, grad_ffn_out, vectors = weight_grads(
        where, [half] + [swap(half, p) for p in range(1, parts)], model, wide
    )

    back_sum = add_low([back[0]] + [swap(back[p], p) for p in range(1, parts)])
    grad_tokens = token_grad(where, across(back_sum), first_grad)

    quarter = add_low([wgrad[0]] + [swap(wgrad[p], p) for p in range(1, parts)])
    copies = lax.all_to_all(jnp.broadcast_to(quarter, (depth,) + quarter.shape), "rows", 0, 0, tiled=True)
    quarter = add_low([copies[z] for z in range(depth)])
    quarters = around(quarter)
    slots = quarters + [swap(q, p) for p in range(1, parts) for q in quarters]
    grad_q, grad_k, grad_v = qkv_grads(where, slots)

    return (
        mixed,
        grad_tokens,
        grad_q,
        grad_k,
        grad_v,
        grad_out_weight,
        vectors[:, 0],
        vectors[:, 1],
        grad_ffn_in,
        grad_ffn_out,
        vectors[:, 2],
        vectors[:, 3],
    )


def solution(mesh):
    tokens = P("rows", "seq", None)
    flags = P("rows", "seq")
    in_specs = (tokens, flags, flags) + (P(),) * 10 + (tokens,)
    out_specs = (tokens, tokens) + (P(),) * 10
    return jax.shard_map(shards, mesh=mesh, in_specs=in_specs, out_specs=out_specs, check_vma=False)
```

```python
import functools

import jax
import jax.numpy as jnp
from jax import lax
from jax.experimental import pallas as pl
from jax.experimental.pallas import tpu as pltpu
from jax.sharding import PartitionSpec as P

HEADS = 12
GROUPS = 4
PENALTY = 2.0**30
VMEM_BYTES = 48 * 2**20
ATTENTION_VMEM = 24 * 2**20
bf16 = jnp.bfloat16
f32 = jnp.float32


def dot(a, b, dims):
    return lax.dot_general(a, b, (dims, ((), ())), preferred_element_type=f32)


NN = ((1,), (0,))
TN = ((0,), (0,))
NT = ((1,), (1,))


def whole(shape):
    return pl.BlockSpec(shape, lambda *_: (0,) * len(shape))


def pieces(row):
    high = row.astype(bf16)
    rest = row - high.astype(f32)
    middle = rest.astype(bf16)
    low = (rest - middle.astype(f32)).astype(bf16)
    count = row.shape[-1]
    index = lax.broadcasted_iota(jnp.int32, (16, count), 0)
    out = jnp.where(index == 0, high.astype(f32), 0.0)
    out = jnp.where(index == 1, middle.astype(f32), out)
    out = jnp.where(index == 2, low.astype(f32), out)
    return out.astype(bf16)


def minus_rows(count):
    index = lax.broadcasted_iota(jnp.int32, (16, count), 0)
    return jnp.where(index < 3, -1.0, 0.0).astype(bf16)


def after(value, *others):
    return lax.optimization_barrier((value, others))[0]


CHEAP = pl.CostEstimate(flops=1, bytes_accessed=1, transcendentals=0)


def attend(head, size, qs, kx_ref, vx_ref, own, valids, qx_ref, full_ref, atts, total_ref, peak_ref):
    toks = atts[0].shape[1]
    tile, keys = 2 * toks, kx_ref.shape[2]
    ext = size + 16

    own_keys = kx_ref[head, :size, own : own + tile]
    self_score = jnp.sum(qs[head, :size].astype(f32) * own_keys.astype(f32), axis=0, keepdims=True)
    qx_ref[0, :ext] = qs[head]
    qx_ref[0, ext:] = pieces(self_score)

    def scores(kt):
        return dot(kx_ref[head, :, kt * tile : (kt + 1) * tile], qx_ref[0], TN)

    total = None
    upcoming = scores(0)
    for kt in range(keys // tile):
        now = upcoming
        if (kt + 1) * tile < keys:
            upcoming = scores(kt + 1)
        mixed = dot(vx_ref[head, :, kt * tile : (kt + 1) * tile], jnp.exp(now).astype(bf16), NN)
        total = mixed if total is None else total + mixed
    total_ref[...] = total
    peak_ref[...] = self_score
    in_range = jnp.max(-total[size : size + 1]) < 2.0**100

    @pl.when(jnp.logical_not(in_range))
    def _():
        total_ref[...] = jnp.zeros_like(total_ref)
        peak_ref[...] = jnp.full_like(peak_ref, -4.0 * PENALTY)

        def step(kt, carry):
            span = pl.ds(pl.multiple_of(kt * tile, tile), tile)
            now = dot(kx_ref[head, :ext, span], qs[head], TN)
            peak = jnp.maximum(peak_ref[...], jnp.max(now, axis=0, keepdims=True))
            mixed = dot(vx_ref[head, :, span], jnp.exp(now - peak).astype(bf16), NN)
            total_ref[...] = total_ref[...] * jnp.exp(peak_ref[...] - peak) + mixed
            peak_ref[...] = peak
            return carry

        lax.fori_loop(0, keys // tile, step, 0)

    row_sum = -total_ref[size : size + 1]
    log_total = peak_ref[...] + jnp.log(row_sum)
    attended = jnp.where(valids, total_ref[:size] / row_sum, 0.0)
    full_ref[...] = attended
    for half in range(2):
        atts[half][...] = attended[:, half * toks : (half + 1) * toks].astype(bf16)
    qx_ref[0, ext:] = pieces(jnp.where(valids, log_total, PENALTY))


def far_kernel(parts, width, heads, where_ref, *refs):
    blocks = refs[:parts]
    w_ref, qx_ref, full_ref, att_a, att_b, kx_ref, vx_ref, near_ref, valid_ref, tok_ref = refs[parts : parts + 10]
    far, wt, total_ref, peak_ref, far_valid = refs[parts + 10 :]
    head = pl.program_id(0)
    size = width // heads
    toks = blocks[0].shape[2]
    tile, ext = 2 * toks, size + 16

    @pl.when(head == 0)
    def _():
        code_index = lax.broadcasted_iota(jnp.int32, (16, tile), 0).astype(f32)
        for which in range(3):
            scale = size**-0.5 if which == 0 else 1.0
            wt[which * width : (which + 1) * width, :] = (w_ref[which, 0].astype(f32) * scale).T.astype(bf16)
        for p in range(parts):
            for j in range(0, GROUPS, 2):
                b = p * GROUPS + j
                span = slice(b * toks, (b + 2) * toks)
                both = jnp.concatenate([blocks[p][j], blocks[p][j + 1]], axis=1)
                tok_ref[:, span] = both[:width]
                first = 0 if p == 0 else width
                made = dot(wt[first:], both[:width], NN).astype(bf16)
                codes = both[width:].astype(f32)
                mask = jnp.where(code_index == codes[1:2], 0.0, -PENALTY).astype(bf16)
                for h in range(heads):
                    keys = width - first + h * size
                    kx_ref[h, :size, span] = made[keys : keys + size]
                    kx_ref[h, size:ext, span] = mask
                    kx_ref[h, ext:, span] = minus_rows(tile)
                    vx_ref[h, :size, span] = made[keys + width : keys + width + size]
                    vx_ref[h, size:, span] = minus_rows(tile)
                if p == 0:
                    target, flags = (near_ref, valid_ref) if j == 0 else (far, far_valid)
                    hot = jnp.where(code_index == codes[0:1], 1.0, 0.0).astype(bf16)
                    flags[...] = jnp.broadcast_to(codes[1:2], (8, tile))
                    for h in range(heads):
                        target[h, :size] = made[h * size : (h + 1) * size]
                        target[h, size:] = hot

    valids = far_valid[0:1, :] >= 0.0
    attend(head, size, far, kx_ref, vx_ref, tile, valids, qx_ref, full_ref, (att_a, att_b), total_ref, peak_ref)


def near_kernel(size, near_ref, valid_ref, kx_ref, vx_ref, qx_ref, full_ref, att_a, att_b, total_ref, peak_ref):
    valids = valid_ref[0:1, :] >= 0.0
    attend(
        pl.program_id(0), size, near_ref, kx_ref, vx_ref, 0, valids, qx_ref, full_ref, (att_a, att_b), total_ref, peak_ref
    )


def attention_outs(heads, size, toks):
    width, tile = heads * size, 2 * toks
    specs = [
        pl.BlockSpec((1, size + 32, tile), lambda h, *_: (h, 0, 0)),
        pl.BlockSpec((size, tile), lambda h, *_: (h, 0)),
        pl.BlockSpec((size, toks), lambda h, *_: (h, 0)),
        pl.BlockSpec((size, toks), lambda h, *_: (h, 0)),
    ]
    shapes = [
        jax.ShapeDtypeStruct((heads, size + 32, tile), bf16),
        jax.ShapeDtypeStruct((width, tile), f32),
        jax.ShapeDtypeStruct((width, toks), bf16),
        jax.ShapeDtypeStruct((width, toks), bf16),
    ]
    scratch = [pltpu.VMEM((size + 16, tile), f32), pltpu.VMEM((1, tile), f32)]
    return specs, shapes, scratch


def far_attention(where, blocks, weights):
    parts = len(blocks)
    _, rows, toks = blocks[0].shape
    width = weights.shape[2]
    heads = HEADS // GROUPS
    size = width // heads
    tile, keys = 2 * toks, parts * GROUPS * toks
    specs, shapes, scratch = attention_outs(heads, size, toks)
    shared = [
        jax.ShapeDtypeStruct((heads, size + 32, keys), bf16),
        jax.ShapeDtypeStruct((heads, size + 16, keys), bf16),
        jax.ShapeDtypeStruct((heads, size + 16, tile), bf16),
        jax.ShapeDtypeStruct((8, tile), f32),
        jax.ShapeDtypeStruct((width, keys), bf16),
    ]
    return pl.pallas_call(
        functools.partial(far_kernel, parts, width, heads),
        name="attention_far",
        grid_spec=pltpu.PrefetchScalarGridSpec(
            num_scalar_prefetch=1,
            grid=(heads,),
            in_specs=[pl.BlockSpec((GROUPS, rows, toks), lambda h, w: (0, 0, 0))] * parts
            + [pl.BlockSpec((3, 1, width, width), lambda h, w: (0, w[0], 0, 0))],
            out_specs=specs + [whole(x.shape) for x in shared],
            scratch_shapes=[pltpu.VMEM((heads, size + 16, tile), bf16), pltpu.VMEM((3 * width, width), bf16)]
            + scratch
            + [pltpu.VMEM((8, tile), f32)],
        ),
        out_shape=shapes + shared,
        cost_estimate=CHEAP,
        compiler_params=pltpu.CompilerParams(vmem_limit_bytes=ATTENTION_VMEM),
    )(where, *blocks, weights)


def near_attention(near, valid, kx, vx):
    heads, ext, tile = near.shape
    size = ext - 16
    specs, shapes, scratch = attention_outs(heads, size, tile // 2)
    return pl.pallas_call(
        functools.partial(near_kernel, size),
        name="attention_near",
        grid=(heads,),
        in_specs=[whole(x.shape) for x in (near, valid, kx, vx)],
        out_specs=specs,
        scratch_shapes=scratch,
        out_shape=shapes,
        cost_estimate=CHEAP,
        compiler_params=pltpu.CompilerParams(vmem_limit_bytes=ATTENTION_VMEM),
    )(near, valid, kx, vx)


def backward_kernel(size, carry, grad_a, grad_b, qx_ref, full_ref, kx_ref, vx_ref, *refs):
    if carry:
        dk_in, dv_in, dq_ref, dk_ref, dv_ref, gx = refs
    else:
        dq_ref, dk_ref, dv_ref, gx = refs
    toks = grad_a.shape[1]
    for half, ref in enumerate((grad_a, grad_b)):
        span = slice(half * toks, (half + 1) * toks)
        grad = ref[...]
        gx[:size, span] = grad
        gx[size:, span] = pieces(jnp.sum(grad.astype(f32) * full_ref[:, span], axis=0, keepdims=True))

    tile = 2 * toks
    dq = None
    for kt in range(kx_ref.shape[2] // tile):
        kspan = slice(kt * tile, (kt + 1) * tile)
        probs = jnp.exp(dot(qx_ref[0], kx_ref[0, :, kspan], TN))
        slopes = dot(gx[...], vx_ref[0, :, kspan], TN)
        probs_low = probs.astype(bf16)
        grad_scores = (probs * slopes).astype(bf16)
        dv_new = dot(gx[:size, :], probs_low, NN)
        dk_new = dot(qx_ref[0, :size, :], grad_scores, NN)
        dq_new = dot(kx_ref[0, :size, kspan], grad_scores, NT)
        if carry:
            dv_new += dv_in[0, :, kspan]
            dk_new += dk_in[0, :, kspan]
        dv_ref[0, :, kspan] = dv_new.astype(dv_ref.dtype)
        dk_ref[0, :, kspan] = dk_new.astype(dk_ref.dtype)
        dq = dq_new if dq is None else dq + dq_new
    dq_ref[0] = (dq * size**-0.5).astype(bf16)


def backward_attention(start, grads, qx, full, kx, vx, sums=None, count=1):
    toks = grads[0].shape[1]
    size = vx.shape[1] - 16
    tile, keys = 2 * toks, vx.shape[2]
    sum_spec = pl.BlockSpec((1, size, keys), lambda h: (h, 0, 0))
    in_specs = [pl.BlockSpec((size, toks), lambda h: (h + start, 0))] * 2 + [
        pl.BlockSpec((1, size + 32, tile), lambda h: (h + start, 0, 0)),
        pl.BlockSpec((size, tile), lambda h: (h + start, 0)),
        pl.BlockSpec((1, size + 32, keys), lambda h: (h + start, 0, 0)),
        pl.BlockSpec((1, size + 16, keys), lambda h: (h + start, 0, 0)),
    ]
    carry = sums is not None
    kind = bf16 if carry else f32
    return pl.pallas_call(
        functools.partial(backward_kernel, size, carry),
        name="attention_backward",
        grid=(count,),
        in_specs=in_specs + [sum_spec] * (2 if carry else 0),
        out_specs=[pl.BlockSpec((1, size, tile), lambda h: (h, 0, 0)), sum_spec, sum_spec],
        scratch_shapes=[pltpu.VMEM((size + 16, tile), bf16)],
        out_shape=[
            jax.ShapeDtypeStruct((count, size, tile), bf16),
            jax.ShapeDtypeStruct((count, size, keys), kind),
            jax.ShapeDtypeStruct((count, size, keys), kind),
        ],
        cost_estimate=CHEAP,
        compiler_params=pltpu.CompilerParams(vmem_limit_bytes=ATTENTION_VMEM),
    )(*grads, qx, full, kx, vx, *(sums if carry else ()))


def project_kernel(parts, width, counts, where_ref, *refs):
    tok_ref, wq_ref, wk_ref, wv_ref = refs[:4]
    refs = refs[4:]
    near, far, dks, dvs = (refs[sum(counts[:i]) : sum(counts[: i + 1])] for i in range(4))
    refs = refs[sum(counts) :]
    backs, wgrads, scratch = refs[:parts], refs[parts : 2 * parts], refs[2 * parts]
    keys = tok_ref.shape[1]
    count = keys // parts
    toks = count // GROUPS

    def joined(pile):
        return jnp.concatenate([ref[h] for ref in pile for h in range(ref.shape[0])])

    dq = jnp.concatenate([joined(near), joined(far)], axis=1)
    dk, dv = joined(dks), joined(dvs)
    scratch[0] = dot(tok_ref[:, :count], dq, NT).astype(bf16)
    scratch[1] = dot(tok_ref[...], dk, NT).astype(bf16)
    scratch[2] = dot(tok_ref[...], dv, NT).astype(bf16)
    for p in reversed(range(parts)):
        span = slice(p * count, (p + 1) * count)
        back = dot(wk_ref[0], dk[:, span], NN) + dot(wv_ref[0], dv[:, span], NN)
        if p == 0:
            back += dot(wq_ref[0], dq, NN)
        for j in range(GROUPS):
            backs[p][j] = back[:, j * toks : (j + 1) * toks].astype(bf16)
    chunk = width // parts
    for p in range(parts):
        rows = pl.ds(pl.multiple_of(jnp.bitwise_xor(where_ref[1], p) * chunk, chunk), chunk)
        wgrads[p][...] = scratch[:, rows, :]


def project_back(where, parts, tok, weights, near, far, dks, dvs):
    width, keys = tok.shape
    toks = keys // parts // GROUPS
    piles = (near, far, dks, dvs)
    flat = [x for pile in piles for x in pile]
    weight_spec = pl.BlockSpec((1, width, width), lambda i, w: (w[0], 0, 0))
    outs = [jax.ShapeDtypeStruct((GROUPS, width, toks), bf16)] * parts + [
        jax.ShapeDtypeStruct((3, width // parts, width), bf16)
    ] * parts
    results = pl.pallas_call(
        functools.partial(project_kernel, parts, width, [len(pile) for pile in piles]),
        name="project_back",
        grid_spec=pltpu.PrefetchScalarGridSpec(
            num_scalar_prefetch=1,
            grid=(1,),
            in_specs=[whole(tok.shape)] + [weight_spec] * 3 + [whole(x.shape) for x in flat],
            out_specs=[whole(o.shape) for o in outs],
            scratch_shapes=[pltpu.VMEM((3, width, width), bf16)],
        ),
        out_shape=outs,
        cost_estimate=CHEAP,
        compiler_params=pltpu.CompilerParams(vmem_limit_bytes=ATTENTION_VMEM),
    )(where, tok, *weights, *flat)
    return results[:parts], results[parts:]


def norm_parts(values):
    mean = jnp.mean(values, axis=0, keepdims=True)
    center = values - mean
    spread = jnp.mean(center * center, axis=0, keepdims=True)
    scale = lax.rsqrt(spread + 1e-06)
    return center * scale, scale


def norm_back(normal, scale, grad):
    mean = jnp.mean(grad, axis=0, keepdims=True)
    cross = jnp.mean(grad * normal, axis=0, keepdims=True)
    return (grad - mean - normal * cross) * scale


def middle_kernel(where_ref, *refs):
    slots = (refs[0], refs[1], refs[2].at[0], refs[2].at[1])
    tok_ref, cot_ref, valid_ref, vec_ref, w_ref, fi_ref, fo_ref = refs[3:10]
    refs = refs[10:]
    mixed_ref, first_grad_ref = refs[:2]
    sends = refs[2 : 2 + GROUPS]
    att, narrow_ref, wide_ref, first_low_ref, vec_out_ref = refs[2 + GROUPS : 7 + GROUPS]
    first_ref, slope_ref, second_ref, gfirst_ref, grad_att = refs[7 + GROUPS :]
    model, toks = tok_ref.shape
    width = model // GROUPS
    own_group = where_ref[0]
    gain_one, bias_one = vec_ref[:, 0:1], vec_ref[:, 1:2]
    gain_two, bias_two = vec_ref[:, 2:3], vec_ref[:, 3:4]

    for j in range(GROUPS):
        start = pl.multiple_of(jnp.bitwise_xor(own_group, j) * width, width)
        att[pl.ds(start, width), :] = slots[j][...]
    first_pre = tok_ref[...].astype(f32) + dot(w_ref[...], att[...], TN)
    normal_one, scale_one = norm_parts(first_pre)
    first_ref[...] = normal_one
    first = normal_one * gain_one + bias_one
    narrow_ref[0] = first.astype(bf16)
    for g in range(GROUPS):
        mine = slice(g * width, (g + 1) * width)
        pre = dot(fi_ref[g], narrow_ref[0, mine, :], TN)
        phi = 0.5 * (1.0 + lax.erf(pre * 0.5**0.5))
        density = jnp.exp(-0.5 * pre * pre) * 0.3989422804014327
        wide_ref[1, g] = (pre * phi).astype(bf16)
        slope_ref[g] = phi + pre * density
        second_ref[mine, :] = (first_ref[mine, :] * gain_one[mine] + bias_one[mine]) + dot(fo_ref[g], wide_ref[1, g], NN)
    normal_two, scale_two = norm_parts(second_ref[...])
    mixed_ref[0] = (normal_two * gain_two + bias_two).T
    cot = cot_ref[0].T
    grad_gain_two = jnp.sum(cot * normal_two, axis=1, keepdims=True)
    grad_bias_two = jnp.sum(cot, axis=1, keepdims=True)
    grad_second = norm_back(normal_two, scale_two, cot * gain_two)
    second_ref[...] = grad_second
    grad_low = grad_second.astype(bf16)
    narrow_ref[1] = grad_low
    for g in range(GROUPS):
        mine = slice(g * width, (g + 1) * width)
        ghp = (dot(fo_ref[g], grad_low[mine, :], TN) * slope_ref[g]).astype(bf16)
        wide_ref[0, g] = ghp
        gfirst_ref[mine, :] = second_ref[mine, :] + dot(fi_ref[g], ghp, NN)
    grad_first = gfirst_ref[...]
    normal_one = first_ref[...]
    grad_gain_one = jnp.sum(grad_first * normal_one, axis=1, keepdims=True)
    grad_bias_one = jnp.sum(grad_first, axis=1, keepdims=True)
    first_grad = norm_back(normal_one, scale_one, grad_first * gain_one)
    first_grad_ref[...] = first_grad
    first_low = first_grad.astype(bf16)
    first_low_ref[...] = first_low
    grad_att[...] = jnp.where(valid_ref[...] == 1, dot(w_ref[...], first_low, NN), 0.0).astype(bf16)
    for j in range(GROUPS):
        start = pl.multiple_of(jnp.bitwise_xor(own_group, j) * width, width)
        sends[j][...] = grad_att[pl.ds(start, width), :]

    lane = lax.broadcasted_iota(jnp.int32, (model, 128), 1)
    vectors = jnp.where(lane == 0, grad_gain_one, 0.0)
    vectors = jnp.where(lane == 1, grad_bias_one, vectors)
    vectors = jnp.where(lane == 2, grad_gain_two, vectors)
    vectors = jnp.where(lane == 3, grad_bias_two, vectors)
    vec_out_ref[...] = vectors.astype(bf16)


def middle(where, slots, tok_t, cotangent, valid, vecs, out_weight, ffn_in, ffn_out_t):
    model, toks = tok_t.shape
    width = model // GROUPS
    wide = ffn_in.shape[2]
    args = (*slots, tok_t, cotangent, valid, vecs, out_weight, ffn_in, ffn_out_t)
    outs = (
        [jax.ShapeDtypeStruct((1, toks, model), f32), jax.ShapeDtypeStruct((model, toks), f32)]
        + [jax.ShapeDtypeStruct((width, toks), bf16)] * GROUPS
        + [
            jax.ShapeDtypeStruct((model, toks), bf16),
            jax.ShapeDtypeStruct((2, model, toks), bf16),
            jax.ShapeDtypeStruct((2, GROUPS, wide, toks), bf16),
            jax.ShapeDtypeStruct((model, toks), bf16),
            jax.ShapeDtypeStruct((model, 128), bf16),
        ]
    )
    results = pl.pallas_call(
        middle_kernel,
        name="middle",
        grid_spec=pltpu.PrefetchScalarGridSpec(
            num_scalar_prefetch=1,
            grid=(1,),
            in_specs=[whole(a.shape) for a in args],
            out_specs=[whole(o.shape) for o in outs],
            scratch_shapes=[
                pltpu.VMEM((model, toks), f32),
                pltpu.VMEM((GROUPS, wide, toks), f32),
                pltpu.VMEM((model, toks), f32),
                pltpu.VMEM((model, toks), f32),
                pltpu.VMEM((model, toks), bf16),
            ],
        ),
        out_shape=outs,
        cost_estimate=CHEAP,
        compiler_params=pltpu.CompilerParams(vmem_limit_bytes=VMEM_BYTES),
    )(where, *args)
    return results[0], results[1], results[2 : 2 + GROUPS], results[2 + GROUPS :]


def swapped(slot, odd):
    return jnp.where(odd, slot, (slot % 2) * 2 + slot // 2)


def outer_kernel(parts, slot, where_ref, att, narrow_ref, wide_ref, first_low_ref, vec_ref, near_ref, far_ref):
    model = att.shape[0]
    width = model // GROUPS
    wide = wide_ref.shape[2]
    half = parts // 2
    own_group, part = where_ref[0], jnp.bitwise_xor(where_ref[1], slot)
    ffn_rows, out_rows = width // half, model // (parts * GROUPS)
    array, piece = part // half, part % half
    tiles, wide_tiles = model // 128, wide // 128

    out_start = pl.multiple_of(part * (model // parts), model // parts)
    out = dot(att[pl.ds(out_start, model // parts), :], first_low_ref[...], NT).astype(bf16)
    for target, slots in ((near_ref, (0, 1)), (far_ref, (2, 3))):
        for index, m in enumerate(slots):
            group = jnp.bitwise_xor(own_group, swapped(m, part % 2 == 1))
            start = pl.multiple_of(group * width + piece * ffn_rows, ffn_rows)
            made = dot(narrow_ref[array, pl.ds(start, ffn_rows), :], wide_ref[array, group], NT).astype(bf16)
            for t in range(wide_tiles):
                target[index, t * ffn_rows : (t + 1) * ffn_rows] = made[:, t * 128 : (t + 1) * 128]
    base = wide_tiles * ffn_rows
    for g in range(GROUPS):
        distance = jnp.bitwise_xor(own_group, g)
        m = swapped(distance, part % 2 == 1)
        rows = slice(g * out_rows, (g + 1) * out_rows)
        vec_start = pl.multiple_of(part * (model // parts) + g * out_rows, out_rows)
        vec = vec_ref[pl.ds(vec_start, out_rows), :]

        def put(target, index):
            for t in range(tiles):
                span = slice(base + t * out_rows, base + (t + 1) * out_rows)
                target[index, span] = out[rows, t * 128 : (t + 1) * 128]
            target[index, base + tiles * out_rows : base + (tiles + 1) * out_rows] = vec

        @pl.when(m < 2)
        def _():
            put(near_ref, m)

        @pl.when(m >= 2)
        def _():
            put(far_ref, m - 2)


def outer_products(where, parts, slot, kept):
    att, narrow, wide_pair, _, _ = kept
    model = att.shape[0]
    wide = wide_pair.shape[2]
    rows = (wide // 128) * (model // GROUPS // (parts // 2)) + (model // 128 + 1) * (model // (parts * GROUPS))
    outs = [jax.ShapeDtypeStruct((2, rows, 128), bf16)] * 2
    return pl.pallas_call(
        functools.partial(outer_kernel, parts, slot),
        name="outer_products",
        grid_spec=pltpu.PrefetchScalarGridSpec(
            num_scalar_prefetch=1,
            grid=(1,),
            in_specs=[whole(a.shape) for a in kept],
            out_specs=[whole(o.shape) for o in outs],
        ),
        out_shape=outs,
        cost_estimate=CHEAP,
        compiler_params=pltpu.CompilerParams(vmem_limit_bytes=ATTENTION_VMEM),
    )(where, *kept)


def token_grad_kernel(where_ref, *refs):
    slots = refs[:GROUPS]
    first_grad_ref, out_ref, scratch = refs[GROUPS:]
    width = slots[0].shape[0]
    for j in range(GROUPS):
        start = pl.multiple_of(jnp.bitwise_xor(where_ref[0], j) * width, width)
        mine = pl.ds(start, width)
        scratch[mine, :] = first_grad_ref[mine, :] + slots[j][...].astype(f32)
    out_ref[0] = scratch[...].T


def token_grad(where, slots, first_grad):
    model, toks = first_grad.shape

    return pl.pallas_call(
        token_grad_kernel,
        name="token_grad",
        grid_spec=pltpu.PrefetchScalarGridSpec(
            num_scalar_prefetch=1,
            grid=(1,),
            in_specs=[whole(s.shape) for s in slots] + [whole(first_grad.shape)],
            out_specs=whole((1, toks, model)),
            scratch_shapes=[pltpu.VMEM((model, toks), f32)],
        ),
        out_shape=jax.ShapeDtypeStruct((1, toks, model), f32),
        cost_estimate=CHEAP,
        compiler_params=pltpu.CompilerParams(vmem_limit_bytes=VMEM_BYTES),
    )(where, *slots, first_grad)


def row_distances(depth):
    steps = depth.bit_length() - 1
    even = [sum(((m >> (steps - 1 - i)) & 1) << i for i in range(steps)) for m in range(depth)]
    return even, list(range(depth))


def weight_grad_kernel(parts, depth, model, wide, where_ref, *refs):
    slots = refs[:parts]
    out_ref, in_ref, ffn_out_ref, vec_ref, scratch, vec_scratch = refs[parts:]
    step = pl.program_id(0)
    group = jnp.bitwise_xor(step, where_ref[0])
    piece = slots[0].shape[2]
    width = model // GROUPS
    half = parts // 2
    ffn_rows, out_rows = width // half, model // (parts * GROUPS)
    tiles, wide_tiles = model // 128, wide // 128
    even, odd = row_distances(depth)
    for p in range(parts):
        part = jnp.bitwise_xor(where_ref[1], p)
        for z in range(depth):
            distance = jnp.where(part % 2 == 1, odd[z], even[z])
            scratch[part, jnp.bitwise_xor(where_ref[2], distance)] = slots[p][0, z].astype(f32)

    def rows(part, first, count):
        last = first + count
        cuts = [first] + [c for c in range(0, depth * piece, piece) if first < c < last] + [last]
        return jnp.concatenate(
            [scratch[part, x // piece, x % piece : x % piece + y - x, :] for x, y in zip(cuts, cuts[1:])]
        )

    base = wide_tiles * ffn_rows
    for part in range(parts):
        target = in_ref if part < half else ffn_out_ref
        mine = slice((part % half) * ffn_rows, (part % half + 1) * ffn_rows)
        for t in range(wide_tiles):
            target[0, mine, t * 128 : (t + 1) * 128] = rows(part, t * ffn_rows, ffn_rows)
        for t in range(tiles):
            out_ref[part, 0, :, t * 128 : (t + 1) * 128] = rows(part, base + t * out_rows, out_rows)
        start = pl.multiple_of(part * (model // parts) + group * out_rows, out_rows)
        vec_scratch[pl.ds(start, out_rows), :] = rows(part, base + tiles * out_rows, out_rows)

    @pl.when(step == GROUPS - 1)
    def _():
        vec_ref[...] = vec_scratch[...].T[:8]


def weight_grads(where, slots, model, wide):
    parts = len(slots)
    _, depth, piece, _ = slots[0].shape
    width = model // GROUPS
    out_rows = model // (parts * GROUPS)

    def slot_spec(p):
        def place(j, w):
            return (swapped(j, jnp.bitwise_xor(w[1], p) % 2 == 1), 0, 0, 0)

        return pl.BlockSpec((1, depth, piece, 128), place)

    out, ffn_in, ffn_out_t, vectors = pl.pallas_call(
        functools.partial(weight_grad_kernel, parts, depth, model, wide),
        name="weight_grads",
        grid_spec=pltpu.PrefetchScalarGridSpec(
            num_scalar_prefetch=1,
            grid=(GROUPS,),
            in_specs=[slot_spec(p) for p in range(parts)],
            out_specs=[
                pl.BlockSpec((parts, 1, out_rows, model), lambda j, w: (0, jnp.bitwise_xor(j, w[0]), 0, 0)),
                pl.BlockSpec((1, width, wide), lambda j, w: (jnp.bitwise_xor(j, w[0]), 0, 0)),
                pl.BlockSpec((1, width, wide), lambda j, w: (jnp.bitwise_xor(j, w[0]), 0, 0)),
                pl.BlockSpec((8, model), lambda j, w: (0, 0)),
            ],
            scratch_shapes=[pltpu.VMEM((parts, depth, piece, 128), f32), pltpu.VMEM((model, 128), f32)],
        ),
        out_shape=[
            jax.ShapeDtypeStruct((parts, GROUPS, out_rows, model), f32),
            jax.ShapeDtypeStruct((GROUPS, width, wide), f32),
            jax.ShapeDtypeStruct((GROUPS, width, wide), f32),
            jax.ShapeDtypeStruct((8, model), f32),
        ],
        cost_estimate=CHEAP,
        compiler_params=pltpu.CompilerParams(vmem_limit_bytes=ATTENTION_VMEM),
    )(where, *slots)
    return out.reshape(model, model), ffn_in, ffn_out_t, vectors


def qkv_grad_kernel(parts, where_ref, *refs):
    slots = refs[:parts]
    outs = refs[parts:]
    chunk = slots[0].shape[2]
    for p in range(parts):
        part = jnp.bitwise_xor(where_ref[1], p)
        start = pl.multiple_of(part * chunk, chunk)
        for m in range(GROUPS):
            group = jnp.bitwise_xor(where_ref[0], swapped(m, part % 2 == 1))
            for which in range(3):
                outs[which][group, pl.ds(start, chunk), :] = slots[p][m, which].astype(f32)


def qkv_grads(where, slots):
    parts = len(slots)
    _, _, chunk, width = slots[0].shape

    out = (GROUPS, width, width)
    return pl.pallas_call(
        functools.partial(qkv_grad_kernel, parts),
        name="qkv_grads",
        grid_spec=pltpu.PrefetchScalarGridSpec(
            num_scalar_prefetch=1,
            grid=(1,),
            in_specs=[whole(s.shape) for s in slots],
            out_specs=[whole(out)] * 3,
        ),
        out_shape=[jax.ShapeDtypeStruct(out, f32)] * 3,
        cost_estimate=CHEAP,
        compiler_params=pltpu.CompilerParams(vmem_limit_bytes=VMEM_BYTES),
    )(where, *slots)


def add_low(terms):
    total = terms[0].astype(f32)
    for term in terms[1:]:
        total = total + term.astype(f32)
    return total.astype(bf16)


def shards(
    tokens,
    segment_ids,
    valid_tokens,
    q_weight,
    k_weight,
    v_weight,
    out_weight,
    gain_one,
    bias_one,
    ffn_in,
    ffn_out,
    gain_two,
    bias_two,
    cotangent,
):
    seq = lax.axis_size("seq")
    depth = lax.axis_size("rows")
    parts = seq // GROUPS
    _, toks, model = tokens.shape
    width = model // GROUPS
    wide = ffn_in.shape[2]
    place = lax.axis_index("seq")
    own_group, own_part = place // parts, place % parts
    own_row = lax.axis_index("rows")
    where = jnp.stack([own_group, own_part, own_row]).astype(jnp.int32)

    def swap(value, distance):
        return lax.ppermute(value, "seq", [(k, k ^ distance) for k in range(seq)])

    def across(value):
        return [value[0]] + [swap(value[j], parts * j) for j in range(1, GROUPS)]

    def group_swap(value, step):
        apart = [(1, 2), (2, 1)][step]
        return lax.ppermute(value, "seq", [(k, k ^ parts * apart[k % parts % 2]) for k in range(seq)])

    row_steps = depth.bit_length() - 1

    def row_swap(value, step):
        pairs = []
        for k in range(seq):
            distance = 1 << (row_steps - 1 - step if k % parts % 2 else step)
            pairs += [(k * depth + z, k * depth + (z ^ distance)) for z in range(depth)]
        return lax.ppermute(value, ("seq", "rows"), pairs)

    tok_t = tokens[0].T
    key_code = jnp.where(valid_tokens == 1, segment_ids, -1)
    codes = jnp.concatenate([segment_ids, key_code, jnp.zeros((14, toks), jnp.int32)]).astype(bf16)
    grouped = tok_t.reshape(GROUPS, width, toks)
    sends = [
        jnp.concatenate([lax.dynamic_index_in_dim(grouped, own_group ^ j, 0, False), codes])
        for j in range(GROUPS)
    ]
    mine = jnp.stack(across(sends))
    blocks = [mine] + [swap(mine, p) for p in range(1, parts)]

    qx_far, full_far, att_c, att_d, kx, vx, near, near_valid, tok = far_attention(
        where, blocks, jnp.stack([q_weight, k_weight, v_weight])
    )
    att_far = jnp.stack([swap(att_c, parts * 2), swap(att_d, parts * 3)])
    qx_near, full_near, att_a, att_b = near_attention(near, near_valid, kx, vx)
    att_b = swap(att_b, parts)
    vecs = jnp.stack([gain_one, bias_one, gain_two, bias_two], axis=1)
    mixed, first_grad, sends, kept = middle(
        where,
        [att_a, att_b, att_far],
        tok_t,
        cotangent,
        valid_tokens,
        vecs,
        out_weight,
        ffn_in,
        jnp.swapaxes(ffn_out, 1, 2),
    )
    grads = across(sends)

    pays = [outer_products(where, parts, p, kept) for p in range(1, parts)]
    pay = outer_products(where, parts, 0, after(kept, pays))
    moved = [[swap(x, p) for x in after(pays[p - 1], grads[1])] for p in range(1, parts)]
    near_a = backward_attention(0, after(grads[:2], pay), qx_near, full_near, kx, vx, count=1)
    moved = after(moved, near_a, grads)
    low = add_low([pay[0]] + [x[0] for x in moved])
    high = add_low([pay[1]] + [x[1] for x in moved])
    moved = group_swap(high, 0)
    near_b = backward_attention(1, after(grads[:2], high, low), qx_near, full_near, kx, vx, count=2)
    moved = after(moved, near_b)
    low, high = add_low([low[0], moved[0]]), add_low([low[1], moved[1]])
    moved = group_swap(high, 1)
    far = [
        backward_attention(
            0, after(grads[2:], high, low), qx_far, full_far, kx, vx, [x[0:1] for x in near_a[1:]], count=1
        )
    ]
    piece = add_low([low, after(moved, far[0])]).reshape(depth, -1, 128)
    even, odd = row_distances(depth)
    picks = [own_row ^ jnp.where(own_part % 2 == 1, odd[m], even[m]) for m in range(depth)]
    piece = jnp.stack([lax.dynamic_index_in_dim(piece, z, 0, False) for z in picks])
    for step in range(row_steps):
        count = piece.shape[0] // 2
        low, high = piece[:count], piece[count:]
        moved = row_swap(high, step)
        if len(far) < 3:
            head = len(far)
            sums = [x[head - 1 : head] for x in near_b[1:]]
            far.append(
                backward_attention(head, after(grads[2:], high, low), qx_far, full_far, kx, vx, sums, count=1)
            )
            moved = after(moved, far[-1])
        piece = add_low([low, moved])
    moved = row_swap(piece, row_steps - 1)
    backs, wgrads = project_back(
        where,
        parts,
        tok,
        (q_weight, k_weight, v_weight),
        after([near_a[0], near_b[0]], piece),
        [x[0] for x in far],
        [x[1] for x in far],
        [x[2] for x in far],
    )
    piece = jnp.concatenate([piece, after(moved, backs, wgrads)])
    quarter = add_low([wgrads[0]] + [swap(wgrads[p], p) for p in range(1, parts)])
    back_sum = add_low([backs[0]] + [swap(backs[p], p) for p in range(1, parts)])
    for step in reversed(range(row_steps - 1)):
        moved = row_swap(piece, step)
        if step == 0:
            moved = after(moved, quarter, back_sum)
        piece = jnp.concatenate([piece, moved])
    back_moved = across(back_sum)
    grad_tokens = token_grad(where, back_moved, first_grad)
    moved = group_swap(piece[None], 1)
    for step in range(row_steps):
        quarter = add_low([quarter, row_swap(quarter, step)])
    piece = jnp.concatenate([piece[None], after(moved, grad_tokens, quarter)])
    moved = group_swap(piece, 0)
    quarter = quarter[None]
    for step in (1, 0):
        quarter = jnp.concatenate([quarter, group_swap(quarter, step)])
    piece = jnp.concatenate([piece, after(moved, quarter)])
    slots = [piece] + [swap(piece, p) for p in range(1, parts)]
    grad_q, grad_k, grad_v = qkv_grads(where, [quarter] + [swap(quarter, p) for p in range(1, parts)])
    slots = after(slots, grad_q)
    grad_out_weight, grad_ffn_in, grad_ffn_out_t, vectors = weight_grads(where, slots, model, wide)

    return (
        mixed,
        grad_tokens,
        grad_q,
        grad_k,
        grad_v,
        grad_out_weight,
        vectors[0],
        vectors[1],
        grad_ffn_in,
        jnp.swapaxes(grad_ffn_out_t, 1, 2),
        vectors[2],
        vectors[3],
    )


def solution(mesh):
    tokens = P("rows", "seq", None)
    flags = P("rows", "seq")
    in_specs = (tokens, flags, flags) + (P(),) * 10 + (tokens,)
    out_specs = (tokens, tokens) + (P(),) * 10
    return jax.shard_map(shards, mesh=mesh, in_specs=in_specs, out_specs=out_specs, check_vma=False)
```

```python
import functools

import jax
import jax.numpy as jnp
from jax import lax
from jax.experimental import pallas as pl
from jax.experimental.pallas import tpu as pltpu
from jax.sharding import PartitionSpec as P

HEADS = 12
GROUPS = 4
PENALTY = 2.0**30
VMEM_BYTES = 36 * 2**20
SMALL_VMEM = 20 * 2**20
ATT_BASE = 9
bf16 = jnp.bfloat16
f32 = jnp.float32


def dot(a, b, dims):
    return lax.dot_general(a, b, (dims, ((), ())), preferred_element_type=f32)


NN = ((1,), (0,))
TN = ((0,), (0,))
NT = ((1,), (1,))


def whole(shape):
    return pl.BlockSpec(shape, lambda *_: (0,) * len(shape), pipeline_mode=pl.Buffered(1))


def pieces(row):
    high = row.astype(bf16)
    rest = row - high.astype(f32)
    middle = rest.astype(bf16)
    low = (rest - middle.astype(f32)).astype(bf16)
    count = row.shape[-1]
    index = lax.broadcasted_iota(jnp.int32, (16, count), 0)
    out = jnp.where(index == 0, high.astype(f32), 0.0)
    out = jnp.where(index == 1, middle.astype(f32), out)
    out = jnp.where(index == 2, low.astype(f32), out)
    return out.astype(bf16)


def minus_rows(count):
    index = lax.broadcasted_iota(jnp.int32, (16, count), 0)
    return jnp.where(index < 3, -1.0, 0.0).astype(bf16)


def attention_vmem(keys):
    return 2**20 * (ATT_BASE + 2 * keys // 1024)


def after(value, *others):
    return lax.optimization_barrier((value, others))[0]


CHEAP = pl.CostEstimate(flops=1, bytes_accessed=1, transcendentals=0)


def arrange_kernel(where_ref, tok_ref, segment_ref, valid_ref, grouped_ref, *sends):
    _, width, toks = grouped_ref.shape
    flipped = tok_ref[0].astype(f32).T.astype(bf16)
    for g in range(GROUPS):
        grouped_ref[g] = flipped[g * width : (g + 1) * width]
    segment = segment_ref[...]
    index = lax.broadcasted_iota(jnp.int32, (16, toks), 0)
    codes = jnp.where(index == 0, segment, jnp.where(valid_ref[...] == 1, segment, -1))
    for j, send in enumerate(sends):
        send[:width] = grouped_ref[jnp.bitwise_xor(where_ref[0], j)]
        send[width:] = codes.astype(f32).astype(bf16)


def arrange(where, tokens, segment_ids, valid_tokens):
    _, toks, model = tokens.shape
    width = model // GROUPS
    args = (tokens, segment_ids, valid_tokens)
    outs = [jax.ShapeDtypeStruct((GROUPS, width, toks), bf16)] + [
        jax.ShapeDtypeStruct((width + 16, toks), bf16)
    ] * GROUPS
    grouped, *sends = pl.pallas_call(
        arrange_kernel,
        name="arrange",
        grid_spec=pltpu.PrefetchScalarGridSpec(
            num_scalar_prefetch=1,
            grid=(1,),
            in_specs=[whole(a.shape) for a in args],
            out_specs=[whole(o.shape) for o in outs],
        ),
        out_shape=outs,
        cost_estimate=CHEAP,
        compiler_params=pltpu.CompilerParams(vmem_limit_bytes=SMALL_VMEM),
    )(where, *args)
    return grouped, sends


def attend(head, size, qs, kx_ref, vx_ref, own, valids, qx_ref, full_ref, atts, total_ref, peak_ref):
    toks = atts[0].shape[1]
    tile, keys = 2 * toks, kx_ref.shape[2]
    ext = size + 16

    own_keys = kx_ref[head, :size, own : own + tile]
    self_score = jnp.sum(qs[head, :size].astype(f32) * own_keys.astype(f32), axis=0, keepdims=True)
    qx_ref[0, :ext] = qs[head]
    qx_ref[0, ext:] = pieces(self_score)

    def scores(kt):
        return dot(kx_ref[head, :, kt * tile : (kt + 1) * tile], qx_ref[0], TN)

    total = None
    upcoming = scores(0)
    for kt in range(keys // tile):
        now = upcoming
        if (kt + 1) * tile < keys:
            upcoming = scores(kt + 1)
        mixed = dot(vx_ref[head, :, kt * tile : (kt + 1) * tile], jnp.exp(now).astype(bf16), NN)
        total = mixed if total is None else total + mixed
    total_ref[...] = total
    peak_ref[...] = self_score
    in_range = jnp.max(-total[size : size + 1]) < 2.0**100

    @pl.when(jnp.logical_not(in_range))
    def _():
        total_ref[...] = jnp.zeros_like(total_ref)
        peak_ref[...] = jnp.full_like(peak_ref, -4.0 * PENALTY)

        def step(kt, carry):
            span = pl.ds(pl.multiple_of(kt * tile, tile), tile)
            now = dot(kx_ref[head, :ext, span], qs[head], TN)
            peak = jnp.maximum(peak_ref[...], jnp.max(now, axis=0, keepdims=True))
            mixed = dot(vx_ref[head, :, span], jnp.exp(now - peak).astype(bf16), NN)
            total_ref[...] = total_ref[...] * jnp.exp(peak_ref[...] - peak) + mixed
            peak_ref[...] = peak
            return carry

        lax.fori_loop(0, keys // tile, step, 0)

    row_sum = -total_ref[size : size + 1]
    log_total = peak_ref[...] + jnp.log(row_sum)
    attended = jnp.where(valids, total_ref[:size] / row_sum, 0.0)
    full_ref[...] = attended
    for half in range(2):
        atts[half][...] = attended[:, half * toks : (half + 1) * toks].astype(bf16)
    qx_ref[0, ext:] = pieces(jnp.where(valids, log_total, PENALTY))


def far_kernel(parts, width, heads, where_ref, *refs):
    blocks, w_ref, qx_ref, full_ref, att_a, att_b, kx_ref, vx_ref, near_ref, valid_ref, tok_ref = refs[:11]
    far, wt, total_ref, peak_ref, far_valid = refs[11:]
    head = pl.program_id(0)
    size = width // heads
    toks = blocks.shape[2]
    tile, ext = 2 * toks, size + 16

    @pl.when(head == 0)
    def _():
        code_index = lax.broadcasted_iota(jnp.int32, (16, tile), 0).astype(f32)
        for which in range(3):
            scale = size**-0.5 if which == 0 else 1.0
            wt[which * width : (which + 1) * width, :] = (w_ref[which, 0].astype(f32) * scale).T.astype(bf16)
        for p in range(parts):
            for j in range(0, GROUPS, 2):
                b = p * GROUPS + j
                span = slice(b * toks, (b + 2) * toks)
                both = jnp.concatenate([blocks[b], blocks[b + 1]], axis=1)
                tok_ref[:, span] = both[:width]
                first = 0 if p == 0 else width
                made = dot(wt[first:], both[:width], NN).astype(bf16)
                codes = both[width:].astype(f32)
                mask = jnp.where(code_index == codes[1:2], 0.0, -PENALTY).astype(bf16)
                for h in range(heads):
                    keys = width - first + h * size
                    kx_ref[h, :size, span] = made[keys : keys + size]
                    kx_ref[h, size:ext, span] = mask
                    kx_ref[h, ext:, span] = minus_rows(tile)
                    vx_ref[h, :size, span] = made[keys + width : keys + width + size]
                    vx_ref[h, size:, span] = minus_rows(tile)
                if p == 0:
                    target, flags = (near_ref, valid_ref) if j == 0 else (far, far_valid)
                    hot = jnp.where(code_index == codes[0:1], 1.0, 0.0).astype(bf16)
                    flags[...] = jnp.broadcast_to(codes[1:2], (8, tile))
                    for h in range(heads):
                        target[h, :size] = made[h * size : (h + 1) * size]
                        target[h, size:] = hot

    valids = far_valid[0:1, :] >= 0.0
    attend(head, size, far, kx_ref, vx_ref, tile, valids, qx_ref, full_ref, (att_a, att_b), total_ref, peak_ref)


def near_kernel(size, *refs):
    near_ref, valid_ref, kx_ref, vx_ref, qx_far, full_far, qx_ref, full_ref, att_a, att_b, total_ref, peak_ref = refs
    tile = qx_far.shape[2]
    valids = valid_ref[0:1, :] >= 0.0
    qx_ref[0, :, tile:] = qx_far[0]
    full_ref[:, tile:] = full_far[...]
    attend(
        pl.program_id(0),
        size,
        near_ref,
        kx_ref,
        vx_ref,
        0,
        valids,
        qx_ref.at[:, :, :tile],
        full_ref.at[:, :tile],
        (att_a, att_b),
        total_ref,
        peak_ref,
    )


def attention_outs(heads, size, toks, tiles):
    width, count = heads * size, 2 * toks * tiles
    specs = [
        pl.BlockSpec((1, size + 32, count), lambda h, *_: (h, 0, 0)),
        pl.BlockSpec((size, count), lambda h, *_: (h, 0)),
        pl.BlockSpec((size, toks), lambda h, *_: (h, 0)),
        pl.BlockSpec((size, toks), lambda h, *_: (h, 0)),
    ]
    shapes = [
        jax.ShapeDtypeStruct((heads, size + 32, count), bf16),
        jax.ShapeDtypeStruct((width, count), f32),
        jax.ShapeDtypeStruct((width, toks), bf16),
        jax.ShapeDtypeStruct((width, toks), bf16),
    ]
    scratch = [pltpu.VMEM((size + 16, 2 * toks), f32), pltpu.VMEM((1, 2 * toks), f32)]
    return specs, shapes, scratch


def far_attention(where, blocks, weights):
    count, _, toks = blocks.shape
    parts = count // GROUPS
    width = weights.shape[2]
    heads = HEADS // GROUPS
    size = width // heads
    tile, keys = 2 * toks, count * toks
    specs, shapes, scratch = attention_outs(heads, size, toks, 1)
    shared = [
        jax.ShapeDtypeStruct((heads, size + 32, keys), bf16),
        jax.ShapeDtypeStruct((heads, size + 16, keys), bf16),
        jax.ShapeDtypeStruct((heads, size + 16, tile), bf16),
        jax.ShapeDtypeStruct((8, tile), f32),
        pltpu.HBM((width, keys), bf16),
    ]
    return pl.pallas_call(
        functools.partial(far_kernel, parts, width, heads),
        name="attention_far",
        grid_spec=pltpu.PrefetchScalarGridSpec(
            num_scalar_prefetch=1,
            grid=(heads,),
            in_specs=[whole(blocks.shape), pl.BlockSpec((3, 1, width, width), lambda h, w: (0, w[0], 0, 0))],
            out_specs=specs + [whole(x.shape) for x in shared],
            scratch_shapes=[pltpu.VMEM((heads, size + 16, tile), bf16), pltpu.VMEM((3 * width, width), bf16)]
            + scratch
            + [pltpu.VMEM((8, tile), f32)],
        ),
        out_shape=shapes + shared,
        cost_estimate=CHEAP,
        compiler_params=pltpu.CompilerParams(vmem_limit_bytes=attention_vmem(keys)),
    )(where, blocks, weights)


def near_attention(near, valid, kx, vx, qx, full):
    heads, ext, tile = near.shape
    size = ext - 16
    far_specs, _, _ = attention_outs(heads, size, tile // 2, 1)
    specs, shapes, scratch = attention_outs(heads, size, tile // 2, 2)
    return pl.pallas_call(
        functools.partial(near_kernel, size),
        name="attention_near",
        grid=(heads,),
        in_specs=[whole(x.shape) for x in (near, valid, kx, vx)] + far_specs[:2],
        out_specs=specs,
        scratch_shapes=scratch,
        out_shape=shapes,
        cost_estimate=CHEAP,
        compiler_params=pltpu.CompilerParams(vmem_limit_bytes=attention_vmem(kx.shape[2])),
    )(near, valid, kx, vx, qx, full)


def prepare_kernel(size, *refs):
    grads, full_ref, gx_ref = refs[:GROUPS], refs[GROUPS], refs[GROUPS + 1]
    toks = grads[0].shape[1]
    for head in range(gx_ref.shape[0]):
        rows = slice(head * size, (head + 1) * size)
        for j in range(GROUPS):
            span = slice(j * toks, (j + 1) * toks)
            grad = grads[j][rows, :]
            gx_ref[head, :size, span] = grad
            gx_ref[head, size:, span] = pieces(
                jnp.sum(grad.astype(f32) * full_ref[rows, span], axis=0, keepdims=True)
            )


def prepare(grads, full, size):
    width, count = full.shape
    out = jax.ShapeDtypeStruct((width // size, size + 16, count), bf16)
    return pl.pallas_call(
        functools.partial(prepare_kernel, size),
        name="prepare_backward",
        grid=(1,),
        in_specs=[whole(x.shape) for x in (*grads, full)],
        out_specs=whole(out.shape),
        out_shape=out,
        cost_estimate=CHEAP,
        compiler_params=pltpu.CompilerParams(vmem_limit_bytes=SMALL_VMEM),
    )(*grads, full)


def backward_kernel(size, tile, last, qx_ref, gx_ref, kx_ref, vx_ref, *refs):
    if last:
        dq_in, dq_ref, dk_ref, dv_ref = refs
    else:
        dq_ref, dk_ref, dv_ref = refs
    tiles = [slice(i * tile, (i + 1) * tile) for i in range(qx_ref.shape[2] // tile)]
    dq = [None] * len(tiles)
    for kt in range(kx_ref.shape[2] // tile):
        kspan = slice(kt * tile, (kt + 1) * tile)
        dk = dv = None
        for qt, qspan in enumerate(tiles):
            probs = jnp.exp(dot(qx_ref[0, :, qspan], kx_ref[0, :, kspan], TN))
            slopes = dot(gx_ref[0, :, qspan], vx_ref[0, :, kspan], TN)
            probs_low = probs.astype(bf16)
            grad_scores = (probs * slopes).astype(bf16)
            dv_new = dot(gx_ref[0, :size, qspan], probs_low, NN)
            dk_new = dot(qx_ref[0, :size, qspan], grad_scores, NN)
            dq_new = dot(kx_ref[0, :size, kspan], grad_scores, NT)
            dv = dv_new if dv is None else dv + dv_new
            dk = dk_new if dk is None else dk + dk_new
            dq[qt] = dq_new if dq[qt] is None else dq[qt] + dq_new
        dv_ref[:, kspan] = dv.astype(bf16)
        dk_ref[:, kspan] = dk.astype(bf16)
    for qt, qspan in enumerate(tiles):
        if last:
            dq_ref[:, qspan] = ((dq[qt] + dq_in[:, qspan]) * size**-0.5).astype(bf16)
        else:
            dq_ref[:, qspan] = dq[qt]


def backward_attention(head, part, cuts, qx, gx, kx, vx, dq=None):
    size, count = vx.shape[1] - 16, qx.shape[2]
    keys = vx.shape[2] // cuts
    last = dq is not None
    dq_shape, sum_shape = (size, count), (size, keys)
    return pl.pallas_call(
        functools.partial(backward_kernel, size, count // 2, last),
        name="attention_backward",
        grid=(1,),
        in_specs=[
            pl.BlockSpec((1, size + 32, count), lambda i: (head, 0, 0)),
            pl.BlockSpec((1, size + 16, count), lambda i: (head, 0, 0)),
            pl.BlockSpec((1, size + 32, keys), lambda i: (head, 0, part)),
            pl.BlockSpec((1, size + 16, keys), lambda i: (head, 0, part)),
        ]
        + [whole(dq_shape)] * last,
        out_specs=[whole(dq_shape), whole(sum_shape), whole(sum_shape)],
        out_shape=[
            jax.ShapeDtypeStruct(dq_shape, bf16 if last else f32),
            jax.ShapeDtypeStruct(sum_shape, bf16),
            jax.ShapeDtypeStruct(sum_shape, bf16),
        ],
        cost_estimate=CHEAP,
        compiler_params=pltpu.CompilerParams(vmem_limit_bytes=attention_vmem(vx.shape[2])),
    )(qx, gx, kx, vx, *([dq] if last else []))


def project_kernel(parts, heads, cuts, where_ref, *refs):
    tok_ref, wq_ref, wk_ref, wv_ref = refs[:4]
    refs = refs[4:]
    dq = jnp.concatenate([ref[...] for ref in refs[:heads]])
    piles, refs = refs[heads : heads + 2 * heads * cuts], refs[heads + 2 * heads * cuts :]
    dk, dv = (
        jnp.concatenate(
            [jnp.concatenate([ref[...] for ref in pile[h * cuts : (h + 1) * cuts]], axis=1) for h in range(heads)]
        )
        for pile in (piles[: heads * cuts], piles[heads * cuts :])
    )
    backs, wgrads, scratch = refs[:parts], refs[parts : 2 * parts], refs[2 * parts]
    width, keys = tok_ref.shape
    count = keys // parts
    toks = count // GROUPS

    scratch[0] = dot(tok_ref[:, :count], dq, NT).astype(bf16)
    scratch[1] = dot(tok_ref[...], dk, NT).astype(bf16)
    scratch[2] = dot(tok_ref[...], dv, NT).astype(bf16)
    for p in reversed(range(parts)):
        span = slice(p * count, (p + 1) * count)
        back = dot(wk_ref[0], dk[:, span], NN) + dot(wv_ref[0], dv[:, span], NN)
        if p == 0:
            back += dot(wq_ref[0], dq, NN)
        for j in range(GROUPS):
            backs[p][j] = back[:, j * toks : (j + 1) * toks].astype(bf16)
    chunk = width // parts
    for p in range(parts):
        rows = pl.ds(pl.multiple_of(jnp.bitwise_xor(where_ref[1], p) * chunk, chunk), chunk)
        wgrads[p][...] = scratch[:, rows, :]


def project_back(where, parts, tok, weights, dqs, dks, dvs):
    width, keys = tok.shape
    toks = keys // parts // GROUPS
    heads, cuts = len(dqs), len(dks) // len(dqs)
    flat = [*dqs, *dks, *dvs]
    weight_spec = pl.BlockSpec((1, width, width), lambda i, w: (w[0], 0, 0))
    outs = [jax.ShapeDtypeStruct((GROUPS, width, toks), bf16)] * parts + [
        jax.ShapeDtypeStruct((3, width // parts, width), bf16)
    ] * parts
    results = pl.pallas_call(
        functools.partial(project_kernel, parts, heads, cuts),
        name="project_back",
        grid_spec=pltpu.PrefetchScalarGridSpec(
            num_scalar_prefetch=1,
            grid=(1,),
            in_specs=[whole(tok.shape)] + [weight_spec] * 3 + [whole(x.shape) for x in flat],
            out_specs=[whole(o.shape) for o in outs],
            scratch_shapes=[pltpu.VMEM((3, width, width), bf16)],
        ),
        out_shape=outs,
        cost_estimate=CHEAP,
        compiler_params=pltpu.CompilerParams(vmem_limit_bytes=attention_vmem(keys)),
    )(where, tok, *weights, *flat)
    return results[:parts], results[parts:]


def norm_parts(values):
    mean = jnp.mean(values, axis=0, keepdims=True)
    center = values - mean
    spread = jnp.mean(center * center, axis=0, keepdims=True)
    scale = lax.rsqrt(spread + 1e-06)
    return center * scale, scale


def norm_back(normal, scale, grad):
    mean = jnp.mean(grad, axis=0, keepdims=True)
    cross = jnp.mean(grad * normal, axis=0, keepdims=True)
    return (grad - mean - normal * cross) * scale


def middle_kernel(where_ref, *refs):
    slot_ref, far_ref, cot_ref, valid_ref, vec_ref, w_ref, fi_ref, fo_ref = refs[:8]
    refs = refs[8:]
    mixed_ref, first_grad_ref = refs[:2]
    sends = refs[2 : 2 + GROUPS]
    att, narrow_ref, wide_ref, first_low_ref, vec_out_ref = refs[2 + GROUPS : 7 + GROUPS]
    first_ref, slope_ref, second_ref, gfirst_ref, grad_att = refs[7 + GROUPS :]
    _, width, toks = slot_ref.shape
    model = width * GROUPS
    own_group = where_ref[0]
    vecs = vec_ref[...].T
    gain_one, bias_one = vecs[:, 0:1], vecs[:, 1:2]
    gain_two, bias_two = vecs[:, 2:3], vecs[:, 3:4]

    for j in range(GROUPS):
        start = pl.multiple_of(jnp.bitwise_xor(own_group, j) * width, width)
        att[pl.ds(start, width), :] = slot_ref[j] if j < 2 else far_ref[j - 2]
    tok = jnp.concatenate([slot_ref[2 + g] for g in range(GROUPS)])
    first_pre = tok.astype(f32) + dot(w_ref[...], att[...], TN)
    normal_one, scale_one = norm_parts(first_pre)
    first_ref[...] = normal_one
    first = normal_one * gain_one + bias_one
    narrow_ref[0] = first.astype(bf16)
    for g in range(GROUPS):
        mine = slice(g * width, (g + 1) * width)
        pre = dot(fi_ref[g], narrow_ref[0, mine, :], TN)
        phi = 0.5 * (1.0 + lax.erf(pre * 0.5**0.5))
        density = jnp.exp(-0.5 * pre * pre) * 0.3989422804014327
        wide_ref[1, g] = (pre * phi).astype(bf16)
        slope_ref[g] = phi + pre * density
        second_ref[mine, :] = (first_ref[mine, :] * gain_one[mine] + bias_one[mine]) + dot(fo_ref[g], wide_ref[1, g], NN)
    normal_two, scale_two = norm_parts(second_ref[...])
    mixed_ref[0] = (normal_two * gain_two + bias_two).T
    cot = cot_ref[0].T
    grad_gain_two = jnp.sum(cot * normal_two, axis=1, keepdims=True)
    grad_bias_two = jnp.sum(cot, axis=1, keepdims=True)
    grad_second = norm_back(normal_two, scale_two, cot * gain_two)
    second_ref[...] = grad_second
    grad_low = grad_second.astype(bf16)
    narrow_ref[1] = grad_low
    for g in range(GROUPS):
        mine = slice(g * width, (g + 1) * width)
        ghp = (dot(fo_ref[g], grad_low[mine, :], TN) * slope_ref[g]).astype(bf16)
        wide_ref[0, g] = ghp
        gfirst_ref[mine, :] = second_ref[mine, :] + dot(fi_ref[g], ghp, NN)
    grad_first = gfirst_ref[...]
    normal_one = first_ref[...]
    grad_gain_one = jnp.sum(grad_first * normal_one, axis=1, keepdims=True)
    grad_bias_one = jnp.sum(grad_first, axis=1, keepdims=True)
    first_grad = norm_back(normal_one, scale_one, grad_first * gain_one)
    first_grad_ref[...] = first_grad
    first_low = first_grad.astype(bf16)
    first_low_ref[...] = first_low
    grad_att[...] = jnp.where(valid_ref[...] == 1, dot(w_ref[...], first_low, NN), 0.0).astype(bf16)
    for j in range(GROUPS):
        start = pl.multiple_of(jnp.bitwise_xor(own_group, j) * width, width)
        sends[j][...] = grad_att[pl.ds(start, width), :]

    lane = lax.broadcasted_iota(jnp.int32, (model, 128), 1)
    vectors = jnp.where(lane == 0, grad_gain_one, 0.0)
    vectors = jnp.where(lane == 1, grad_bias_one, vectors)
    vectors = jnp.where(lane == 2, grad_gain_two, vectors)
    vectors = jnp.where(lane == 3, grad_bias_two, vectors)
    vec_out_ref[...] = vectors.astype(bf16)


def middle(where, slots, far, cotangent, valid, vecs, out_weight, ffn_in, ffn_out_t):
    _, width, toks = slots.shape
    model = width * GROUPS
    wide = ffn_in.shape[2]
    args = (slots, far, cotangent, valid, vecs, out_weight, ffn_in, ffn_out_t)
    outs = (
        [jax.ShapeDtypeStruct((1, toks, model), f32), pltpu.HBM((model, toks), f32)]
        + [jax.ShapeDtypeStruct((width, toks), bf16)] * GROUPS
        + [
            jax.ShapeDtypeStruct((model, toks), bf16),
            jax.ShapeDtypeStruct((2, model, toks), bf16),
            jax.ShapeDtypeStruct((2, GROUPS, wide, toks), bf16),
            jax.ShapeDtypeStruct((model, toks), bf16),
            jax.ShapeDtypeStruct((model, 128), bf16),
        ]
    )
    results = pl.pallas_call(
        middle_kernel,
        name="middle",
        grid_spec=pltpu.PrefetchScalarGridSpec(
            num_scalar_prefetch=1,
            grid=(1,),
            in_specs=[whole(a.shape) for a in args],
            out_specs=[whole(o.shape) for o in outs],
            scratch_shapes=[
                pltpu.VMEM((model, toks), f32),
                pltpu.VMEM((GROUPS, wide, toks), f32),
                pltpu.VMEM((model, toks), f32),
                pltpu.VMEM((model, toks), f32),
                pltpu.VMEM((model, toks), bf16),
            ],
        ),
        out_shape=outs,
        cost_estimate=CHEAP,
        compiler_params=pltpu.CompilerParams(vmem_limit_bytes=VMEM_BYTES),
    )(where, *args)
    return results[0], results[1], results[2 : 2 + GROUPS], results[2 + GROUPS :]


def swapped(slot, odd):
    return jnp.where(odd, slot, (slot % 2) * 2 + slot // 2)


def outer_kernel(parts, slot, where_ref, att, narrow_ref, wide_ref, first_low_ref, vec_ref, near_ref, far_ref):
    model = att.shape[0]
    width = model // GROUPS
    wide = wide_ref.shape[2]
    half = parts // 2
    own_group, part = where_ref[0], jnp.bitwise_xor(where_ref[1], slot)
    ffn_rows, out_rows = width // half, model // (parts * GROUPS)
    array, piece = part // half, part % half
    tiles, wide_tiles = model // 128, wide // 128

    out_start = pl.multiple_of(part * (model // parts), model // parts)
    out = dot(att[pl.ds(out_start, model // parts), :], first_low_ref[...], NT).astype(bf16)
    for target, slots in ((near_ref, (0, 1)), (far_ref, (2, 3))):
        for index, m in enumerate(slots):
            group = jnp.bitwise_xor(own_group, swapped(m, part % 2 == 1))
            start = pl.multiple_of(group * width + piece * ffn_rows, ffn_rows)
            made = dot(narrow_ref[array, pl.ds(start, ffn_rows), :], wide_ref[array, group], NT).astype(bf16)
            for t in range(wide_tiles):
                target[index, t * ffn_rows : (t + 1) * ffn_rows] = made[:, t * 128 : (t + 1) * 128]
    base = wide_tiles * ffn_rows
    for g in range(GROUPS):
        distance = jnp.bitwise_xor(own_group, g)
        m = swapped(distance, part % 2 == 1)
        rows = slice(g * out_rows, (g + 1) * out_rows)
        vec_start = pl.multiple_of(part * (model // parts) + g * out_rows, out_rows)
        vec = vec_ref[pl.ds(vec_start, out_rows), :]

        def put(target, index):
            for t in range(tiles):
                span = slice(base + t * out_rows, base + (t + 1) * out_rows)
                target[index, span] = out[rows, t * 128 : (t + 1) * 128]
            target[index, base + tiles * out_rows : base + (tiles + 1) * out_rows] = vec

        @pl.when(m < 2)
        def _():
            put(near_ref, m)

        @pl.when(m >= 2)
        def _():
            put(far_ref, m - 2)


def outer_products(where, parts, slot, kept):
    att, narrow, wide_pair, _, _ = kept
    model = att.shape[0]
    wide = wide_pair.shape[2]
    rows = (wide // 128) * (model // GROUPS // (parts // 2)) + (model // 128 + 1) * (model // (parts * GROUPS))
    outs = [jax.ShapeDtypeStruct((2, rows, 128), bf16)] * 2
    return pl.pallas_call(
        functools.partial(outer_kernel, parts, slot),
        name="outer_products",
        grid_spec=pltpu.PrefetchScalarGridSpec(
            num_scalar_prefetch=1,
            grid=(1,),
            in_specs=[whole(a.shape) for a in kept],
            out_specs=[whole(o.shape) for o in outs],
        ),
        out_shape=outs,
        cost_estimate=CHEAP,
        compiler_params=pltpu.CompilerParams(vmem_limit_bytes=SMALL_VMEM),
    )(where, *kept)


def token_grad_kernel(where_ref, *refs):
    slots = refs[:GROUPS]
    first_grad_ref, out_ref, scratch = refs[GROUPS:]
    width = slots[0].shape[0]
    for j in range(GROUPS):
        start = pl.multiple_of(jnp.bitwise_xor(where_ref[0], j) * width, width)
        mine = pl.ds(start, width)
        scratch[mine, :] = first_grad_ref[mine, :] + slots[j][...].astype(f32)
    out_ref[0] = scratch[...].T


def token_grad(where, slots, first_grad):
    model, toks = first_grad.shape

    return pl.pallas_call(
        token_grad_kernel,
        name="token_grad",
        grid_spec=pltpu.PrefetchScalarGridSpec(
            num_scalar_prefetch=1,
            grid=(1,),
            in_specs=[whole(s.shape) for s in slots] + [whole(first_grad.shape)],
            out_specs=whole((1, toks, model)),
            scratch_shapes=[pltpu.VMEM((model, toks), f32)],
        ),
        out_shape=jax.ShapeDtypeStruct((1, toks, model), f32),
        cost_estimate=CHEAP,
        compiler_params=pltpu.CompilerParams(vmem_limit_bytes=VMEM_BYTES),
    )(where, *slots, first_grad)


def row_distances(depth):
    steps = depth.bit_length() - 1
    even = [sum(((m >> (steps - 1 - i)) & 1) << i for i in range(steps)) for m in range(depth)]
    return even, list(range(depth))


def weight_grad_kernel(parts, depth, model, wide, where_ref, *refs):
    slots = refs[:parts]
    out_ref, in_ref, ffn_out_ref, vec_ref, scratch, vec_scratch = refs[parts:]
    step = pl.program_id(0)
    group = jnp.bitwise_xor(step, where_ref[0])
    piece = slots[0].shape[2]
    width = model // GROUPS
    half = parts // 2
    ffn_rows, out_rows = width // half, model // (parts * GROUPS)
    tiles, wide_tiles = model // 128, wide // 128
    even, odd = row_distances(depth)
    for p in range(parts):
        part = jnp.bitwise_xor(where_ref[1], p)
        for z in range(depth):
            distance = jnp.where(part % 2 == 1, odd[z], even[z])
            scratch[part, jnp.bitwise_xor(where_ref[2], distance)] = slots[p][0, z].astype(f32)

    def rows(part, first, count):
        last = first + count
        cuts = [first] + [c for c in range(0, depth * piece, piece) if first < c < last] + [last]
        return jnp.concatenate(
            [scratch[part, x // piece, x % piece : x % piece + y - x, :] for x, y in zip(cuts, cuts[1:])]
        )

    base = wide_tiles * ffn_rows
    for part in range(parts):
        target = in_ref if part < half else ffn_out_ref
        mine = slice((part % half) * ffn_rows, (part % half + 1) * ffn_rows)
        for t in range(wide_tiles):
            target[0, mine, t * 128 : (t + 1) * 128] = rows(part, t * ffn_rows, ffn_rows)
        for t in range(tiles):
            out_ref[part, 0, :, t * 128 : (t + 1) * 128] = rows(part, base + t * out_rows, out_rows)
        start = pl.multiple_of(part * (model // parts) + group * out_rows, out_rows)
        vec_scratch[pl.ds(start, out_rows), :] = rows(part, base + tiles * out_rows, out_rows)

    @pl.when(step == GROUPS - 1)
    def _():
        vec_ref[...] = vec_scratch[...].T[:8]


def weight_grads(where, slots, model, wide):
    parts = len(slots)
    _, depth, piece, _ = slots[0].shape
    width = model // GROUPS
    out_rows = model // (parts * GROUPS)

    def slot_spec(p):
        def place(j, w):
            return (swapped(j, jnp.bitwise_xor(w[1], p) % 2 == 1), 0, 0, 0)

        return pl.BlockSpec((1, depth, piece, 128), place)

    out, ffn_in, ffn_out_t, vectors = pl.pallas_call(
        functools.partial(weight_grad_kernel, parts, depth, model, wide),
        name="weight_grads",
        grid_spec=pltpu.PrefetchScalarGridSpec(
            num_scalar_prefetch=1,
            grid=(GROUPS,),
            in_specs=[slot_spec(p) for p in range(parts)],
            out_specs=[
                pl.BlockSpec((parts, 1, out_rows, model), lambda j, w: (0, jnp.bitwise_xor(j, w[0]), 0, 0)),
                pl.BlockSpec((1, width, wide), lambda j, w: (jnp.bitwise_xor(j, w[0]), 0, 0)),
                pl.BlockSpec((1, width, wide), lambda j, w: (jnp.bitwise_xor(j, w[0]), 0, 0)),
                pl.BlockSpec((8, model), lambda j, w: (0, 0)),
            ],
            scratch_shapes=[pltpu.VMEM((parts, depth, piece, 128), f32), pltpu.VMEM((model, 128), f32)],
        ),
        out_shape=[
            jax.ShapeDtypeStruct((parts, GROUPS, out_rows, model), f32),
            jax.ShapeDtypeStruct((GROUPS, width, wide), f32),
            jax.ShapeDtypeStruct((GROUPS, width, wide), f32),
            jax.ShapeDtypeStruct((8, model), f32),
        ],
        cost_estimate=CHEAP,
        compiler_params=pltpu.CompilerParams(vmem_limit_bytes=SMALL_VMEM),
    )(where, *slots)
    return out.reshape(model, model), ffn_in, ffn_out_t, vectors


def qkv_grad_kernel(parts, where_ref, *refs):
    slots = refs[:parts]
    outs = refs[parts:]
    chunk = slots[0].shape[2]
    for p in range(parts):
        part = jnp.bitwise_xor(where_ref[1], p)
        start = pl.multiple_of(part * chunk, chunk)
        for m in range(GROUPS):
            group = jnp.bitwise_xor(where_ref[0], swapped(m, part % 2 == 1))
            for which in range(3):
                outs[which][group, pl.ds(start, chunk), :] = slots[p][m, which].astype(f32)


def qkv_grads(where, slots):
    parts = len(slots)
    _, _, chunk, width = slots[0].shape

    out = (GROUPS, width, width)
    return pl.pallas_call(
        functools.partial(qkv_grad_kernel, parts),
        name="qkv_grads",
        grid_spec=pltpu.PrefetchScalarGridSpec(
            num_scalar_prefetch=1,
            grid=(1,),
            in_specs=[whole(s.shape) for s in slots],
            out_specs=[whole(out)] * 3,
        ),
        out_shape=[jax.ShapeDtypeStruct(out, f32)] * 3,
        cost_estimate=CHEAP,
        compiler_params=pltpu.CompilerParams(vmem_limit_bytes=VMEM_BYTES),
    )(where, *slots)


def add_low(terms):
    total = terms[0].astype(f32)
    for term in terms[1:]:
        total = total + term.astype(f32)
    return total.astype(bf16)


def shards(
    tokens,
    segment_ids,
    valid_tokens,
    q_weight,
    k_weight,
    v_weight,
    out_weight,
    gain_one,
    bias_one,
    ffn_in,
    ffn_out,
    gain_two,
    bias_two,
    cotangent,
):
    seq = lax.axis_size("seq")
    depth = lax.axis_size("rows")
    parts = seq // GROUPS
    _, toks, model = tokens.shape
    width = model // GROUPS
    wide = ffn_in.shape[2]
    place = lax.axis_index("seq")
    own_group, own_part = place // parts, place % parts
    own_row = lax.axis_index("rows")
    where = jnp.stack([own_group, own_part, own_row]).astype(jnp.int32)

    def swap(value, distance):
        return lax.ppermute(value, "seq", [(k, k ^ distance) for k in range(seq)])

    def across(value):
        return [value[0]] + [swap(value[j], parts * j) for j in range(1, GROUPS)]

    def group_swap(value, step):
        apart = [(1, 2), (2, 1)][step]
        return lax.ppermute(value, "seq", [(k, k ^ parts * apart[k % parts % 2]) for k in range(seq)])

    row_steps = depth.bit_length() - 1

    def row_swap(value, step):
        pairs = []
        for k in range(seq):
            distance = 1 << (row_steps - 1 - step if k % parts % 2 else step)
            pairs += [(k * depth + z, k * depth + (z ^ distance)) for z in range(depth)]
        return lax.ppermute(value, ("seq", "rows"), pairs)

    grouped, sends = arrange(where, tokens, segment_ids, valid_tokens)
    mine = across(sends)
    others = [swap(jnp.stack(mine), p) for p in range(1, parts)]
    blocks = jnp.stack(mine + [x[j] for x in others for j in range(GROUPS)])

    qx_far, full_far, att_c, att_d, kx, vx, near, near_valid, tok = far_attention(
        where, blocks, jnp.stack([q_weight, k_weight, v_weight])
    )
    att_far = jnp.stack([swap(att_c, parts * 2), swap(att_d, parts * 3)])
    qx, full, att_a, att_b = near_attention(near, near_valid, kx, vx, qx_far, full_far)
    att_b = swap(att_b, parts)
    slots = jnp.concatenate([att_a[None], att_b[None], grouped])
    vecs = jnp.pad(jnp.stack(after([gain_one, bias_one, gain_two, bias_two], att_a)), ((0, 4), (0, 0)))
    mixed, first_grad, sends, kept = middle(
        where, slots, att_far, cotangent, valid_tokens, vecs, out_weight, ffn_in, jnp.swapaxes(ffn_out, 1, 2)
    )
    grads = across(sends)

    pays = [outer_products(where, parts, p, kept) for p in range(1, parts)]
    moved = [[swap(x, p) for x in pays[p - 1]] for p in range(1, parts)]
    pay = outer_products(where, parts, 0, after(kept, pays))
    gx = prepare(after(grads, pay), full, model // HEADS)
    moved = after(moved, gx)
    low = add_low([pay[0]] + [x[0] for x in moved])
    high = add_low([pay[1]] + [x[1] for x in moved])

    heads, cuts = HEADS // GROUPS, 2
    calls = [(head, part) for head in range(heads) for part in range(cuts)]
    dqs, dks, dvs = [], [], []

    def work(*ready):
        head, part = calls.pop(0)
        dq, dk, dv = backward_attention(
            head,
            part,
            cuts,
            qx,
            after(gx, ready),
            kx,
            vx,
            dqs.pop() if part else None,
        )
        dqs.append(dq)
        dks.append(dk)
        dvs.append(dv)
        return dq

    moved = group_swap(high, 0)
    first = work(high, low)
    moved = after(moved, work(first))
    low, high = add_low([low[0], moved[0]]), add_low([low[1], moved[1]])
    moved = group_swap(high, 1)
    piece = add_low([low, after(moved, work(high, low))]).reshape(depth, -1, 128)
    even, odd = row_distances(depth)
    picks = [own_row ^ jnp.where(own_part % 2 == 1, odd[m], even[m]) for m in range(depth)]
    piece = jnp.stack([lax.dynamic_index_in_dim(piece, z, 0, False) for z in picks])
    for step in range(row_steps):
        count = piece.shape[0] // 2
        low, high = piece[:count], piece[count:]
        moved = row_swap(high, step)
        if len(calls) > 1:
            moved = after(moved, work(high, low))
        piece = add_low([low, moved])
    moved = row_swap(piece, row_steps - 1)
    while calls:
        done = work(piece)
        moved, dqs[-1] = after((moved, dqs[-1]), done)
    piece = jnp.concatenate([piece, moved])
    step = row_steps - 2
    moved = row_swap(piece, step)
    backs, wgrads = project_back(where, parts, tok, (q_weight, k_weight, v_weight), after(dqs, piece), dks, dvs)
    piece = jnp.concatenate([piece, moved])
    for step in reversed(range(row_steps - 2)):
        piece = jnp.concatenate([piece, row_swap(piece, step)])
    wgrads, backs, piece = after((wgrads, backs, piece[None]), piece)
    swaps = [[swap(x[p], p) for p in range(1, parts)] for x in (wgrads, backs)]
    moved = group_swap(piece, 1)
    quarter, back_sum = add_low([wgrads[0]] + swaps[0]), add_low([backs[0]] + swaps[1])
    for step in range(row_steps - 1):
        quarter = add_low([quarter, row_swap(quarter, step)])
    piece = jnp.concatenate([piece, moved])
    quarter, back_sum, piece = after((quarter, back_sum, piece), quarter)
    moved = group_swap(piece, 0)
    quarter = add_low([quarter, row_swap(quarter, row_steps - 1)])
    quarter = jnp.stack([quarter, group_swap(quarter, 1)])
    piece = jnp.concatenate([piece, moved])
    quarter, back_sum, piece = after((quarter, back_sum, piece), quarter)
    slots = [piece] + [swap(piece, p) for p in range(1, parts)]
    back_moved = across(back_sum)
    moved = group_swap(quarter, 0)
    grad_out_weight, grad_ffn_in, grad_ffn_out_t, vectors = weight_grads(where, slots, model, wide)
    moved, back_moved = after((moved, back_moved), vectors)
    quarter = jnp.concatenate([quarter, moved])
    moved = [swap(quarter, p) for p in range(1, parts)]
    grad_tokens = token_grad(where, back_moved, first_grad)
    grad_q, grad_k, grad_v = qkv_grads(where, [quarter] + after(moved, grad_tokens))

    return (
        mixed,
        grad_tokens,
        grad_q,
        grad_k,
        grad_v,
        grad_out_weight,
        vectors[0],
        vectors[1],
        grad_ffn_in,
        jnp.swapaxes(grad_ffn_out_t, 1, 2),
        vectors[2],
        vectors[3],
    )


def solution(mesh):
    tokens = P("rows", "seq", None)
    flags = P("rows", "seq")
    in_specs = (tokens, flags, flags) + (P(),) * 10 + (tokens,)
    out_specs = (tokens, tokens) + (P(),) * 10
    return jax.shard_map(shards, mesh=mesh, in_specs=in_specs, out_specs=out_specs, check_vma=False)
```

```python
import functools

import jax
import jax.numpy as jnp
from jax import lax
from jax.experimental import pallas as pl
from jax.experimental.pallas import tpu as pltpu
from jax.sharding import PartitionSpec as P

HEADS = 12
GROUPS = 4
PENALTY = 2.0**30
VMEM_BYTES = 36 * 2**20
SMALL_VMEM = 20 * 2**20
ATT_BASE = 9
bf16 = jnp.bfloat16
f32 = jnp.float32


def dot(a, b, dims):
    return lax.dot_general(a, b, (dims, ((), ())), preferred_element_type=f32)


NN = ((1,), (0,))
TN = ((0,), (0,))
NT = ((1,), (1,))


def whole(shape):
    return pl.BlockSpec(shape, lambda *_: (0,) * len(shape), pipeline_mode=pl.Buffered(1))


def pieces(row):
    high = row.astype(bf16)
    rest = row - high.astype(f32)
    middle = rest.astype(bf16)
    low = (rest - middle.astype(f32)).astype(bf16)
    count = row.shape[-1]
    index = lax.broadcasted_iota(jnp.int32, (16, count), 0)
    out = jnp.where(index == 0, high.astype(f32), 0.0)
    out = jnp.where(index == 1, middle.astype(f32), out)
    out = jnp.where(index == 2, low.astype(f32), out)
    return out.astype(bf16)


def minus_rows(count):
    index = lax.broadcasted_iota(jnp.int32, (16, count), 0)
    return jnp.where(index < 3, -1.0, 0.0).astype(bf16)


def attention_vmem(keys):
    return 2**20 * (ATT_BASE + 2 * keys // 1024)


def after(value, *others):
    return lax.optimization_barrier((value, others))[0]


CHEAP = pl.CostEstimate(flops=1, bytes_accessed=1, transcendentals=0)


def arrange_kernel(where_ref, tok_ref, code_ref, grouped_ref, *sends):
    _, width, _ = grouped_ref.shape
    flipped = tok_ref[0].astype(f32).T.astype(bf16)
    for g in range(GROUPS):
        grouped_ref[g] = flipped[g * width : (g + 1) * width]
    for j, send in enumerate(sends):
        send[:width] = grouped_ref[jnp.bitwise_xor(where_ref[0], j)]
        send[width:] = code_ref[...]


def arrange(where, tokens, segment_ids, valid_tokens):
    _, toks, model = tokens.shape
    width = model // GROUPS
    index = lax.broadcasted_iota(jnp.int32, (16, toks), 0)
    codes = jnp.where(index == 0, segment_ids, jnp.where(valid_tokens == 1, segment_ids, -1))
    args = (tokens, codes.astype(bf16))
    outs = [jax.ShapeDtypeStruct((GROUPS, width, toks), bf16)] + [
        jax.ShapeDtypeStruct((width + 16, toks), bf16)
    ] * GROUPS
    grouped, *sends = pl.pallas_call(
        arrange_kernel,
        name="arrange",
        grid_spec=pltpu.PrefetchScalarGridSpec(
            num_scalar_prefetch=1,
            grid=(1,),
            in_specs=[whole(a.shape) for a in args],
            out_specs=[whole(o.shape) for o in outs],
        ),
        out_shape=outs,
        cost_estimate=CHEAP,
        compiler_params=pltpu.CompilerParams(vmem_limit_bytes=SMALL_VMEM),
    )(where, *args)
    return grouped, sends


def attend(head, size, qs, kx_ref, vx_ref, own, valids, qx_ref, full_ref, atts, total_ref, peak_ref):
    toks = atts[0].shape[1]
    tile, keys = 2 * toks, kx_ref.shape[2]
    ext = size + 16

    own_keys = kx_ref[head, :size, own : own + tile]
    self_score = jnp.sum(qs[head, :size].astype(f32) * own_keys.astype(f32), axis=0, keepdims=True)
    qx_ref[0, :ext] = qs[head]
    qx_ref[0, ext:] = pieces(self_score)

    step = 256

    def scores(first):
        return dot(kx_ref[head, :, first : first + step], qx_ref[0], TN)

    total = None
    upcoming = [scores(0), scores(step)]
    for first in range(0, keys, step):
        now = upcoming.pop(0)
        if first + 2 * step < keys:
            upcoming.append(scores(first + 2 * step))
        mixed = dot(vx_ref[head, :, first : first + step], jnp.exp(now).astype(bf16), NN)
        total = mixed if total is None else total + mixed
    total_ref[...] = total
    peak_ref[...] = self_score
    in_range = jnp.max(-total[size : size + 1]) < 2.0**100

    @pl.when(jnp.logical_not(in_range))
    def _():
        total_ref[...] = jnp.zeros_like(total_ref)
        peak_ref[...] = jnp.full_like(peak_ref, -4.0 * PENALTY)

        def step(kt, carry):
            span = pl.ds(pl.multiple_of(kt * tile, tile), tile)
            now = dot(kx_ref[head, :ext, span], qs[head], TN)
            peak = jnp.maximum(peak_ref[...], jnp.max(now, axis=0, keepdims=True))
            mixed = dot(vx_ref[head, :, span], jnp.exp(now - peak).astype(bf16), NN)
            total_ref[...] = total_ref[...] * jnp.exp(peak_ref[...] - peak) + mixed
            peak_ref[...] = peak
            return carry

        lax.fori_loop(0, keys // tile, step, 0)

    row_sum = -total_ref[size : size + 1]
    log_total = peak_ref[...] + jnp.log(row_sum)
    attended = jnp.where(valids, total_ref[:size] / row_sum, 0.0)
    full_ref[...] = attended
    for half in range(2):
        atts[half][...] = attended[:, half * toks : (half + 1) * toks].astype(bf16)
    qx_ref[0, ext:] = pieces(jnp.where(valids, log_total, PENALTY))


def far_kernel(parts, width, heads, where_ref, *refs):
    blocks, w_ref, qx_ref, full_ref, att_a, att_b, kx_ref, vx_ref, near_ref, valid_ref, tok_ref = refs[:11]
    far, wt, total_ref, peak_ref, far_valid = refs[11:]
    head = pl.program_id(0)
    size = width // heads
    toks = blocks.shape[2]
    tile, ext = 2 * toks, size + 16

    @pl.when(head == 0)
    def _():
        code_index = lax.broadcasted_iota(jnp.int32, (16, tile), 0).astype(f32)
        for which in range(3):
            scale = size**-0.5 if which == 0 else 1.0
            wt[which * width : (which + 1) * width, :] = (w_ref[which, 0].astype(f32) * scale).T.astype(bf16)
        for p in range(parts):
            for j in range(0, GROUPS, 2):
                b = p * GROUPS + j
                span = slice(b * toks, (b + 2) * toks)
                both = jnp.concatenate([blocks[b], blocks[b + 1]], axis=1)
                tok_ref[:, span] = both[:width]
                first = 0 if p == 0 else width
                made = dot(wt[first:], both[:width], NN).astype(bf16)
                codes = both[width:].astype(f32)
                mask = jnp.where(code_index == codes[1:2], 0.0, -PENALTY).astype(bf16)
                for h in range(heads):
                    keys = width - first + h * size
                    kx_ref[h, :size, span] = made[keys : keys + size]
                    kx_ref[h, size:ext, span] = mask
                    kx_ref[h, ext:, span] = minus_rows(tile)
                    vx_ref[h, :size, span] = made[keys + width : keys + width + size]
                    vx_ref[h, size:, span] = minus_rows(tile)
                if p == 0:
                    target, flags = (near_ref, valid_ref) if j == 0 else (far, far_valid)
                    hot = jnp.where(code_index == codes[0:1], 1.0, 0.0).astype(bf16)
                    flags[...] = jnp.broadcast_to(codes[1:2], (8, tile))
                    for h in range(heads):
                        target[h, :size] = made[h * size : (h + 1) * size]
                        target[h, size:] = hot

    valids = far_valid[0:1, :] >= 0.0
    attend(head, size, far, kx_ref, vx_ref, tile, valids, qx_ref, full_ref, (att_a, att_b), total_ref, peak_ref)


def near_kernel(size, *refs):
    near_ref, valid_ref, kx_ref, vx_ref, qx_far, full_far, qx_ref, full_ref, att_a, att_b, total_ref, peak_ref = refs
    tile = qx_far.shape[2]
    valids = valid_ref[0:1, :] >= 0.0
    qx_ref[0, :, tile:] = qx_far[0]
    full_ref[:, tile:] = full_far[...]
    attend(
        pl.program_id(0),
        size,
        near_ref,
        kx_ref,
        vx_ref,
        0,
        valids,
        qx_ref.at[:, :, :tile],
        full_ref.at[:, :tile],
        (att_a, att_b),
        total_ref,
        peak_ref,
    )


def attention_outs(heads, size, toks, tiles):
    width, count = heads * size, 2 * toks * tiles
    specs = [
        pl.BlockSpec((1, size + 32, count), lambda h, *_: (h, 0, 0)),
        pl.BlockSpec((size, count), lambda h, *_: (h, 0)),
        pl.BlockSpec((size, toks), lambda h, *_: (h, 0)),
        pl.BlockSpec((size, toks), lambda h, *_: (h, 0)),
    ]
    shapes = [
        jax.ShapeDtypeStruct((heads, size + 32, count), bf16),
        jax.ShapeDtypeStruct((width, count), f32),
        jax.ShapeDtypeStruct((width, toks), bf16),
        jax.ShapeDtypeStruct((width, toks), bf16),
    ]
    scratch = [pltpu.VMEM((size + 16, 2 * toks), f32), pltpu.VMEM((1, 2 * toks), f32)]
    return specs, shapes, scratch


def far_attention(where, blocks, weights):
    count, _, toks = blocks.shape
    parts = count // GROUPS
    width = weights.shape[2]
    heads = HEADS // GROUPS
    size = width // heads
    tile, keys = 2 * toks, count * toks
    specs, shapes, scratch = attention_outs(heads, size, toks, 1)
    shared = [
        jax.ShapeDtypeStruct((heads, size + 32, keys), bf16),
        jax.ShapeDtypeStruct((heads, size + 16, keys), bf16),
        jax.ShapeDtypeStruct((heads, size + 16, tile), bf16),
        jax.ShapeDtypeStruct((8, tile), f32),
        pltpu.HBM((width, keys), bf16),
    ]
    return pl.pallas_call(
        functools.partial(far_kernel, parts, width, heads),
        name="attention_far",
        grid_spec=pltpu.PrefetchScalarGridSpec(
            num_scalar_prefetch=1,
            grid=(heads,),
            in_specs=[whole(blocks.shape), pl.BlockSpec((3, 1, width, width), lambda h, w: (0, w[0], 0, 0))],
            out_specs=specs + [whole(x.shape) for x in shared],
            scratch_shapes=[pltpu.VMEM((heads, size + 16, tile), bf16), pltpu.VMEM((3 * width, width), bf16)]
            + scratch
            + [pltpu.VMEM((8, tile), f32)],
        ),
        out_shape=shapes + shared,
        cost_estimate=CHEAP,
        compiler_params=pltpu.CompilerParams(vmem_limit_bytes=attention_vmem(keys)),
    )(where, blocks, weights)


def near_attention(near, valid, kx, vx, qx, full):
    heads, ext, tile = near.shape
    size = ext - 16
    far_specs, _, _ = attention_outs(heads, size, tile // 2, 1)
    specs, shapes, scratch = attention_outs(heads, size, tile // 2, 2)
    return pl.pallas_call(
        functools.partial(near_kernel, size),
        name="attention_near",
        grid=(heads,),
        in_specs=[whole(x.shape) for x in (near, valid, kx, vx)] + far_specs[:2],
        out_specs=specs,
        scratch_shapes=scratch,
        out_shape=shapes,
        cost_estimate=CHEAP,
        compiler_params=pltpu.CompilerParams(vmem_limit_bytes=attention_vmem(kx.shape[2])),
    )(near, valid, kx, vx, qx, full)


def prepare_kernel(size, *refs):
    grads, full_ref, gx_ref = refs[:GROUPS], refs[GROUPS], refs[GROUPS + 1]
    toks = grads[0].shape[1]
    for head in range(gx_ref.shape[0]):
        rows = slice(head * size, (head + 1) * size)
        for j in range(GROUPS):
            span = slice(j * toks, (j + 1) * toks)
            grad = grads[j][rows, :]
            gx_ref[head, :size, span] = grad
            gx_ref[head, size:, span] = pieces(
                jnp.sum(grad.astype(f32) * full_ref[rows, span], axis=0, keepdims=True)
            )


def prepare(grads, full, size):
    width, count = full.shape
    out = jax.ShapeDtypeStruct((width // size, size + 16, count), bf16)
    return pl.pallas_call(
        functools.partial(prepare_kernel, size),
        name="prepare_backward",
        grid=(1,),
        in_specs=[whole(x.shape) for x in (*grads, full)],
        out_specs=whole(out.shape),
        out_shape=out,
        cost_estimate=CHEAP,
        compiler_params=pltpu.CompilerParams(vmem_limit_bytes=SMALL_VMEM),
    )(*grads, full)


def backward_kernel(size, step, tile, last, qx_ref, gx_ref, kx_ref, vx_ref, *refs):
    if last:
        dq_in, dq_ref, dk_ref, dv_ref = refs
    else:
        dq_ref, dk_ref, dv_ref = refs
    tiles = [slice(i * tile, (i + 1) * tile) for i in range(qx_ref.shape[2] // tile)]
    dq = [None] * len(tiles)
    for first in range(0, kx_ref.shape[2], step):
        kspan = slice(first, first + step)
        dk = dv = None
        for qt, qspan in enumerate(tiles):
            probs = jnp.exp(dot(qx_ref[0, :, qspan], kx_ref[0, :, kspan], TN))
            slopes = dot(gx_ref[0, :, qspan], vx_ref[0, :, kspan], TN)
            probs_low = probs.astype(bf16)
            grad_scores = (probs * slopes).astype(bf16)
            dv_new = dot(gx_ref[0, :size, qspan], probs_low, NN)
            dk_new = dot(qx_ref[0, :size, qspan], grad_scores, NN)
            dq_new = dot(kx_ref[0, :size, kspan], grad_scores, NT)
            dv = dv_new if dv is None else dv + dv_new
            dk = dk_new if dk is None else dk + dk_new
            dq[qt] = dq_new if dq[qt] is None else dq[qt] + dq_new
        dv_ref[:, kspan] = dv.astype(bf16)
        dk_ref[:, kspan] = dk.astype(bf16)
    for qt, qspan in enumerate(tiles):
        if last:
            dq_ref[:, qspan] = ((dq[qt] + dq_in[:, qspan]) * size**-0.5).astype(bf16)
        else:
            dq_ref[:, qspan] = dq[qt]


def backward_attention(head, part, cuts, qx, gx, kx, vx, dq=None):
    size, count = vx.shape[1] - 16, qx.shape[2]
    keys = vx.shape[2] // cuts
    last = dq is not None
    dq_shape, sum_shape = (size, count), (size, keys)
    return pl.pallas_call(
        functools.partial(backward_kernel, size, count // 2, count // 3, last),
        name="attention_backward",
        grid=(1,),
        in_specs=[
            pl.BlockSpec((1, size + 32, count), lambda i: (head, 0, 0)),
            pl.BlockSpec((1, size + 16, count), lambda i: (head, 0, 0)),
            pl.BlockSpec((1, size + 32, keys), lambda i: (head, 0, part)),
            pl.BlockSpec((1, size + 16, keys), lambda i: (head, 0, part)),
        ]
        + [whole(dq_shape)] * last,
        out_specs=[whole(dq_shape), whole(sum_shape), whole(sum_shape)],
        out_shape=[
            jax.ShapeDtypeStruct(dq_shape, bf16 if last else f32),
            jax.ShapeDtypeStruct(sum_shape, bf16),
            jax.ShapeDtypeStruct(sum_shape, bf16),
        ],
        cost_estimate=CHEAP,
        compiler_params=pltpu.CompilerParams(vmem_limit_bytes=attention_vmem(vx.shape[2])),
    )(qx, gx, kx, vx, *([dq] if last else []))


def project_kernel(parts, heads, cuts, where_ref, *refs):
    tok_ref, wq_ref, wk_ref, wv_ref = refs[:4]
    refs = refs[4:]
    dq = jnp.concatenate([ref[...] for ref in refs[:heads]])
    piles, refs = refs[heads : heads + 2 * heads * cuts], refs[heads + 2 * heads * cuts :]
    dk, dv = (
        jnp.concatenate(
            [jnp.concatenate([ref[...] for ref in pile[h * cuts : (h + 1) * cuts]], axis=1) for h in range(heads)]
        )
        for pile in (piles[: heads * cuts], piles[heads * cuts :])
    )
    backs, wgrads, scratch = refs[:parts], refs[parts : 2 * parts], refs[2 * parts]
    width, keys = tok_ref.shape
    count = keys // parts
    toks = count // GROUPS

    scratch[0] = dot(tok_ref[:, :count], dq, NT).astype(bf16)
    scratch[1] = dot(tok_ref[...], dk, NT).astype(bf16)
    scratch[2] = dot(tok_ref[...], dv, NT).astype(bf16)
    for p in reversed(range(parts)):
        span = slice(p * count, (p + 1) * count)
        back = dot(wk_ref[0], dk[:, span], NN) + dot(wv_ref[0], dv[:, span], NN)
        if p == 0:
            back += dot(wq_ref[0], dq, NN)
        for j in range(GROUPS):
            backs[p][j] = back[:, j * toks : (j + 1) * toks].astype(bf16)
    chunk = width // parts
    for p in range(parts):
        rows = pl.ds(pl.multiple_of(jnp.bitwise_xor(where_ref[1], p) * chunk, chunk), chunk)
        wgrads[p][...] = scratch[:, rows, :]


def project_back(where, parts, tok, weights, dqs, dks, dvs):
    width, keys = tok.shape
    toks = keys // parts // GROUPS
    heads, cuts = len(dqs), len(dks) // len(dqs)
    flat = [*dqs, *dks, *dvs]
    weight_spec = pl.BlockSpec((1, width, width), lambda i, w: (w[0], 0, 0))
    outs = [jax.ShapeDtypeStruct((GROUPS, width, toks), bf16)] * parts + [
        jax.ShapeDtypeStruct((3, width // parts, width), bf16)
    ] * parts
    results = pl.pallas_call(
        functools.partial(project_kernel, parts, heads, cuts),
        name="project_back",
        grid_spec=pltpu.PrefetchScalarGridSpec(
            num_scalar_prefetch=1,
            grid=(1,),
            in_specs=[whole(tok.shape)] + [weight_spec] * 3 + [whole(x.shape) for x in flat],
            out_specs=[whole(o.shape) for o in outs],
            scratch_shapes=[pltpu.VMEM((3, width, width), bf16)],
        ),
        out_shape=outs,
        cost_estimate=CHEAP,
        compiler_params=pltpu.CompilerParams(vmem_limit_bytes=attention_vmem(keys)),
    )(where, tok, *weights, *flat)
    return results[:parts], results[parts:]


def norm_parts(values):
    mean = jnp.mean(values, axis=0, keepdims=True)
    center = values - mean
    spread = jnp.mean(center * center, axis=0, keepdims=True)
    scale = lax.rsqrt(spread + 1e-06)
    return center * scale, scale


def norm_back(normal, scale, grad):
    mean = jnp.mean(grad, axis=0, keepdims=True)
    cross = jnp.mean(grad * normal, axis=0, keepdims=True)
    return (grad - mean - normal * cross) * scale


def middle_kernel(where_ref, *refs):
    slot_ref, far_ref, cot_ref, valid_ref, vec_ref, w_ref, fi_ref, fo_ref = refs[:8]
    refs = refs[8:]
    mixed_ref, first_grad_ref = refs[:2]
    sends = refs[2 : 2 + GROUPS]
    att, narrow_ref, wide_ref, first_low_ref, vec_out_ref = refs[2 + GROUPS : 7 + GROUPS]
    first_ref, slope_ref, second_ref, gfirst_ref, grad_att = refs[7 + GROUPS :]
    _, width, toks = slot_ref.shape
    model = width * GROUPS
    own_group = where_ref[0]
    vecs = vec_ref[...].T
    gain_one, bias_one = vecs[:, 0:1], vecs[:, 1:2]
    gain_two, bias_two = vecs[:, 2:3], vecs[:, 3:4]

    for j in range(GROUPS):
        start = pl.multiple_of(jnp.bitwise_xor(own_group, j) * width, width)
        att[pl.ds(start, width), :] = slot_ref[j] if j < 2 else far_ref[j - 2]
    tok = jnp.concatenate([slot_ref[2 + g] for g in range(GROUPS)])
    first_pre = tok.astype(f32) + dot(w_ref[...], att[...], TN)
    normal_one, scale_one = norm_parts(first_pre)
    first_ref[...] = normal_one
    first = normal_one * gain_one + bias_one
    narrow_ref[0] = first.astype(bf16)
    for g in range(GROUPS):
        mine = slice(g * width, (g + 1) * width)
        pre = dot(fi_ref[g], narrow_ref[0, mine, :], TN)
        phi = 0.5 * (1.0 + lax.erf(pre * 0.5**0.5))
        density = jnp.exp(-0.5 * pre * pre) * 0.3989422804014327
        wide_ref[1, g] = (pre * phi).astype(bf16)
        slope_ref[g] = phi + pre * density
        second_ref[mine, :] = (first_ref[mine, :] * gain_one[mine] + bias_one[mine]) + dot(fo_ref[g], wide_ref[1, g], NN)
    normal_two, scale_two = norm_parts(second_ref[...])
    mixed_ref[0] = (normal_two * gain_two + bias_two).T
    cot = cot_ref[0].T
    grad_gain_two = jnp.sum(cot * normal_two, axis=1, keepdims=True)
    grad_bias_two = jnp.sum(cot, axis=1, keepdims=True)
    grad_second = norm_back(normal_two, scale_two, cot * gain_two)
    second_ref[...] = grad_second
    grad_low = grad_second.astype(bf16)
    narrow_ref[1] = grad_low
    for g in range(GROUPS):
        mine = slice(g * width, (g + 1) * width)
        ghp = (dot(fo_ref[g], grad_low[mine, :], TN) * slope_ref[g]).astype(bf16)
        wide_ref[0, g] = ghp
        gfirst_ref[mine, :] = second_ref[mine, :] + dot(fi_ref[g], ghp, NN)
    grad_first = gfirst_ref[...]
    normal_one = first_ref[...]
    grad_gain_one = jnp.sum(grad_first * normal_one, axis=1, keepdims=True)
    grad_bias_one = jnp.sum(grad_first, axis=1, keepdims=True)
    first_grad = norm_back(normal_one, scale_one, grad_first * gain_one)
    first_grad_ref[...] = first_grad
    first_low = first_grad.astype(bf16)
    first_low_ref[...] = first_low
    grad_att[...] = jnp.where(valid_ref[...] == 1, dot(w_ref[...], first_low, NN), 0.0).astype(bf16)
    for j in range(GROUPS):
        start = pl.multiple_of(jnp.bitwise_xor(own_group, j) * width, width)
        sends[j][...] = grad_att[pl.ds(start, width), :]

    lane = lax.broadcasted_iota(jnp.int32, (model, 128), 1)
    vectors = jnp.where(lane == 0, grad_gain_one, 0.0)
    vectors = jnp.where(lane == 1, grad_bias_one, vectors)
    vectors = jnp.where(lane == 2, grad_gain_two, vectors)
    vectors = jnp.where(lane == 3, grad_bias_two, vectors)
    vec_out_ref[...] = vectors.astype(bf16)


def middle(where, slots, far, cotangent, valid, vecs, out_weight, ffn_in, ffn_out_t):
    _, width, toks = slots.shape
    model = width * GROUPS
    wide = ffn_in.shape[2]
    args = (slots, far, cotangent, valid, vecs, out_weight, ffn_in, ffn_out_t)
    outs = (
        [jax.ShapeDtypeStruct((1, toks, model), f32), pltpu.HBM((model, toks), f32)]
        + [jax.ShapeDtypeStruct((width, toks), bf16)] * GROUPS
        + [
            jax.ShapeDtypeStruct((model, toks), bf16),
            jax.ShapeDtypeStruct((2, model, toks), bf16),
            jax.ShapeDtypeStruct((2, GROUPS, wide, toks), bf16),
            jax.ShapeDtypeStruct((model, toks), bf16),
            jax.ShapeDtypeStruct((model, 128), bf16),
        ]
    )
    results = pl.pallas_call(
        middle_kernel,
        name="middle",
        grid_spec=pltpu.PrefetchScalarGridSpec(
            num_scalar_prefetch=1,
            grid=(1,),
            in_specs=[whole(a.shape) for a in args],
            out_specs=[whole(o.shape) for o in outs],
            scratch_shapes=[
                pltpu.VMEM((model, toks), f32),
                pltpu.VMEM((GROUPS, wide, toks), f32),
                pltpu.VMEM((model, toks), f32),
                pltpu.VMEM((model, toks), f32),
                pltpu.VMEM((model, toks), bf16),
            ],
        ),
        out_shape=outs,
        cost_estimate=CHEAP,
        compiler_params=pltpu.CompilerParams(vmem_limit_bytes=VMEM_BYTES),
    )(where, *args)
    return results[0], results[1], results[2 : 2 + GROUPS], results[2 + GROUPS :]


def swapped(slot, odd):
    return jnp.where(odd, slot, (slot % 2) * 2 + slot // 2)


def outer_kernel(parts, slot, where_ref, att, narrow_ref, wide_ref, first_low_ref, vec_ref, near_ref, far_ref):
    model = att.shape[0]
    width = model // GROUPS
    wide = wide_ref.shape[2]
    half = parts // 2
    own_group, part = where_ref[0], jnp.bitwise_xor(where_ref[1], slot)
    ffn_rows, out_rows = width // half, model // (parts * GROUPS)
    array, piece = part // half, part % half
    tiles, wide_tiles = model // 128, wide // 128

    out_start = pl.multiple_of(part * (model // parts), model // parts)
    out = dot(att[pl.ds(out_start, model // parts), :], first_low_ref[...], NT).astype(bf16)
    for target, slots in ((near_ref, (0, 1)), (far_ref, (2, 3))):
        for index, m in enumerate(slots):
            group = jnp.bitwise_xor(own_group, swapped(m, part % 2 == 1))
            start = pl.multiple_of(group * width + piece * ffn_rows, ffn_rows)
            made = dot(narrow_ref[array, pl.ds(start, ffn_rows), :], wide_ref[array, group], NT).astype(bf16)
            for t in range(wide_tiles):
                target[index, t * ffn_rows : (t + 1) * ffn_rows] = made[:, t * 128 : (t + 1) * 128]
    base = wide_tiles * ffn_rows
    for g in range(GROUPS):
        distance = jnp.bitwise_xor(own_group, g)
        m = swapped(distance, part % 2 == 1)
        rows = slice(g * out_rows, (g + 1) * out_rows)
        vec_start = pl.multiple_of(part * (model // parts) + g * out_rows, out_rows)
        vec = vec_ref[pl.ds(vec_start, out_rows), :]

        def put(target, index):
            for t in range(tiles):
                span = slice(base + t * out_rows, base + (t + 1) * out_rows)
                target[index, span] = out[rows, t * 128 : (t + 1) * 128]
            target[index, base + tiles * out_rows : base + (tiles + 1) * out_rows] = vec

        @pl.when(m < 2)
        def _():
            put(near_ref, m)

        @pl.when(m >= 2)
        def _():
            put(far_ref, m - 2)


def outer_products(where, parts, slot, kept):
    att, narrow, wide_pair, _, _ = kept
    model = att.shape[0]
    wide = wide_pair.shape[2]
    rows = (wide // 128) * (model // GROUPS // (parts // 2)) + (model // 128 + 1) * (model // (parts * GROUPS))
    outs = [jax.ShapeDtypeStruct((2, rows, 128), bf16)] * 2
    return pl.pallas_call(
        functools.partial(outer_kernel, parts, slot),
        name="outer_products",
        grid_spec=pltpu.PrefetchScalarGridSpec(
            num_scalar_prefetch=1,
            grid=(1,),
            in_specs=[whole(a.shape) for a in kept],
            out_specs=[whole(o.shape) for o in outs],
        ),
        out_shape=outs,
        cost_estimate=CHEAP,
        compiler_params=pltpu.CompilerParams(vmem_limit_bytes=SMALL_VMEM),
    )(where, *kept)


def row_distances(depth):
    steps = depth.bit_length() - 1
    even = [sum(((m >> (steps - 1 - i)) & 1) << i for i in range(steps)) for m in range(depth)]
    return even, list(range(depth))


def weight_grad_kernel(parts, depth, model, wide, where_ref, *refs):
    slots = refs[:parts]
    out_ref, in_ref, ffn_out_ref, vec_ref, scratch, vec_scratch = refs[parts:]
    step = pl.program_id(0)
    group = jnp.bitwise_xor(step, where_ref[0])
    piece = slots[0].shape[2]
    width = model // GROUPS
    half = parts // 2
    ffn_rows, out_rows = width // half, model // (parts * GROUPS)
    tiles, wide_tiles = model // 128, wide // 128
    even, odd = row_distances(depth)
    for p in range(parts):
        part = jnp.bitwise_xor(where_ref[1], p)
        for z in range(depth):
            distance = jnp.where(part % 2 == 1, odd[z], even[z])
            scratch[part, jnp.bitwise_xor(where_ref[2], distance)] = slots[p][0, z].astype(f32)

    def rows(part, first, count):
        last = first + count
        cuts = [first] + [c for c in range(0, depth * piece, piece) if first < c < last] + [last]
        return jnp.concatenate(
            [scratch[part, x // piece, x % piece : x % piece + y - x, :] for x, y in zip(cuts, cuts[1:])]
        )

    base = wide_tiles * ffn_rows
    for part in range(parts):
        target = in_ref if part < half else ffn_out_ref
        mine = slice((part % half) * ffn_rows, (part % half + 1) * ffn_rows)
        for t in range(wide_tiles):
            target[0, mine, t * 128 : (t + 1) * 128] = rows(part, t * ffn_rows, ffn_rows)
        for t in range(tiles):
            out_ref[part, 0, :, t * 128 : (t + 1) * 128] = rows(part, base + t * out_rows, out_rows)
        start = pl.multiple_of(part * (model // parts) + group * out_rows, out_rows)
        vec_scratch[pl.ds(start, out_rows), :] = rows(part, base + tiles * out_rows, out_rows)

    @pl.when(step == GROUPS - 1)
    def _():
        vec_ref[...] = vec_scratch[...].T[:8]


def weight_grads(where, slots, model, wide):
    parts = len(slots)
    _, depth, piece, _ = slots[0].shape
    width = model // GROUPS
    out_rows = model // (parts * GROUPS)

    def slot_spec(p):
        def place(j, w):
            return (swapped(j, jnp.bitwise_xor(w[1], p) % 2 == 1), 0, 0, 0)

        return pl.BlockSpec((1, depth, piece, 128), place)

    out, ffn_in, ffn_out_t, vectors = pl.pallas_call(
        functools.partial(weight_grad_kernel, parts, depth, model, wide),
        name="weight_grads",
        grid_spec=pltpu.PrefetchScalarGridSpec(
            num_scalar_prefetch=1,
            grid=(GROUPS,),
            in_specs=[slot_spec(p) for p in range(parts)],
            out_specs=[
                pl.BlockSpec((parts, 1, out_rows, model), lambda j, w: (0, jnp.bitwise_xor(j, w[0]), 0, 0)),
                pl.BlockSpec((1, width, wide), lambda j, w: (jnp.bitwise_xor(j, w[0]), 0, 0)),
                pl.BlockSpec((1, width, wide), lambda j, w: (jnp.bitwise_xor(j, w[0]), 0, 0)),
                pl.BlockSpec((8, model), lambda j, w: (0, 0)),
            ],
            scratch_shapes=[pltpu.VMEM((parts, depth, piece, 128), f32), pltpu.VMEM((model, 128), f32)],
        ),
        out_shape=[
            jax.ShapeDtypeStruct((parts, GROUPS, out_rows, model), f32),
            jax.ShapeDtypeStruct((GROUPS, width, wide), f32),
            jax.ShapeDtypeStruct((GROUPS, width, wide), f32),
            jax.ShapeDtypeStruct((8, model), f32),
        ],
        cost_estimate=CHEAP,
        compiler_params=pltpu.CompilerParams(vmem_limit_bytes=SMALL_VMEM),
    )(where, *slots)
    return out.reshape(model, model), ffn_in, ffn_out_t, vectors


def finish_kernel(parts, where_ref, *refs):
    slots, thirds, refs = refs[:GROUPS], refs[GROUPS : GROUPS + parts], refs[GROUPS + parts :]
    first_grad_ref, out_ref, *outs = refs[:-1]
    scratch = refs[-1]
    width = slots[0].shape[0]
    for j in range(GROUPS):
        mine = pl.ds(pl.multiple_of(jnp.bitwise_xor(where_ref[0], j) * width, width), width)
        scratch[mine, :] = first_grad_ref[mine, :] + slots[j][...].astype(f32)
    out_ref[0] = scratch[...].T
    for p in range(parts):
        chunk = thirds[p].shape[2]
        part = jnp.bitwise_xor(where_ref[1], p)
        rows = pl.ds(pl.multiple_of(part * chunk, chunk), chunk)
        for m in range(GROUPS):
            group = jnp.bitwise_xor(where_ref[0], swapped(m, part % 2 == 1))
            for which in range(3):
                outs[which][group, rows, :] = thirds[p][m, which].astype(f32)


def finish(where, slots, thirds, first_grad):
    model, toks = first_grad.shape
    width = model // GROUPS
    args = (*slots, *thirds, first_grad)
    outs = [jax.ShapeDtypeStruct((1, toks, model), f32)] + [
        jax.ShapeDtypeStruct((GROUPS, width, width), f32)
    ] * 3
    return pl.pallas_call(
        functools.partial(finish_kernel, len(thirds)),
        name="finish",
        grid_spec=pltpu.PrefetchScalarGridSpec(
            num_scalar_prefetch=1,
            grid=(1,),
            in_specs=[whole(a.shape) for a in args],
            out_specs=[whole(o.shape) for o in outs],
            scratch_shapes=[pltpu.VMEM((model, toks), f32)],
        ),
        out_shape=outs,
        cost_estimate=CHEAP,
        compiler_params=pltpu.CompilerParams(vmem_limit_bytes=SMALL_VMEM),
    )(where, *args)


def add_low(terms):
    total = terms[0].astype(f32)
    for term in terms[1:]:
        total = total + term.astype(f32)
    return total.astype(bf16)


def shards(
    tokens,
    segment_ids,
    valid_tokens,
    q_weight,
    k_weight,
    v_weight,
    out_weight,
    gain_one,
    bias_one,
    ffn_in,
    ffn_out,
    gain_two,
    bias_two,
    cotangent,
):
    seq = lax.axis_size("seq")
    depth = lax.axis_size("rows")
    parts = seq // GROUPS
    _, toks, model = tokens.shape
    width = model // GROUPS
    wide = ffn_in.shape[2]
    place = lax.axis_index("seq")
    own_group, own_part = place // parts, place % parts
    own_row = lax.axis_index("rows")
    where = jnp.stack([own_group, own_part, own_row]).astype(jnp.int32)

    def swap(value, distance):
        return lax.ppermute(value, "seq", [(k, k ^ distance) for k in range(seq)])

    def across(value):
        return [value[0]] + [swap(value[j], parts * j) for j in range(1, GROUPS)]

    def group_swap(value, step):
        apart = [(1, 2), (2, 1)][step]
        return lax.ppermute(value, "seq", [(k, k ^ parts * apart[k % parts % 2]) for k in range(seq)])

    row_steps = depth.bit_length() - 1

    def row_swap(value, step):
        pairs = []
        for k in range(seq):
            distance = 1 << (row_steps - 1 - step if k % parts % 2 else step)
            pairs += [(k * depth + z, k * depth + (z ^ distance)) for z in range(depth)]
        return lax.ppermute(value, ("seq", "rows"), pairs)

    grouped, sends = arrange(where, tokens, segment_ids, valid_tokens)
    mine = across(sends)
    others = [swap(jnp.stack(mine), p) for p in range(1, parts)]
    blocks = jnp.stack(mine + [x[j] for x in others for j in range(GROUPS)])

    qx_far, full_far, att_c, att_d, kx, vx, near, near_valid, tok = far_attention(
        where, blocks, jnp.stack([q_weight, k_weight, v_weight])
    )
    att_far = jnp.stack([swap(att_c, parts * 2), swap(att_d, parts * 3)])
    qx, full, att_a, att_b = near_attention(near, near_valid, kx, vx, qx_far, full_far)
    att_b = swap(att_b, parts)
    slots = jnp.concatenate([att_a[None], att_b[None], grouped])
    vecs = jnp.pad(jnp.stack(after([gain_one, bias_one, gain_two, bias_two], att_a)), ((0, 4), (0, 0)))
    mixed, first_grad, sends, kept = middle(
        where, slots, att_far, cotangent, valid_tokens, vecs, out_weight, ffn_in, jnp.swapaxes(ffn_out, 1, 2)
    )
    grads = across(sends)

    pays = [outer_products(where, parts, p, kept) for p in range(1, parts)]
    moved = [[swap(x, p) for x in pays[p - 1]] for p in range(1, parts)]
    pay = outer_products(where, parts, 0, after(kept, pays))
    gx = prepare(after(grads, pay), full, model // HEADS)
    moved = after(moved, gx)
    low = add_low([pay[0]] + [x[0] for x in moved])
    high = add_low([pay[1]] + [x[1] for x in moved])

    heads, cuts = HEADS // GROUPS, 2
    calls = [(head, part) for head in range(heads) for part in range(cuts)]
    dqs, dks, dvs = [], [], []

    def work(*ready):
        head, part = calls.pop(0)
        dq, dk, dv = backward_attention(
            head,
            part,
            cuts,
            qx,
            after(gx, ready),
            kx,
            vx,
            dqs.pop() if part else None,
        )
        dqs.append(dq)
        dks.append(dk)
        dvs.append(dv)
        return dq

    moved = group_swap(high, 0)
    first = work(high, low)
    moved = after(moved, work(first))
    low, high = add_low([low[0], moved[0]]), add_low([low[1], moved[1]])
    moved = group_swap(high, 1)
    piece = add_low([low, after(moved, work(high, low))]).reshape(depth, -1, 128)
    even, odd = row_distances(depth)
    picks = [own_row ^ jnp.where(own_part % 2 == 1, odd[m], even[m]) for m in range(depth)]
    piece = jnp.stack([lax.dynamic_index_in_dim(piece, z, 0, False) for z in picks])
    for step in range(row_steps):
        count = piece.shape[0] // 2
        low, high = piece[:count], piece[count:]
        moved = row_swap(high, step)
        if len(calls) > 1:
            moved = after(moved, work(high, low))
        piece = add_low([low, moved])
    moved = row_swap(piece, row_steps - 1)
    while calls:
        done = work(piece)
        moved, dqs[-1] = after((moved, dqs[-1]), done)
    piece = jnp.concatenate([piece, moved])
    step = row_steps - 2
    moved = row_swap(piece, step)
    backs, wgrads = project_back(where, parts, tok, (q_weight, k_weight, v_weight), after(dqs, piece), dks, dvs)
    piece = jnp.concatenate([piece, moved])
    for step in reversed(range(row_steps - 2)):
        piece = jnp.concatenate([piece, row_swap(piece, step)])
    wgrads, backs, piece = after((wgrads, backs, piece[None]), piece)
    swaps = [[swap(x[p], p) for p in range(1, parts)] for x in (wgrads, backs)]
    moved = group_swap(piece, 1)
    quarter, back_sum = add_low([wgrads[0]] + swaps[0]), add_low([backs[0]] + swaps[1])
    back_first = swap(back_sum[1], parts)
    for step in range(row_steps - 1):
        quarter = add_low([quarter, row_swap(quarter, step)])
    piece = jnp.concatenate([piece, moved])
    quarter, back_sum, back_first, piece = after((quarter, back_sum, back_first, piece), quarter)
    moved = group_swap(piece, 0)
    quarter = add_low([quarter, row_swap(quarter, row_steps - 1)])
    quarter = jnp.stack([quarter, group_swap(quarter, 1)])
    piece = jnp.concatenate([piece, moved])
    quarter, back_sum, piece = after((quarter, back_sum, piece), quarter)
    slots = [piece] + [swap(piece, p) for p in range(1, parts)]
    back_moved = [back_sum[0], back_first] + [swap(back_sum[j], parts * j) for j in (2, 3)]
    moved = group_swap(quarter, 0)
    grad_out_weight, grad_ffn_in, grad_ffn_out_t, vectors = weight_grads(where, slots, model, wide)
    moved, back_moved = after((moved, back_moved), vectors)
    quarter = jnp.concatenate([quarter, moved])
    thirds = [quarter] + [swap(quarter, p) for p in range(1, parts)]
    grad_tokens, grad_q, grad_k, grad_v = finish(where, back_moved, thirds, first_grad)

    return (
        mixed,
        grad_tokens,
        grad_q,
        grad_k,
        grad_v,
        grad_out_weight,
        vectors[0],
        vectors[1],
        grad_ffn_in,
        jnp.swapaxes(grad_ffn_out_t, 1, 2),
        vectors[2],
        vectors[3],
    )


def solution(mesh):
    tokens = P("rows", "seq", None)
    flags = P("rows", "seq")
    in_specs = (tokens, flags, flags) + (P(),) * 10 + (tokens,)
    out_specs = (tokens, tokens) + (P(),) * 10
    return jax.shard_map(shards, mesh=mesh, in_specs=in_specs, out_specs=out_specs, check_vma=False)
```

```python
import functools

import jax
import jax.numpy as jnp
from jax import lax
from jax.experimental import pallas as pl
from jax.experimental.pallas import tpu as pltpu
from jax.sharding import PartitionSpec as P

HEADS = 12
GROUPS = 4
PENALTY = 2.0**30
VMEM_BYTES = 36 * 2**20
SMALL_VMEM = 20 * 2**20
ATT_BASE = 9
bf16 = jnp.bfloat16
f32 = jnp.float32


def dot(a, b, dims):
    return lax.dot_general(a, b, (dims, ((), ())), preferred_element_type=f32)


NN = ((1,), (0,))
TN = ((0,), (0,))
NT = ((1,), (1,))


def whole(shape):
    return pl.BlockSpec(shape, lambda *_: (0,) * len(shape), pipeline_mode=pl.Buffered(1))


def pieces(row):
    high = row.astype(bf16)
    rest = row - high.astype(f32)
    middle = rest.astype(bf16)
    low = (rest - middle.astype(f32)).astype(bf16)
    count = row.shape[-1]
    index = lax.broadcasted_iota(jnp.int32, (16, count), 0)
    out = jnp.where(index == 0, high.astype(f32), 0.0)
    out = jnp.where(index == 1, middle.astype(f32), out)
    out = jnp.where(index == 2, low.astype(f32), out)
    return out.astype(bf16)


def minus_rows(count):
    index = lax.broadcasted_iota(jnp.int32, (16, count), 0)
    return jnp.where(index < 3, -1.0, 0.0).astype(bf16)


def attention_vmem(keys):
    return 2**20 * (ATT_BASE + 2 * keys // 1024)


def after(value, *others):
    return lax.optimization_barrier((value, others))[0]


CHEAP = pl.CostEstimate(flops=1, bytes_accessed=1, transcendentals=0)


def arrange_kernel(where_ref, tok_ref, code_ref, grouped_ref, *sends):
    _, width, _ = grouped_ref.shape
    flipped = tok_ref[0].astype(f32).T.astype(bf16)
    for g in range(GROUPS):
        grouped_ref[g] = flipped[g * width : (g + 1) * width]
    for j, send in enumerate(sends):
        send[:width] = grouped_ref[jnp.bitwise_xor(where_ref[0], j)]
        send[width:] = code_ref[...]


def arrange(where, tokens, segment_ids, valid_tokens):
    _, toks, model = tokens.shape
    width = model // GROUPS
    index = lax.broadcasted_iota(jnp.int32, (16, toks), 0)
    codes = jnp.where(index == 0, segment_ids, jnp.where(valid_tokens == 1, segment_ids, -1))
    args = (tokens, codes.astype(bf16))
    outs = [jax.ShapeDtypeStruct((GROUPS, width, toks), bf16)] + [
        jax.ShapeDtypeStruct((width + 16, toks), bf16)
    ] * GROUPS
    grouped, *sends = pl.pallas_call(
        arrange_kernel,
        name="arrange",
        grid_spec=pltpu.PrefetchScalarGridSpec(
            num_scalar_prefetch=1,
            grid=(1,),
            in_specs=[whole(a.shape) for a in args],
            out_specs=[whole(o.shape) for o in outs],
        ),
        out_shape=outs,
        cost_estimate=CHEAP,
        compiler_params=pltpu.CompilerParams(vmem_limit_bytes=SMALL_VMEM),
    )(where, *args)
    return grouped, sends


def attend(head, size, qs, kx_ref, vx_ref, own, valids, qx_ref, full_ref, atts, total_ref, peak_ref):
    toks = atts[0].shape[1]
    tile, keys = 2 * toks, kx_ref.shape[2]
    ext = size + 16

    own_keys = kx_ref[head, :size, own : own + tile]
    self_score = jnp.sum(qs[head, :size].astype(f32) * own_keys.astype(f32), axis=0, keepdims=True)
    qx_ref[0, :ext] = qs[head]
    qx_ref[0, ext:] = pieces(self_score)

    step = 256

    def scores(first):
        return dot(kx_ref[head, :, first : first + step], qx_ref[0], TN)

    total = None
    upcoming = [scores(0), scores(step)]
    for first in range(0, keys, step):
        now = upcoming.pop(0)
        if first + 2 * step < keys:
            upcoming.append(scores(first + 2 * step))
        mixed = dot(vx_ref[head, :, first : first + step], jnp.exp(now).astype(bf16), NN)
        total = mixed if total is None else total + mixed
    total_ref[...] = total
    peak_ref[...] = self_score
    in_range = jnp.max(-total[size : size + 1]) < 2.0**100

    @pl.when(jnp.logical_not(in_range))
    def _():
        total_ref[...] = jnp.zeros_like(total_ref)
        peak_ref[...] = jnp.full_like(peak_ref, -4.0 * PENALTY)

        def again(index, carry):
            span = pl.ds(pl.multiple_of(index * step, step), step)
            now = dot(kx_ref[head, :ext, span], qs[head, :ext], TN)
            peak = jnp.maximum(peak_ref[...], jnp.max(now, axis=0, keepdims=True))
            mixed = dot(vx_ref[head, :, span], jnp.exp(now - peak).astype(bf16), NN)
            total_ref[...] = total_ref[...] * jnp.exp(peak_ref[...] - peak) + mixed
            peak_ref[...] = peak
            return carry

        lax.fori_loop(0, keys // step, again, 0)

    row_sum = -total_ref[size : size + 1]
    log_total = peak_ref[...] + jnp.log(row_sum)
    attended = jnp.where(valids, total_ref[:size] / row_sum, 0.0)
    full_ref[...] = attended
    for half in range(2):
        atts[half][...] = attended[:, half * toks : (half + 1) * toks].astype(bf16)
    qx_ref[0, ext:] = pieces(jnp.where(valids, log_total, PENALTY))


def far_kernel(parts, width, heads, where_ref, *refs):
    blocks, w_ref, qx_ref, full_ref, att_a, att_b, kx_ref, vx_ref, near_ref, valid_ref, tok_ref = refs[:11]
    far, wt, total_ref, peak_ref, far_valid = refs[11:]
    head = pl.program_id(0)
    size = width // heads
    toks = blocks.shape[2]
    tile, ext = 2 * toks, size + 16

    @pl.when(head == 0)
    def _():
        code_index = lax.broadcasted_iota(jnp.int32, (16, tile), 0).astype(f32)
        for which in range(3):
            scale = size**-0.5 if which == 0 else 1.0
            wt[which * width : (which + 1) * width, :] = (w_ref[which, 0].astype(f32) * scale).T.astype(bf16)
        for p in range(parts):
            for j in range(0, GROUPS, 2):
                b = p * GROUPS + j
                span = slice(b * toks, (b + 2) * toks)
                both = jnp.concatenate([blocks[b], blocks[b + 1]], axis=1)
                tok_ref[:, span] = both[:width]
                first = 0 if p == 0 else width
                made = dot(wt[first:], both[:width], NN).astype(bf16)
                codes = both[width:].astype(f32)
                mask = jnp.where(code_index == codes[1:2], 0.0, -PENALTY).astype(bf16)
                for h in range(heads):
                    keys = width - first + h * size
                    kx_ref[h, :size, span] = made[keys : keys + size]
                    kx_ref[h, size:ext, span] = mask
                    kx_ref[h, ext:, span] = minus_rows(tile)
                    vx_ref[h, :size, span] = made[keys + width : keys + width + size]
                    vx_ref[h, size:, span] = minus_rows(tile)
                if p == 0:
                    target, flags = (near_ref, valid_ref) if j == 0 else (far, far_valid)
                    hot = jnp.where(code_index == codes[0:1], 1.0, 0.0).astype(bf16)
                    flags[...] = jnp.broadcast_to(codes[1:2], (8, tile))
                    for h in range(heads):
                        target[h, :size] = made[h * size : (h + 1) * size]
                        target[h, size:] = hot

    valids = far_valid[0:1, :] >= 0.0
    attend(head, size, far, kx_ref, vx_ref, tile, valids, qx_ref, full_ref, (att_a, att_b), total_ref, peak_ref)


def near_kernel(size, *refs):
    near_ref, valid_ref, kx_ref, vx_ref, qx_far, full_far, qx_ref, full_ref, att_a, att_b, total_ref, peak_ref = refs
    tile = qx_far.shape[2]
    valids = valid_ref[0:1, :] >= 0.0
    qx_ref[0, :, tile:] = qx_far[0]
    full_ref[:, tile:] = full_far[...]
    attend(
        pl.program_id(0),
        size,
        near_ref,
        kx_ref,
        vx_ref,
        0,
        valids,
        qx_ref.at[:, :, :tile],
        full_ref.at[:, :tile],
        (att_a, att_b),
        total_ref,
        peak_ref,
    )


def attention_outs(heads, size, toks, tiles):
    width, count = heads * size, 2 * toks * tiles
    specs = [
        pl.BlockSpec((1, size + 32, count), lambda h, *_: (h, 0, 0)),
        pl.BlockSpec((size, count), lambda h, *_: (h, 0)),
        pl.BlockSpec((size, toks), lambda h, *_: (h, 0)),
        pl.BlockSpec((size, toks), lambda h, *_: (h, 0)),
    ]
    shapes = [
        jax.ShapeDtypeStruct((heads, size + 32, count), bf16),
        jax.ShapeDtypeStruct((width, count), f32),
        jax.ShapeDtypeStruct((width, toks), bf16),
        jax.ShapeDtypeStruct((width, toks), bf16),
    ]
    scratch = [pltpu.VMEM((size + 16, 2 * toks), f32), pltpu.VMEM((1, 2 * toks), f32)]
    return specs, shapes, scratch


def far_attention(where, blocks, weights):
    count, _, toks = blocks.shape
    parts = count // GROUPS
    width = weights.shape[2]
    heads = HEADS // GROUPS
    size = width // heads
    tile, keys = 2 * toks, count * toks
    specs, shapes, scratch = attention_outs(heads, size, toks, 1)
    shared = [
        jax.ShapeDtypeStruct((heads, size + 32, keys), bf16),
        jax.ShapeDtypeStruct((heads, size + 16, keys), bf16),
        jax.ShapeDtypeStruct((heads, size + 16, tile), bf16),
        jax.ShapeDtypeStruct((8, tile), f32),
        pltpu.HBM((width, keys), bf16),
    ]
    return pl.pallas_call(
        functools.partial(far_kernel, parts, width, heads),
        name="attention_far",
        grid_spec=pltpu.PrefetchScalarGridSpec(
            num_scalar_prefetch=1,
            grid=(heads,),
            in_specs=[whole(blocks.shape), pl.BlockSpec((3, 1, width, width), lambda h, w: (0, w[0], 0, 0))],
            out_specs=specs + [whole(x.shape) for x in shared],
            scratch_shapes=[pltpu.VMEM((heads, size + 16, tile), bf16), pltpu.VMEM((3 * width, width), bf16)]
            + scratch
            + [pltpu.VMEM((8, tile), f32)],
        ),
        out_shape=shapes + shared,
        cost_estimate=CHEAP,
        compiler_params=pltpu.CompilerParams(vmem_limit_bytes=attention_vmem(keys)),
    )(where, blocks, weights)


def near_attention(near, valid, kx, vx, qx, full):
    heads, ext, tile = near.shape
    size = ext - 16
    far_specs, _, _ = attention_outs(heads, size, tile // 2, 1)
    specs, shapes, scratch = attention_outs(heads, size, tile // 2, 2)
    return pl.pallas_call(
        functools.partial(near_kernel, size),
        name="attention_near",
        grid=(heads,),
        in_specs=[whole(x.shape) for x in (near, valid, kx, vx)] + far_specs[:2],
        out_specs=specs,
        scratch_shapes=scratch,
        out_shape=shapes,
        cost_estimate=CHEAP,
        compiler_params=pltpu.CompilerParams(vmem_limit_bytes=attention_vmem(kx.shape[2])),
    )(near, valid, kx, vx, qx, full)


def prepare_kernel(size, *refs):
    grads, full_ref, gx_ref = refs[:GROUPS], refs[GROUPS], refs[GROUPS + 1]
    toks = grads[0].shape[1]
    for head in range(gx_ref.shape[0]):
        rows = slice(head * size, (head + 1) * size)
        for j in range(GROUPS):
            span = slice(j * toks, (j + 1) * toks)
            grad = grads[j][rows, :]
            gx_ref[head, :size, span] = grad
            gx_ref[head, size:, span] = pieces(
                jnp.sum(grad.astype(f32) * full_ref[rows, span], axis=0, keepdims=True)
            )


def prepare(grads, full, size):
    width, count = full.shape
    out = jax.ShapeDtypeStruct((width // size, size + 16, count), bf16)
    return pl.pallas_call(
        functools.partial(prepare_kernel, size),
        name="prepare_backward",
        grid=(1,),
        in_specs=[whole(x.shape) for x in (*grads, full)],
        out_specs=whole(out.shape),
        out_shape=out,
        cost_estimate=CHEAP,
        compiler_params=pltpu.CompilerParams(vmem_limit_bytes=SMALL_VMEM),
    )(*grads, full)


def backward_kernel(size, step, tile, last, qx_ref, gx_ref, kx_ref, vx_ref, *refs):
    if last:
        dq_in, dq_ref, dk_ref, dv_ref, total = refs
        total[...] = dq_in[...]
    else:
        dq_ref, dk_ref, dv_ref = refs
        total = dq_ref
        total[...] = jnp.zeros_like(total)

    def keys(index, carry):
        kspan = pl.ds(pl.multiple_of(index * step, step), step)
        dk = dv = None
        for first in range(0, qx_ref.shape[2], tile):
            qspan = slice(first, first + tile)
            probs = jnp.exp(dot(qx_ref[0, :, qspan], kx_ref[0, :, kspan], TN))
            slopes = dot(gx_ref[0, :, qspan], vx_ref[0, :, kspan], TN)
            probs_low = probs.astype(bf16)
            grad_scores = (probs * slopes).astype(bf16)
            dv_new = dot(gx_ref[0, :size, qspan], probs_low, NN)
            dk_new = dot(qx_ref[0, :size, qspan], grad_scores, NN)
            total[:, qspan] += dot(kx_ref[0, :size, kspan], grad_scores, NT)
            dv = dv_new if dv is None else dv + dv_new
            dk = dk_new if dk is None else dk + dk_new
        dv_ref[:, kspan] = dv.astype(bf16)
        dk_ref[:, kspan] = dk.astype(bf16)
        return carry

    lax.fori_loop(0, kx_ref.shape[2] // step, keys, 0)
    if last:
        dq_ref[...] = (total[...] * size**-0.5).astype(bf16)


def backward_attention(head, part, cuts, qx, gx, kx, vx, dq=None):
    size, count = vx.shape[1] - 16, qx.shape[2]
    keys = vx.shape[2] // cuts
    last = dq is not None
    dq_shape, sum_shape = (size, count), (size, keys)
    return pl.pallas_call(
        functools.partial(backward_kernel, size, count // 2, count // 3, last),
        name="attention_backward",
        grid=(1,),
        in_specs=[
            pl.BlockSpec((1, size + 32, count), lambda i: (head, 0, 0)),
            pl.BlockSpec((1, size + 16, count), lambda i: (head, 0, 0)),
            pl.BlockSpec((1, size + 32, keys), lambda i: (head, 0, part)),
            pl.BlockSpec((1, size + 16, keys), lambda i: (head, 0, part)),
        ]
        + [whole(dq_shape)] * last,
        out_specs=[whole(dq_shape), whole(sum_shape), whole(sum_shape)],
        scratch_shapes=[pltpu.VMEM(dq_shape, f32)] * last,
        out_shape=[
            jax.ShapeDtypeStruct(dq_shape, bf16 if last else f32),
            jax.ShapeDtypeStruct(sum_shape, bf16),
            jax.ShapeDtypeStruct(sum_shape, bf16),
        ],
        cost_estimate=CHEAP,
        compiler_params=pltpu.CompilerParams(vmem_limit_bytes=attention_vmem(vx.shape[2])),
    )(qx, gx, kx, vx, *([dq] if last else []))


def project_kernel(parts, heads, cuts, where_ref, *refs):
    tok_ref, wq_ref, wk_ref, wv_ref = refs[:4]
    refs = refs[4:]
    dq = jnp.concatenate([ref[...] for ref in refs[:heads]])
    piles, refs = refs[heads : heads + 2 * heads * cuts], refs[heads + 2 * heads * cuts :]
    dk, dv = (
        jnp.concatenate(
            [jnp.concatenate([ref[...] for ref in pile[h * cuts : (h + 1) * cuts]], axis=1) for h in range(heads)]
        )
        for pile in (piles[: heads * cuts], piles[heads * cuts :])
    )
    backs, wgrads, scratch = refs[:parts], refs[parts : 2 * parts], refs[2 * parts]
    width, keys = tok_ref.shape
    count = keys // parts
    toks = count // GROUPS

    scratch[0] = dot(tok_ref[:, :count], dq, NT).astype(bf16)
    scratch[1] = dot(tok_ref[...], dk, NT).astype(bf16)
    scratch[2] = dot(tok_ref[...], dv, NT).astype(bf16)
    for p in reversed(range(parts)):
        span = slice(p * count, (p + 1) * count)
        back = dot(wk_ref[0], dk[:, span], NN) + dot(wv_ref[0], dv[:, span], NN)
        if p == 0:
            back += dot(wq_ref[0], dq, NN)
        for j in range(GROUPS):
            backs[p][j] = back[:, j * toks : (j + 1) * toks].astype(bf16)
    chunk = width // parts
    for p in range(parts):
        rows = pl.ds(pl.multiple_of(jnp.bitwise_xor(where_ref[1], p) * chunk, chunk), chunk)
        wgrads[p][...] = scratch[:, rows, :]


def project_back(where, parts, tok, weights, dqs, dks, dvs):
    width, keys = tok.shape
    toks = keys // parts // GROUPS
    heads, cuts = len(dqs), len(dks) // len(dqs)
    flat = [*dqs, *dks, *dvs]
    weight_spec = pl.BlockSpec((1, width, width), lambda i, w: (w[0], 0, 0))
    outs = [jax.ShapeDtypeStruct((GROUPS, width, toks), bf16)] * parts + [
        jax.ShapeDtypeStruct((3, width // parts, width), bf16)
    ] * parts
    results = pl.pallas_call(
        functools.partial(project_kernel, parts, heads, cuts),
        name="project_back",
        grid_spec=pltpu.PrefetchScalarGridSpec(
            num_scalar_prefetch=1,
            grid=(1,),
            in_specs=[whole(tok.shape)] + [weight_spec] * 3 + [whole(x.shape) for x in flat],
            out_specs=[whole(o.shape) for o in outs],
            scratch_shapes=[pltpu.VMEM((3, width, width), bf16)],
        ),
        out_shape=outs,
        cost_estimate=CHEAP,
        compiler_params=pltpu.CompilerParams(vmem_limit_bytes=attention_vmem(keys)),
    )(where, tok, *weights, *flat)
    return results[:parts], results[parts:]


def norm_parts(values):
    mean = jnp.mean(values, axis=0, keepdims=True)
    center = values - mean
    spread = jnp.mean(center * center, axis=0, keepdims=True)
    scale = lax.rsqrt(spread + 1e-06)
    return center * scale, scale


def norm_back(normal, scale, grad):
    mean = jnp.mean(grad, axis=0, keepdims=True)
    cross = jnp.mean(grad * normal, axis=0, keepdims=True)
    return (grad - mean - normal * cross) * scale


def middle_kernel(where_ref, *refs):
    slot_ref, far_ref, cot_ref, valid_ref, vec_ref, w_ref, fi_ref, fo_ref = refs[:8]
    refs = refs[8:]
    mixed_ref, first_grad_ref = refs[:2]
    sends = refs[2 : 2 + GROUPS]
    att, narrow_ref, wide_ref, first_low_ref, vec_out_ref = refs[2 + GROUPS : 7 + GROUPS]
    first_ref, slope_ref, second_ref, gfirst_ref, grad_att = refs[7 + GROUPS :]
    _, width, toks = slot_ref.shape
    model = width * GROUPS
    own_group = where_ref[0]
    vecs = vec_ref[...].T
    gain_one, bias_one = vecs[:, 0:1], vecs[:, 1:2]
    gain_two, bias_two = vecs[:, 2:3], vecs[:, 3:4]

    for j in range(GROUPS):
        start = pl.multiple_of(jnp.bitwise_xor(own_group, j) * width, width)
        att[pl.ds(start, width), :] = slot_ref[j] if j < 2 else far_ref[j - 2]
    tok = jnp.concatenate([slot_ref[2 + g] for g in range(GROUPS)])
    first_pre = tok.astype(f32) + dot(w_ref[...], att[...], TN)
    normal_one, scale_one = norm_parts(first_pre)
    first_ref[...] = normal_one
    first = normal_one * gain_one + bias_one
    narrow_ref[0] = first.astype(bf16)
    for g in range(GROUPS):
        mine = slice(g * width, (g + 1) * width)
        pre = dot(fi_ref[g], narrow_ref[0, mine, :], TN)
        phi = 0.5 * (1.0 + lax.erf(pre * 0.5**0.5))
        density = jnp.exp(-0.5 * pre * pre) * 0.3989422804014327
        wide_ref[1, g] = (pre * phi).astype(bf16)
        slope_ref[g] = phi + pre * density
        second_ref[mine, :] = (first_ref[mine, :] * gain_one[mine] + bias_one[mine]) + dot(fo_ref[g], wide_ref[1, g], NN)
    normal_two, scale_two = norm_parts(second_ref[...])
    mixed_ref[0] = (normal_two * gain_two + bias_two).T
    cot = cot_ref[0].T
    grad_gain_two = jnp.sum(cot * normal_two, axis=1, keepdims=True)
    grad_bias_two = jnp.sum(cot, axis=1, keepdims=True)
    grad_second = norm_back(normal_two, scale_two, cot * gain_two)
    second_ref[...] = grad_second
    grad_low = grad_second.astype(bf16)
    narrow_ref[1] = grad_low
    for g in range(GROUPS):
        mine = slice(g * width, (g + 1) * width)
        ghp = (dot(fo_ref[g], grad_low[mine, :], TN) * slope_ref[g]).astype(bf16)
        wide_ref[0, g] = ghp
        gfirst_ref[mine, :] = second_ref[mine, :] + dot(fi_ref[g], ghp, NN)
    grad_first = gfirst_ref[...]
    normal_one = first_ref[...]
    grad_gain_one = jnp.sum(grad_first * normal_one, axis=1, keepdims=True)
    grad_bias_one = jnp.sum(grad_first, axis=1, keepdims=True)
    first_grad = norm_back(normal_one, scale_one, grad_first * gain_one)
    first_grad_ref[...] = first_grad
    first_low = first_grad.astype(bf16)
    first_low_ref[...] = first_low
    grad_att[...] = jnp.where(valid_ref[...] == 1, dot(w_ref[...], first_low, NN), 0.0).astype(bf16)
    for j in range(GROUPS):
        start = pl.multiple_of(jnp.bitwise_xor(own_group, j) * width, width)
        sends[j][...] = grad_att[pl.ds(start, width), :]

    lane = lax.broadcasted_iota(jnp.int32, (model, 128), 1)
    vectors = jnp.where(lane == 0, grad_gain_one, 0.0)
    vectors = jnp.where(lane == 1, grad_bias_one, vectors)
    vectors = jnp.where(lane == 2, grad_gain_two, vectors)
    vectors = jnp.where(lane == 3, grad_bias_two, vectors)
    vec_out_ref[...] = vectors.astype(bf16)


def middle(where, slots, far, cotangent, valid, vecs, out_weight, ffn_in, ffn_out_t):
    _, width, toks = slots.shape
    model = width * GROUPS
    wide = ffn_in.shape[2]
    args = (slots, far, cotangent, valid, vecs, out_weight, ffn_in, ffn_out_t)
    outs = (
        [jax.ShapeDtypeStruct((1, toks, model), f32), pltpu.HBM((model, toks), f32)]
        + [jax.ShapeDtypeStruct((width, toks), bf16)] * GROUPS
        + [
            jax.ShapeDtypeStruct((model, toks), bf16),
            jax.ShapeDtypeStruct((2, model, toks), bf16),
            jax.ShapeDtypeStruct((2, GROUPS, wide, toks), bf16),
            jax.ShapeDtypeStruct((model, toks), bf16),
            jax.ShapeDtypeStruct((model, 128), bf16),
        ]
    )
    results = pl.pallas_call(
        middle_kernel,
        name="middle",
        grid_spec=pltpu.PrefetchScalarGridSpec(
            num_scalar_prefetch=1,
            grid=(1,),
            in_specs=[whole(a.shape) for a in args],
            out_specs=[whole(o.shape) for o in outs],
            scratch_shapes=[
                pltpu.VMEM((model, toks), f32),
                pltpu.VMEM((GROUPS, wide, toks), f32),
                pltpu.VMEM((model, toks), f32),
                pltpu.VMEM((model, toks), f32),
                pltpu.VMEM((model, toks), bf16),
            ],
        ),
        out_shape=outs,
        cost_estimate=CHEAP,
        compiler_params=pltpu.CompilerParams(vmem_limit_bytes=VMEM_BYTES),
    )(where, *args)
    return results[0], results[1], results[2 : 2 + GROUPS], results[2 + GROUPS :]


def swapped(slot, odd):
    return jnp.where(odd, slot, (slot % 2) * 2 + slot // 2)


def outer_kernel(parts, slot, where_ref, att, narrow_ref, wide_ref, first_low_ref, vec_ref, near_ref, far_ref):
    model = att.shape[0]
    width = model // GROUPS
    wide = wide_ref.shape[2]
    half = parts // 2
    own_group, part = where_ref[0], jnp.bitwise_xor(where_ref[1], slot)
    ffn_rows, out_rows = width // half, model // (parts * GROUPS)
    array, piece = part // half, part % half
    tiles, wide_tiles = model // 128, wide // 128

    out_start = pl.multiple_of(part * (model // parts), model // parts)
    out = dot(att[pl.ds(out_start, model // parts), :], first_low_ref[...], NT).astype(bf16)
    for target, slots in ((near_ref, (0, 1)), (far_ref, (2, 3))):
        for index, m in enumerate(slots):
            group = jnp.bitwise_xor(own_group, swapped(m, part % 2 == 1))
            start = pl.multiple_of(group * width + piece * ffn_rows, ffn_rows)
            made = dot(narrow_ref[array, pl.ds(start, ffn_rows), :], wide_ref[array, group], NT).astype(bf16)
            for t in range(wide_tiles):
                target[index, t * ffn_rows : (t + 1) * ffn_rows] = made[:, t * 128 : (t + 1) * 128]
    base = wide_tiles * ffn_rows
    for g in range(GROUPS):
        distance = jnp.bitwise_xor(own_group, g)
        m = swapped(distance, part % 2 == 1)
        rows = slice(g * out_rows, (g + 1) * out_rows)
        vec_start = pl.multiple_of(part * (model // parts) + g * out_rows, out_rows)
        vec = vec_ref[pl.ds(vec_start, out_rows), :]

        def put(target, index):
            for t in range(tiles):
                span = slice(base + t * out_rows, base + (t + 1) * out_rows)
                target[index, span] = out[rows, t * 128 : (t + 1) * 128]
            target[index, base + tiles * out_rows : base + (tiles + 1) * out_rows] = vec

        @pl.when(m < 2)
        def _():
            put(near_ref, m)

        @pl.when(m >= 2)
        def _():
            put(far_ref, m - 2)


def outer_products(where, parts, slot, kept):
    att, narrow, wide_pair, _, _ = kept
    model = att.shape[0]
    wide = wide_pair.shape[2]
    rows = (wide // 128) * (model // GROUPS // (parts // 2)) + (model // 128 + 1) * (model // (parts * GROUPS))
    outs = [jax.ShapeDtypeStruct((2, rows, 128), bf16)] * 2
    return pl.pallas_call(
        functools.partial(outer_kernel, parts, slot),
        name="outer_products",
        grid_spec=pltpu.PrefetchScalarGridSpec(
            num_scalar_prefetch=1,
            grid=(1,),
            in_specs=[whole(a.shape) for a in kept],
            out_specs=[whole(o.shape) for o in outs],
        ),
        out_shape=outs,
        cost_estimate=CHEAP,
        compiler_params=pltpu.CompilerParams(vmem_limit_bytes=SMALL_VMEM),
    )(where, *kept)


def row_distances(depth):
    steps = depth.bit_length() - 1
    even = [sum(((m >> (steps - 1 - i)) & 1) << i for i in range(steps)) for m in range(depth)]
    return even, list(range(depth))


def weight_grad_kernel(parts, depth, model, wide, where_ref, *refs):
    slots = refs[:parts]
    out_ref, in_ref, ffn_out_ref, vec_ref, scratch, vec_scratch = refs[parts:]
    step = pl.program_id(0)
    group = jnp.bitwise_xor(step, where_ref[0])
    piece = slots[0].shape[2]
    width = model // GROUPS
    half = parts // 2
    ffn_rows, out_rows = width // half, model // (parts * GROUPS)
    tiles, wide_tiles = model // 128, wide // 128
    even, odd = row_distances(depth)
    for p in range(parts):
        part = jnp.bitwise_xor(where_ref[1], p)
        for z in range(depth):
            distance = jnp.where(part % 2 == 1, odd[z], even[z])
            scratch[part, jnp.bitwise_xor(where_ref[2], distance)] = slots[p][0, z].astype(f32)

    def rows(part, first, count):
        last = first + count
        cuts = [first] + [c for c in range(0, depth * piece, piece) if first < c < last] + [last]
        return jnp.concatenate(
            [scratch[part, x // piece, x % piece : x % piece + y - x, :] for x, y in zip(cuts, cuts[1:])]
        )

    base = wide_tiles * ffn_rows
    for part in range(parts):
        target = in_ref if part < half else ffn_out_ref
        mine = slice((part % half) * ffn_rows, (part % half + 1) * ffn_rows)
        for t in range(wide_tiles):
            target[0, mine, t * 128 : (t + 1) * 128] = rows(part, t * ffn_rows, ffn_rows)
        for t in range(tiles):
            out_ref[part, 0, :, t * 128 : (t + 1) * 128] = rows(part, base + t * out_rows, out_rows)
        start = pl.multiple_of(part * (model // parts) + group * out_rows, out_rows)
        vec_scratch[pl.ds(start, out_rows), :] = rows(part, base + tiles * out_rows, out_rows)

    @pl.when(step == GROUPS - 1)
    def _():
        vec_ref[...] = vec_scratch[...].T[:8]


def weight_grads(where, slots, model, wide):
    parts = len(slots)
    _, depth, piece, _ = slots[0].shape
    width = model // GROUPS
    out_rows = model // (parts * GROUPS)

    def slot_spec(p):
        def place(j, w):
            return (swapped(j, jnp.bitwise_xor(w[1], p) % 2 == 1), 0, 0, 0)

        return pl.BlockSpec((1, depth, piece, 128), place)

    out, ffn_in, ffn_out_t, vectors = pl.pallas_call(
        functools.partial(weight_grad_kernel, parts, depth, model, wide),
        name="weight_grads",
        grid_spec=pltpu.PrefetchScalarGridSpec(
            num_scalar_prefetch=1,
            grid=(GROUPS,),
            in_specs=[slot_spec(p) for p in range(parts)],
            out_specs=[
                pl.BlockSpec((parts, 1, out_rows, model), lambda j, w: (0, jnp.bitwise_xor(j, w[0]), 0, 0)),
                pl.BlockSpec((1, width, wide), lambda j, w: (jnp.bitwise_xor(j, w[0]), 0, 0)),
                pl.BlockSpec((1, width, wide), lambda j, w: (jnp.bitwise_xor(j, w[0]), 0, 0)),
                pl.BlockSpec((8, model), lambda j, w: (0, 0)),
            ],
            scratch_shapes=[pltpu.VMEM((parts, depth, piece, 128), f32), pltpu.VMEM((model, 128), f32)],
        ),
        out_shape=[
            jax.ShapeDtypeStruct((parts, GROUPS, out_rows, model), f32),
            jax.ShapeDtypeStruct((GROUPS, width, wide), f32),
            jax.ShapeDtypeStruct((GROUPS, width, wide), f32),
            jax.ShapeDtypeStruct((8, model), f32),
        ],
        cost_estimate=CHEAP,
        compiler_params=pltpu.CompilerParams(vmem_limit_bytes=SMALL_VMEM),
    )(where, *slots)
    return out.reshape(model, model), ffn_in, ffn_out_t, vectors


def finish_kernel(parts, where_ref, *refs):
    slots, thirds, refs = refs[:GROUPS], refs[GROUPS : GROUPS + parts], refs[GROUPS + parts :]
    first_grad_ref, out_ref, *outs = refs[:-1]
    scratch = refs[-1]
    width = slots[0].shape[0]
    for j in range(GROUPS):
        mine = pl.ds(pl.multiple_of(jnp.bitwise_xor(where_ref[0], j) * width, width), width)
        scratch[mine, :] = first_grad_ref[mine, :] + slots[j][...].astype(f32)
    out_ref[0] = scratch[...].T
    for p in range(parts):
        chunk = thirds[p].shape[2]
        part = jnp.bitwise_xor(where_ref[1], p)
        rows = pl.ds(pl.multiple_of(part * chunk, chunk), chunk)
        for m in range(GROUPS):
            group = jnp.bitwise_xor(where_ref[0], swapped(m, part % 2 == 1))
            for which in range(3):
                outs[which][group, rows, :] = thirds[p][m, which].astype(f32)


def finish(where, slots, thirds, first_grad):
    model, toks = first_grad.shape
    width = model // GROUPS
    args = (*slots, *thirds, first_grad)
    outs = [jax.ShapeDtypeStruct((1, toks, model), f32)] + [
        jax.ShapeDtypeStruct((GROUPS, width, width), f32)
    ] * 3
    return pl.pallas_call(
        functools.partial(finish_kernel, len(thirds)),
        name="finish",
        grid_spec=pltpu.PrefetchScalarGridSpec(
            num_scalar_prefetch=1,
            grid=(1,),
            in_specs=[whole(a.shape) for a in args],
            out_specs=[whole(o.shape) for o in outs],
            scratch_shapes=[pltpu.VMEM((model, toks), f32)],
        ),
        out_shape=outs,
        cost_estimate=CHEAP,
        compiler_params=pltpu.CompilerParams(vmem_limit_bytes=SMALL_VMEM),
    )(where, *args)


def add_low(terms):
    total = terms[0].astype(f32)
    for term in terms[1:]:
        total = total + term.astype(f32)
    return total.astype(bf16)


def shards(
    tokens,
    segment_ids,
    valid_tokens,
    q_weight,
    k_weight,
    v_weight,
    out_weight,
    gain_one,
    bias_one,
    ffn_in,
    ffn_out,
    gain_two,
    bias_two,
    cotangent,
):
    seq = lax.axis_size("seq")
    depth = lax.axis_size("rows")
    parts = seq // GROUPS
    _, toks, model = tokens.shape
    width = model // GROUPS
    wide = ffn_in.shape[2]
    place = lax.axis_index("seq")
    own_group, own_part = place // parts, place % parts
    own_row = lax.axis_index("rows")
    where = jnp.stack([own_group, own_part, own_row]).astype(jnp.int32)

    def swap(value, distance):
        return lax.ppermute(value, "seq", [(k, k ^ distance) for k in range(seq)])

    def across(value):
        return [value[0]] + [swap(value[j], parts * j) for j in range(1, GROUPS)]

    def group_swap(value, step):
        apart = [(1, 2), (2, 1)][step]
        return lax.ppermute(value, "seq", [(k, k ^ parts * apart[k % parts % 2]) for k in range(seq)])

    row_steps = depth.bit_length() - 1

    def row_swap(value, step):
        pairs = []
        for k in range(seq):
            distance = 1 << (row_steps - 1 - step if k % parts % 2 else step)
            pairs += [(k * depth + z, k * depth + (z ^ distance)) for z in range(depth)]
        return lax.ppermute(value, ("seq", "rows"), pairs)

    grouped, sends = arrange(where, tokens, segment_ids, valid_tokens)
    mine = across(sends)
    others = [swap(jnp.stack(mine), p) for p in range(1, parts)]
    blocks = jnp.stack(mine + [x[j] for x in others for j in range(GROUPS)])

    qx_far, full_far, att_c, att_d, kx, vx, near, near_valid, tok = far_attention(
        where, blocks, jnp.stack([q_weight, k_weight, v_weight])
    )
    att_far = jnp.stack([swap(att_c, parts * 2), swap(att_d, parts * 3)])
    qx, full, att_a, att_b = near_attention(near, near_valid, kx, vx, qx_far, full_far)
    att_b = swap(att_b, parts)
    slots = jnp.concatenate([att_a[None], att_b[None], grouped])
    vecs = jnp.pad(jnp.stack(after([gain_one, bias_one, gain_two, bias_two], att_a)), ((0, 4), (0, 0)))
    mixed, first_grad, sends, kept = middle(
        where, slots, att_far, cotangent, valid_tokens, vecs, out_weight, ffn_in, jnp.swapaxes(ffn_out, 1, 2)
    )
    grads = across(sends)

    pays = [outer_products(where, parts, p, kept) for p in range(1, parts)]
    moved = [[swap(x, p) for x in pays[p - 1]] for p in range(1, parts)]
    pay = outer_products(where, parts, 0, after(kept, pays))
    gx = prepare(after(grads, pay), full, model // HEADS)
    moved = after(moved, gx)
    low = add_low([pay[0]] + [x[0] for x in moved])
    high = add_low([pay[1]] + [x[1] for x in moved])

    heads, cuts = HEADS // GROUPS, 2
    calls = [(head, part) for head in range(heads) for part in range(cuts)]
    dqs, dks, dvs = [], [], []

    def work(*ready):
        head, part = calls.pop(0)
        dq, dk, dv = backward_attention(
            head,
            part,
            cuts,
            qx,
            after(gx, ready),
            kx,
            vx,
            dqs.pop() if part else None,
        )
        dqs.append(dq)
        dks.append(dk)
        dvs.append(dv)
        return dq

    moved = group_swap(high, 0)
    first = work(high, low)
    moved = after(moved, work(first))
    low, high = add_low([low[0], moved[0]]), add_low([low[1], moved[1]])
    moved = group_swap(high, 1)
    piece = add_low([low, after(moved, work(high, low))]).reshape(depth, -1, 128)
    even, odd = row_distances(depth)
    picks = [own_row ^ jnp.where(own_part % 2 == 1, odd[m], even[m]) for m in range(depth)]
    piece = jnp.stack([lax.dynamic_index_in_dim(piece, z, 0, False) for z in picks])
    for step in range(row_steps):
        count = piece.shape[0] // 2
        low, high = piece[:count], piece[count:]
        moved = row_swap(high, step)
        if len(calls) > 1:
            moved = after(moved, work(high, low))
        piece = add_low([low, moved])
    moved = row_swap(piece, row_steps - 1)
    while calls:
        done = work(piece)
        moved, dqs[-1] = after((moved, dqs[-1]), done)
    piece = jnp.concatenate([piece, moved])
    step = row_steps - 2
    moved = row_swap(piece, step)
    backs, wgrads = project_back(where, parts, tok, (q_weight, k_weight, v_weight), after(dqs, piece), dks, dvs)
    piece = jnp.concatenate([piece, moved])
    for step in reversed(range(row_steps - 2)):
        piece = jnp.concatenate([piece, row_swap(piece, step)])
    wgrads, backs, piece = after((wgrads, backs, piece[None]), piece)
    swaps = [[swap(x[p], p) for p in range(1, parts)] for x in (wgrads, backs)]
    moved = group_swap(piece, 1)
    quarter, back_sum = add_low([wgrads[0]] + swaps[0]), add_low([backs[0]] + swaps[1])
    back_first = swap(back_sum[1], parts)
    for step in range(row_steps - 1):
        quarter = add_low([quarter, row_swap(quarter, step)])
    piece = jnp.concatenate([piece, moved])
    quarter, back_sum, back_first, piece = after((quarter, back_sum, back_first, piece), quarter)
    moved = group_swap(piece, 0)
    quarter = add_low([quarter, row_swap(quarter, row_steps - 1)])
    quarter = jnp.stack([quarter, group_swap(quarter, 1)])
    piece = jnp.concatenate([piece, moved])
    quarter, back_sum, piece = after((quarter, back_sum, piece), quarter)
    slots = [piece] + [swap(piece, p) for p in range(1, parts)]
    back_moved = [back_sum[0], back_first] + [swap(back_sum[j], parts * j) for j in (2, 3)]
    moved = group_swap(quarter, 0)
    grad_out_weight, grad_ffn_in, grad_ffn_out_t, vectors = weight_grads(where, slots, model, wide)
    moved, back_moved = after((moved, back_moved), vectors)
    quarter = jnp.concatenate([quarter, moved])
    thirds = [quarter] + [swap(quarter, p) for p in range(1, parts)]
    grad_tokens, grad_q, grad_k, grad_v = finish(where, back_moved, thirds, first_grad)

    return (
        mixed,
        grad_tokens,
        grad_q,
        grad_k,
        grad_v,
        grad_out_weight,
        vectors[0],
        vectors[1],
        grad_ffn_in,
        jnp.swapaxes(grad_ffn_out_t, 1, 2),
        vectors[2],
        vectors[3],
    )


def solution(mesh):
    tokens = P("rows", "seq", None)
    flags = P("rows", "seq")
    in_specs = (tokens, flags, flags) + (P(),) * 10 + (tokens,)
    out_specs = (tokens, tokens) + (P(),) * 10
    return jax.shard_map(shards, mesh=mesh, in_specs=in_specs, out_specs=out_specs, check_vma=False)
```

```python
import functools

import jax
import jax.numpy as jnp
from jax import lax
from jax.experimental import pallas as pl
from jax.experimental.pallas import tpu as pltpu
from jax.sharding import PartitionSpec as P

HEADS = 12
GROUPS = 4
PENALTY = 2.0**30
VMEM_BYTES = 36 * 2**20
SMALL_VMEM = 20 * 2**20
ATT_BASE = 9
bf16 = jnp.bfloat16
f32 = jnp.float32


def dot(a, b, dims):
    return lax.dot_general(a, b, (dims, ((), ())), preferred_element_type=f32)


NN = ((1,), (0,))
TN = ((0,), (0,))
NT = ((1,), (1,))


def whole(shape):
    return pl.BlockSpec(shape, lambda *_: (0,) * len(shape), pipeline_mode=pl.Buffered(1))


def pieces(row):
    high = row.astype(bf16)
    rest = row - high.astype(f32)
    middle = rest.astype(bf16)
    low = (rest - middle.astype(f32)).astype(bf16)
    count = row.shape[-1]
    index = lax.broadcasted_iota(jnp.int32, (16, count), 0)
    out = jnp.where(index == 0, high.astype(f32), 0.0)
    out = jnp.where(index == 1, middle.astype(f32), out)
    out = jnp.where(index == 2, low.astype(f32), out)
    return out.astype(bf16)


def minus_rows(count):
    index = lax.broadcasted_iota(jnp.int32, (16, count), 0)
    return jnp.where(index < 3, -1.0, 0.0).astype(bf16)


def attention_vmem(keys):
    return 2**20 * (ATT_BASE + 2 * keys // 1024)


def after(value, *others):
    return lax.optimization_barrier((value, others))[0]


CHEAP = pl.CostEstimate(flops=1, bytes_accessed=1, transcendentals=0)


def arrange_kernel(where_ref, tok_ref, code_ref, grouped_ref, *sends):
    _, width, _ = grouped_ref.shape
    flipped = tok_ref[0].astype(f32).T.astype(bf16)
    for g in range(GROUPS):
        grouped_ref[g] = flipped[g * width : (g + 1) * width]
    for j, send in enumerate(sends):
        send[:width] = grouped_ref[jnp.bitwise_xor(where_ref[0], j)]
        send[width:] = code_ref[...]


def arrange(where, tokens, segment_ids, valid_tokens):
    _, toks, model = tokens.shape
    width = model // GROUPS
    index = lax.broadcasted_iota(jnp.int32, (16, toks), 0)
    codes = jnp.where(index == 0, segment_ids, jnp.where(valid_tokens == 1, segment_ids, -1))
    args = (tokens, codes.astype(bf16))
    outs = [jax.ShapeDtypeStruct((GROUPS, width, toks), bf16)] + [
        jax.ShapeDtypeStruct((width + 16, toks), bf16)
    ] * GROUPS
    grouped, *sends = pl.pallas_call(
        arrange_kernel,
        name="arrange",
        grid_spec=pltpu.PrefetchScalarGridSpec(
            num_scalar_prefetch=1,
            grid=(1,),
            in_specs=[whole(a.shape) for a in args],
            out_specs=[whole(o.shape) for o in outs],
        ),
        out_shape=outs,
        cost_estimate=CHEAP,
        compiler_params=pltpu.CompilerParams(vmem_limit_bytes=SMALL_VMEM),
    )(where, *args)
    return grouped, sends


def attend(head, size, qs, kx_ref, vx_ref, own, valids, qx_ref, full_ref, atts, total_ref, peak_ref):
    toks = atts[0].shape[1]
    tile, keys = 2 * toks, kx_ref.shape[2]
    ext = size + 16

    own_keys = kx_ref[head, :size, own : own + tile]
    self_score = jnp.sum(qs[head, :size].astype(f32) * own_keys.astype(f32), axis=0, keepdims=True)
    qx_ref[0, :ext] = qs[head]
    qx_ref[0, ext:] = pieces(self_score)

    step = 256

    def scores(first):
        return dot(kx_ref[head, :, first : first + step], qx_ref[0], TN)

    total = None
    upcoming = [scores(0), scores(step)]
    for first in range(0, keys, step):
        now = upcoming.pop(0)
        if first + 2 * step < keys:
            upcoming.append(scores(first + 2 * step))
        mixed = dot(vx_ref[head, :, first : first + step], jnp.exp(now).astype(bf16), NN)
        total = mixed if total is None else total + mixed
    total_ref[...] = total
    peak_ref[...] = self_score
    in_range = jnp.max(-total[size : size + 1]) < 2.0**100

    @pl.when(jnp.logical_not(in_range))
    def _():
        total_ref[...] = jnp.zeros_like(total_ref)
        peak_ref[...] = jnp.full_like(peak_ref, -4.0 * PENALTY)

        def again(index, carry):
            span = pl.ds(pl.multiple_of(index * step, step), step)
            now = dot(kx_ref[head, :ext, span], qs[head, :ext], TN)
            peak = jnp.maximum(peak_ref[...], jnp.max(now, axis=0, keepdims=True))
            mixed = dot(vx_ref[head, :, span], jnp.exp(now - peak).astype(bf16), NN)
            total_ref[...] = total_ref[...] * jnp.exp(peak_ref[...] - peak) + mixed
            peak_ref[...] = peak
            return carry

        lax.fori_loop(0, keys // step, again, 0)

    row_sum = -total_ref[size : size + 1]
    log_total = peak_ref[...] + jnp.log(row_sum)
    attended = jnp.where(valids, total_ref[:size] / row_sum, 0.0)
    full_ref[...] = attended
    for half in range(2):
        atts[half][...] = attended[:, half * toks : (half + 1) * toks].astype(bf16)
    qx_ref[0, ext:] = pieces(jnp.where(valids, log_total, PENALTY))


def far_kernel(parts, width, heads, where_ref, *refs):
    blocks, w_ref, qx_ref, full_ref, att_a, att_b, kx_ref, vx_ref, near_ref, valid_ref, tok_ref = refs[:11]
    far, wt, total_ref, peak_ref, far_valid = refs[11:]
    head = pl.program_id(0)
    size = width // heads
    toks = blocks.shape[2]
    tile, ext = 2 * toks, size + 16

    @pl.when(head == 0)
    def _():
        code_index = lax.broadcasted_iota(jnp.int32, (16, tile), 0).astype(f32)
        for which in range(3):
            scale = size**-0.5 if which == 0 else 1.0
            wt[which * width : (which + 1) * width, :] = (w_ref[which, 0].astype(f32) * scale).T.astype(bf16)
        for p in range(parts):
            for j in range(0, GROUPS, 2):
                b = p * GROUPS + j
                span = slice(b * toks, (b + 2) * toks)
                both = jnp.concatenate([blocks[b], blocks[b + 1]], axis=1)
                tok_ref[:, span] = both[:width]
                first = 0 if p == 0 else width
                made = dot(wt[first:], both[:width], NN).astype(bf16)
                codes = both[width:].astype(f32)
                mask = jnp.where(code_index == codes[1:2], 0.0, -PENALTY).astype(bf16)
                for h in range(heads):
                    keys = width - first + h * size
                    kx_ref[h, :size, span] = made[keys : keys + size]
                    kx_ref[h, size:ext, span] = mask
                    kx_ref[h, ext:, span] = minus_rows(tile)
                    vx_ref[h, :size, span] = made[keys + width : keys + width + size]
                    vx_ref[h, size:, span] = minus_rows(tile)
                if p == 0:
                    target, flags = (near_ref, valid_ref) if j == 0 else (far, far_valid)
                    hot = jnp.where(code_index == codes[0:1], 1.0, 0.0).astype(bf16)
                    flags[...] = jnp.broadcast_to(codes[1:2], (8, tile))
                    for h in range(heads):
                        target[h, :size] = made[h * size : (h + 1) * size]
                        target[h, size:] = hot

    valids = far_valid[0:1, :] >= 0.0
    attend(head, size, far, kx_ref, vx_ref, tile, valids, qx_ref, full_ref, (att_a, att_b), total_ref, peak_ref)


def near_kernel(size, *refs):
    near_ref, valid_ref, kx_ref, vx_ref, qx_far, full_far, qx_ref, full_ref, att_a, att_b, total_ref, peak_ref = refs
    tile = qx_far.shape[2]
    valids = valid_ref[0:1, :] >= 0.0
    qx_ref[0, :, tile:] = qx_far[0]
    full_ref[:, tile:] = full_far[...]
    attend(
        pl.program_id(0),
        size,
        near_ref,
        kx_ref,
        vx_ref,
        0,
        valids,
        qx_ref.at[:, :, :tile],
        full_ref.at[:, :tile],
        (att_a, att_b),
        total_ref,
        peak_ref,
    )


def attention_outs(heads, size, toks, tiles):
    width, count = heads * size, 2 * toks * tiles
    specs = [
        pl.BlockSpec((1, size + 32, count), lambda h, *_: (h, 0, 0)),
        pl.BlockSpec((size, count), lambda h, *_: (h, 0)),
        pl.BlockSpec((size, toks), lambda h, *_: (h, 0)),
        pl.BlockSpec((size, toks), lambda h, *_: (h, 0)),
    ]
    shapes = [
        jax.ShapeDtypeStruct((heads, size + 32, count), bf16),
        jax.ShapeDtypeStruct((width, count), f32),
        jax.ShapeDtypeStruct((width, toks), bf16),
        jax.ShapeDtypeStruct((width, toks), bf16),
    ]
    scratch = [pltpu.VMEM((size + 16, 2 * toks), f32), pltpu.VMEM((1, 2 * toks), f32)]
    return specs, shapes, scratch


def far_attention(where, blocks, weights):
    count, _, toks = blocks.shape
    parts = count // GROUPS
    width = weights.shape[2]
    heads = HEADS // GROUPS
    size = width // heads
    tile, keys = 2 * toks, count * toks
    specs, shapes, scratch = attention_outs(heads, size, toks, 1)
    shared = [
        jax.ShapeDtypeStruct((heads, size + 32, keys), bf16),
        jax.ShapeDtypeStruct((heads, size + 16, keys), bf16),
        jax.ShapeDtypeStruct((heads, size + 16, tile), bf16),
        jax.ShapeDtypeStruct((8, tile), f32),
        pltpu.HBM((width, keys), bf16),
    ]
    return pl.pallas_call(
        functools.partial(far_kernel, parts, width, heads),
        name="attention_far",
        grid_spec=pltpu.PrefetchScalarGridSpec(
            num_scalar_prefetch=1,
            grid=(heads,),
            in_specs=[whole(blocks.shape), pl.BlockSpec((3, 1, width, width), lambda h, w: (0, w[0], 0, 0))],
            out_specs=specs + [whole(x.shape) for x in shared],
            scratch_shapes=[pltpu.VMEM((heads, size + 16, tile), bf16), pltpu.VMEM((3 * width, width), bf16)]
            + scratch
            + [pltpu.VMEM((8, tile), f32)],
        ),
        out_shape=shapes + shared,
        cost_estimate=CHEAP,
        compiler_params=pltpu.CompilerParams(vmem_limit_bytes=attention_vmem(keys)),
    )(where, blocks, weights)


def near_attention(near, valid, kx, vx, qx, full):
    heads, ext, tile = near.shape
    size = ext - 16
    far_specs, _, _ = attention_outs(heads, size, tile // 2, 1)
    specs, shapes, scratch = attention_outs(heads, size, tile // 2, 2)
    return pl.pallas_call(
        functools.partial(near_kernel, size),
        name="attention_near",
        grid=(heads,),
        in_specs=[whole(x.shape) for x in (near, valid, kx, vx)] + far_specs[:2],
        out_specs=specs,
        scratch_shapes=scratch,
        out_shape=shapes,
        cost_estimate=CHEAP,
        compiler_params=pltpu.CompilerParams(vmem_limit_bytes=attention_vmem(kx.shape[2])),
    )(near, valid, kx, vx, qx, full)


def prepare_kernel(size, *refs):
    grads, full_ref, gx_ref = refs[:GROUPS], refs[GROUPS], refs[GROUPS + 1]
    toks = grads[0].shape[1]
    for head in range(gx_ref.shape[0]):
        rows = slice(head * size, (head + 1) * size)
        for j in range(GROUPS):
            span = slice(j * toks, (j + 1) * toks)
            grad = grads[j][rows, :]
            gx_ref[head, :size, span] = grad
            gx_ref[head, size:, span] = pieces(
                jnp.sum(grad.astype(f32) * full_ref[rows, span], axis=0, keepdims=True)
            )


def prepare(grads, full, size):
    width, count = full.shape
    out = jax.ShapeDtypeStruct((width // size, size + 16, count), bf16)
    return pl.pallas_call(
        functools.partial(prepare_kernel, size),
        name="prepare_backward",
        grid=(1,),
        in_specs=[whole(x.shape) for x in (*grads, full)],
        out_specs=whole(out.shape),
        out_shape=out,
        cost_estimate=CHEAP,
        compiler_params=pltpu.CompilerParams(vmem_limit_bytes=SMALL_VMEM),
    )(*grads, full)


def backward_kernel(size, step, tile, ends, qx_ref, gx_ref, kx_ref, vx_ref, *refs):
    first, last = ends
    (dq_ref, dk_ref, dv_ref), total = refs[-4:-1] if last else refs[-3:], refs[-1] if last else refs[-3]
    total[...] = jnp.zeros_like(total) if first else refs[0][...]

    def keys(index, carry):
        kspan = pl.ds(pl.multiple_of(index * step, step), step)
        dk = dv = None
        for start in range(0, qx_ref.shape[2], tile):
            qspan = slice(start, start + tile)
            probs = jnp.exp(dot(qx_ref[0, :, qspan], kx_ref[0, :, kspan], TN))
            slopes = dot(gx_ref[0, :, qspan], vx_ref[0, :, kspan], TN)
            probs_low = probs.astype(bf16)
            grad_scores = (probs * slopes).astype(bf16)
            dv_new = dot(gx_ref[0, :size, qspan], probs_low, NN)
            dk_new = dot(qx_ref[0, :size, qspan], grad_scores, NN)
            total[:, qspan] += dot(kx_ref[0, :size, kspan], grad_scores, NT)
            dv = dv_new if dv is None else dv + dv_new
            dk = dk_new if dk is None else dk + dk_new
        dv_ref[:, kspan] = dv.astype(bf16)
        dk_ref[:, kspan] = dk.astype(bf16)
        return carry

    lax.fori_loop(0, kx_ref.shape[2] // step, keys, 0)
    if last:
        dq_ref[...] = (total[...] * size**-0.5).astype(bf16)


def backward_attention(head, part, cuts, qx, gx, kx, vx, dq=None):
    size, count = vx.shape[1] - 16, qx.shape[2]
    keys = vx.shape[2] // cuts
    first, last = part == 0, part == cuts - 1
    dq_shape, sum_shape = (size, count), (size, keys)
    return pl.pallas_call(
        functools.partial(backward_kernel, size, count // 2, count // 3, (first, last)),
        name="attention_backward",
        grid=(1,),
        in_specs=[
            pl.BlockSpec((1, size + 32, count), lambda i: (head, 0, 0)),
            pl.BlockSpec((1, size + 16, count), lambda i: (head, 0, 0)),
            pl.BlockSpec((1, size + 32, keys), lambda i: (head, 0, part)),
            pl.BlockSpec((1, size + 16, keys), lambda i: (head, 0, part)),
        ]
        + [whole(dq_shape)] * (not first),
        out_specs=[whole(dq_shape), whole(sum_shape), whole(sum_shape)],
        scratch_shapes=[pltpu.VMEM(dq_shape, f32)] * last,
        out_shape=[
            jax.ShapeDtypeStruct(dq_shape, bf16 if last else f32),
            jax.ShapeDtypeStruct(sum_shape, bf16),
            jax.ShapeDtypeStruct(sum_shape, bf16),
        ],
        cost_estimate=CHEAP,
        compiler_params=pltpu.CompilerParams(vmem_limit_bytes=attention_vmem(vx.shape[2])),
    )(qx, gx, kx, vx, *([] if first else [dq]))


def project_kernel(parts, heads, cuts, where_ref, *refs):
    tok_ref, wq_ref, wk_ref, wv_ref = refs[:4]
    refs = refs[4:]
    dq = jnp.concatenate([ref[...] for ref in refs[:heads]])
    piles, refs = refs[heads : heads + 2 * sum(cuts)], refs[heads + 2 * sum(cuts) :]
    starts = [sum(cuts[:h]) for h in range(heads + 1)]
    dk, dv = (
        jnp.concatenate(
            [jnp.concatenate([ref[...] for ref in pile[x:y]], axis=1) for x, y in zip(starts, starts[1:])]
        )
        for pile in (piles[: sum(cuts)], piles[sum(cuts) :])
    )
    backs, wgrads, scratch = refs[:parts], refs[parts : 2 * parts], refs[2 * parts]
    width, keys = tok_ref.shape
    count = keys // parts
    toks = count // GROUPS

    scratch[0] = dot(tok_ref[:, :count], dq, NT).astype(bf16)
    scratch[1] = dot(tok_ref[...], dk, NT).astype(bf16)
    scratch[2] = dot(tok_ref[...], dv, NT).astype(bf16)
    for p in reversed(range(parts)):
        span = slice(p * count, (p + 1) * count)
        back = dot(wk_ref[0], dk[:, span], NN) + dot(wv_ref[0], dv[:, span], NN)
        if p == 0:
            back += dot(wq_ref[0], dq, NN)
        for j in range(GROUPS):
            backs[p][j] = back[:, j * toks : (j + 1) * toks].astype(bf16)
    chunk = width // parts
    for p in range(parts):
        rows = pl.ds(pl.multiple_of(jnp.bitwise_xor(where_ref[1], p) * chunk, chunk), chunk)
        wgrads[p][...] = scratch[:, rows, :]


def project_back(where, parts, tok, weights, cuts, dqs, dks, dvs):
    width, keys = tok.shape
    toks = keys // parts // GROUPS
    heads = len(dqs)
    flat = [*dqs, *dks, *dvs]
    weight_spec = pl.BlockSpec((1, width, width), lambda i, w: (w[0], 0, 0))
    outs = [jax.ShapeDtypeStruct((GROUPS, width, toks), bf16)] * parts + [
        jax.ShapeDtypeStruct((3, width // parts, width), bf16)
    ] * parts
    results = pl.pallas_call(
        functools.partial(project_kernel, parts, heads, cuts),
        name="project_back",
        grid_spec=pltpu.PrefetchScalarGridSpec(
            num_scalar_prefetch=1,
            grid=(1,),
            in_specs=[whole(tok.shape)] + [weight_spec] * 3 + [whole(x.shape) for x in flat],
            out_specs=[whole(o.shape) for o in outs],
            scratch_shapes=[pltpu.VMEM((3, width, width), bf16)],
        ),
        out_shape=outs,
        cost_estimate=CHEAP,
        compiler_params=pltpu.CompilerParams(vmem_limit_bytes=attention_vmem(keys)),
    )(where, tok, *weights, *flat)
    return results[:parts], results[parts:]


def norm_parts(values):
    mean = jnp.mean(values, axis=0, keepdims=True)
    center = values - mean
    spread = jnp.mean(center * center, axis=0, keepdims=True)
    scale = lax.rsqrt(spread + 1e-06)
    return center * scale, scale


def norm_back(normal, scale, grad):
    mean = jnp.mean(grad, axis=0, keepdims=True)
    cross = jnp.mean(grad * normal, axis=0, keepdims=True)
    return (grad - mean - normal * cross) * scale


def middle_kernel(where_ref, *refs):
    slot_ref, far_ref, cot_ref, valid_ref, vec_ref, w_ref, fi_ref, fo_ref = refs[:8]
    refs = refs[8:]
    mixed_ref, first_grad_ref = refs[:2]
    sends = refs[2 : 2 + GROUPS]
    att, narrow_ref, wide_ref, first_low_ref, vec_out_ref = refs[2 + GROUPS : 7 + GROUPS]
    first_ref, slope_ref, second_ref, gfirst_ref, grad_att = refs[7 + GROUPS :]
    _, width, toks = slot_ref.shape
    model = width * GROUPS
    own_group = where_ref[0]
    vecs = vec_ref[...].T
    gain_one, bias_one = vecs[:, 0:1], vecs[:, 1:2]
    gain_two, bias_two = vecs[:, 2:3], vecs[:, 3:4]

    for j in range(GROUPS):
        start = pl.multiple_of(jnp.bitwise_xor(own_group, j) * width, width)
        att[pl.ds(start, width), :] = slot_ref[j] if j < 2 else far_ref[j - 2]
    tok = jnp.concatenate([slot_ref[2 + g] for g in range(GROUPS)])
    first_pre = tok.astype(f32) + dot(w_ref[...], att[...], TN)
    normal_one, scale_one = norm_parts(first_pre)
    first_ref[...] = normal_one
    first = normal_one * gain_one + bias_one
    narrow_ref[0] = first.astype(bf16)
    for g in range(GROUPS):
        mine = slice(g * width, (g + 1) * width)
        pre = dot(fi_ref[g], narrow_ref[0, mine, :], TN)
        phi = 0.5 * (1.0 + lax.erf(pre * 0.5**0.5))
        density = jnp.exp(-0.5 * pre * pre) * 0.3989422804014327
        wide_ref[1, g] = (pre * phi).astype(bf16)
        slope_ref[g] = phi + pre * density
        second_ref[mine, :] = (first_ref[mine, :] * gain_one[mine] + bias_one[mine]) + dot(fo_ref[g], wide_ref[1, g], NN)
    normal_two, scale_two = norm_parts(second_ref[...])
    mixed_ref[0] = (normal_two * gain_two + bias_two).T
    cot = cot_ref[0].T
    grad_gain_two = jnp.sum(cot * normal_two, axis=1, keepdims=True)
    grad_bias_two = jnp.sum(cot, axis=1, keepdims=True)
    grad_second = norm_back(normal_two, scale_two, cot * gain_two)
    second_ref[...] = grad_second
    grad_low = grad_second.astype(bf16)
    narrow_ref[1] = grad_low
    for g in range(GROUPS):
        mine = slice(g * width, (g + 1) * width)
        ghp = (dot(fo_ref[g], grad_low[mine, :], TN) * slope_ref[g]).astype(bf16)
        wide_ref[0, g] = ghp
        gfirst_ref[mine, :] = second_ref[mine, :] + dot(fi_ref[g], ghp, NN)
    grad_first = gfirst_ref[...]
    normal_one = first_ref[...]
    grad_gain_one = jnp.sum(grad_first * normal_one, axis=1, keepdims=True)
    grad_bias_one = jnp.sum(grad_first, axis=1, keepdims=True)
    first_grad = norm_back(normal_one, scale_one, grad_first * gain_one)
    first_grad_ref[...] = first_grad
    first_low = first_grad.astype(bf16)
    first_low_ref[...] = first_low
    grad_att[...] = jnp.where(valid_ref[...] == 1, dot(w_ref[...], first_low, NN), 0.0).astype(bf16)
    for j in range(GROUPS):
        start = pl.multiple_of(jnp.bitwise_xor(own_group, j) * width, width)
        sends[j][...] = grad_att[pl.ds(start, width), :]

    lane = lax.broadcasted_iota(jnp.int32, (model, 128), 1)
    vectors = jnp.where(lane == 0, grad_gain_one, 0.0)
    vectors = jnp.where(lane == 1, grad_bias_one, vectors)
    vectors = jnp.where(lane == 2, grad_gain_two, vectors)
    vectors = jnp.where(lane == 3, grad_bias_two, vectors)
    vec_out_ref[...] = vectors.astype(bf16)


def middle(where, slots, far, cotangent, valid, vecs, out_weight, ffn_in, ffn_out_t):
    _, width, toks = slots.shape
    model = width * GROUPS
    wide = ffn_in.shape[2]
    args = (slots, far, cotangent, valid, vecs, out_weight, ffn_in, ffn_out_t)
    outs = (
        [jax.ShapeDtypeStruct((1, toks, model), f32), pltpu.HBM((model, toks), f32)]
        + [jax.ShapeDtypeStruct((width, toks), bf16)] * GROUPS
        + [
            jax.ShapeDtypeStruct((model, toks), bf16),
            jax.ShapeDtypeStruct((2, model, toks), bf16),
            jax.ShapeDtypeStruct((2, GROUPS, wide, toks), bf16),
            jax.ShapeDtypeStruct((model, toks), bf16),
            jax.ShapeDtypeStruct((model, 128), bf16),
        ]
    )
    results = pl.pallas_call(
        middle_kernel,
        name="middle",
        grid_spec=pltpu.PrefetchScalarGridSpec(
            num_scalar_prefetch=1,
            grid=(1,),
            in_specs=[whole(a.shape) for a in args],
            out_specs=[whole(o.shape) for o in outs],
            scratch_shapes=[
                pltpu.VMEM((model, toks), f32),
                pltpu.VMEM((GROUPS, wide, toks), f32),
                pltpu.VMEM((model, toks), f32),
                pltpu.VMEM((model, toks), f32),
                pltpu.VMEM((model, toks), bf16),
            ],
        ),
        out_shape=outs,
        cost_estimate=CHEAP,
        compiler_params=pltpu.CompilerParams(vmem_limit_bytes=VMEM_BYTES),
    )(where, *args)
    return results[0], results[1], results[2 : 2 + GROUPS], results[2 + GROUPS :]


def swapped(slot, odd):
    return jnp.where(odd, slot, (slot % 2) * 2 + slot // 2)


def outer_kernel(parts, slot, where_ref, att, narrow_ref, wide_ref, first_low_ref, vec_ref, near_ref, far_ref, scratch):
    model = att.shape[0]
    width = model // GROUPS
    wide = wide_ref.shape[2]
    half = parts // 2
    own_group, part = where_ref[0], jnp.bitwise_xor(where_ref[1], slot)
    ffn_rows, out_rows = width // half, model // (parts * GROUPS)
    array, piece = part // half, part % half
    tiles, wide_tiles = model // 128, wide // 128

    out_start = pl.multiple_of(part * (model // parts), model // parts)
    scratch[...] = dot(att[pl.ds(out_start, model // parts), :], first_low_ref[...], NT).astype(bf16)
    base = wide_tiles * ffn_rows
    for m in range(GROUPS):
        target, index = (near_ref, far_ref)[m // 2], m % 2
        group = jnp.bitwise_xor(own_group, swapped(m, part % 2 == 1))
        start = pl.multiple_of(group * width + piece * ffn_rows, ffn_rows)
        made = dot(narrow_ref[array, pl.ds(start, ffn_rows), :], wide_ref[array, group], NT).astype(bf16)
        for t in range(wide_tiles):
            target[index, t * ffn_rows : (t + 1) * ffn_rows] = made[:, t * 128 : (t + 1) * 128]
        rows = pl.ds(pl.multiple_of(group * out_rows, out_rows), out_rows)
        for t in range(tiles):
            span = slice(base + t * out_rows, base + (t + 1) * out_rows)
            target[index, span] = scratch[rows, t * 128 : (t + 1) * 128]
        rows = pl.ds(pl.multiple_of(out_start + group * out_rows, out_rows), out_rows)
        target[index, base + tiles * out_rows :] = vec_ref[rows, :]


def outer_products(where, parts, slot, kept):
    att, narrow, wide_pair, _, _ = kept
    model = att.shape[0]
    wide = wide_pair.shape[2]
    rows = (wide // 128) * (model // GROUPS // (parts // 2)) + (model // 128 + 1) * (model // (parts * GROUPS))
    outs = [jax.ShapeDtypeStruct((2, rows, 128), bf16)] * 2
    return pl.pallas_call(
        functools.partial(outer_kernel, parts, slot),
        name="outer_products",
        grid_spec=pltpu.PrefetchScalarGridSpec(
            num_scalar_prefetch=1,
            grid=(1,),
            in_specs=[whole(a.shape) for a in kept],
            out_specs=[whole(o.shape) for o in outs],
            scratch_shapes=[pltpu.VMEM((model // parts, model), bf16)],
        ),
        out_shape=outs,
        cost_estimate=CHEAP,
        compiler_params=pltpu.CompilerParams(vmem_limit_bytes=SMALL_VMEM),
    )(where, *kept)


def row_distances(depth):
    steps = depth.bit_length() - 1
    even = [sum(((m >> (steps - 1 - i)) & 1) << i for i in range(steps)) for m in range(depth)]
    return even, list(range(depth))


def weight_grad_kernel(parts, depth, model, wide, where_ref, *refs):
    slots = refs[:parts]
    out_ref, in_ref, ffn_out_ref, vec_ref, scratch, vec_scratch = refs[parts:]
    step = pl.program_id(0)
    group = jnp.bitwise_xor(step, where_ref[0])
    piece = slots[0].shape[2]
    width = model // GROUPS
    half = parts // 2
    ffn_rows, out_rows = width // half, model // (parts * GROUPS)
    tiles, wide_tiles = model // 128, wide // 128
    even, odd = row_distances(depth)
    for p in range(parts):
        part = jnp.bitwise_xor(where_ref[1], p)
        for z in range(depth):
            distance = jnp.where(part % 2 == 1, odd[z], even[z])
            scratch[part, jnp.bitwise_xor(where_ref[2], distance)] = slots[p][0, z].astype(f32)

    def rows(part, first, count):
        last = first + count
        cuts = [first] + [c for c in range(0, depth * piece, piece) if first < c < last] + [last]
        return jnp.concatenate(
            [scratch[part, x // piece, x % piece : x % piece + y - x, :] for x, y in zip(cuts, cuts[1:])]
        )

    base = wide_tiles * ffn_rows
    for part in range(parts):
        target = in_ref if part < half else ffn_out_ref
        mine = slice((part % half) * ffn_rows, (part % half + 1) * ffn_rows)
        for t in range(wide_tiles):
            target[0, mine, t * 128 : (t + 1) * 128] = rows(part, t * ffn_rows, ffn_rows)
        for t in range(tiles):
            out_ref[part, 0, :, t * 128 : (t + 1) * 128] = rows(part, base + t * out_rows, out_rows)
        start = pl.multiple_of(part * (model // parts) + group * out_rows, out_rows)
        vec_scratch[pl.ds(start, out_rows), :] = rows(part, base + tiles * out_rows, out_rows)

    @pl.when(step == GROUPS - 1)
    def _():
        vec_ref[...] = vec_scratch[...].T[:8]


def weight_grads(where, slots, model, wide):
    parts = len(slots)
    _, depth, piece, _ = slots[0].shape
    width = model // GROUPS
    out_rows = model // (parts * GROUPS)

    def slot_spec(p):
        def place(j, w):
            return (swapped(j, jnp.bitwise_xor(w[1], p) % 2 == 1), 0, 0, 0)

        return pl.BlockSpec((1, depth, piece, 128), place)

    out, ffn_in, ffn_out_t, vectors = pl.pallas_call(
        functools.partial(weight_grad_kernel, parts, depth, model, wide),
        name="weight_grads",
        grid_spec=pltpu.PrefetchScalarGridSpec(
            num_scalar_prefetch=1,
            grid=(GROUPS,),
            in_specs=[slot_spec(p) for p in range(parts)],
            out_specs=[
                pl.BlockSpec((parts, 1, out_rows, model), lambda j, w: (0, jnp.bitwise_xor(j, w[0]), 0, 0)),
                pl.BlockSpec((1, width, wide), lambda j, w: (jnp.bitwise_xor(j, w[0]), 0, 0)),
                pl.BlockSpec((1, width, wide), lambda j, w: (jnp.bitwise_xor(j, w[0]), 0, 0)),
                pl.BlockSpec((8, model), lambda j, w: (0, 0)),
            ],
            scratch_shapes=[pltpu.VMEM((parts, depth, piece, 128), f32), pltpu.VMEM((model, 128), f32)],
        ),
        out_shape=[
            jax.ShapeDtypeStruct((parts, GROUPS, out_rows, model), f32),
            jax.ShapeDtypeStruct((GROUPS, width, wide), f32),
            jax.ShapeDtypeStruct((GROUPS, width, wide), f32),
            jax.ShapeDtypeStruct((8, model), f32),
        ],
        cost_estimate=CHEAP,
        compiler_params=pltpu.CompilerParams(vmem_limit_bytes=SMALL_VMEM),
    )(where, *slots)
    return out.reshape(model, model), ffn_in, ffn_out_t, vectors


def finish_kernel(parts, where_ref, *refs):
    slots, thirds, refs = refs[:GROUPS], refs[GROUPS : GROUPS + parts], refs[GROUPS + parts :]
    first_grad_ref, out_ref, *outs = refs[:-1]
    scratch = refs[-1]
    width = slots[0].shape[0]
    for j in range(GROUPS):
        mine = pl.ds(pl.multiple_of(jnp.bitwise_xor(where_ref[0], j) * width, width), width)
        scratch[mine, :] = first_grad_ref[mine, :] + slots[j][...].astype(f32)
    out_ref[0] = scratch[...].T
    for p in range(parts):
        chunk = thirds[p].shape[2]
        part = jnp.bitwise_xor(where_ref[1], p)
        rows = pl.ds(pl.multiple_of(part * chunk, chunk), chunk)
        for m in range(GROUPS):
            group = jnp.bitwise_xor(where_ref[0], swapped(m, part % 2 == 1))
            for which in range(3):
                outs[which][group, rows, :] = thirds[p][m, which].astype(f32)


def finish(where, slots, thirds, first_grad):
    model, toks = first_grad.shape
    width = model // GROUPS
    args = (*slots, *thirds, first_grad)
    outs = [jax.ShapeDtypeStruct((1, toks, model), f32)] + [
        jax.ShapeDtypeStruct((GROUPS, width, width), f32)
    ] * 3
    return pl.pallas_call(
        functools.partial(finish_kernel, len(thirds)),
        name="finish",
        grid_spec=pltpu.PrefetchScalarGridSpec(
            num_scalar_prefetch=1,
            grid=(1,),
            in_specs=[whole(a.shape) for a in args],
            out_specs=[whole(o.shape) for o in outs],
            scratch_shapes=[pltpu.VMEM((model, toks), f32)],
        ),
        out_shape=outs,
        cost_estimate=CHEAP,
        compiler_params=pltpu.CompilerParams(vmem_limit_bytes=SMALL_VMEM),
    )(where, *args)


def add_low(terms):
    total = terms[0].astype(f32)
    for term in terms[1:]:
        total = total + term.astype(f32)
    return total.astype(bf16)


def shards(
    tokens,
    segment_ids,
    valid_tokens,
    q_weight,
    k_weight,
    v_weight,
    out_weight,
    gain_one,
    bias_one,
    ffn_in,
    ffn_out,
    gain_two,
    bias_two,
    cotangent,
):
    seq = lax.axis_size("seq")
    depth = lax.axis_size("rows")
    parts = seq // GROUPS
    _, toks, model = tokens.shape
    width = model // GROUPS
    wide = ffn_in.shape[2]
    place = lax.axis_index("seq")
    own_group, own_part = place // parts, place % parts
    own_row = lax.axis_index("rows")
    where = jnp.stack([own_group, own_part, own_row]).astype(jnp.int32)

    def swap(value, distance):
        return lax.ppermute(value, "seq", [(k, k ^ distance) for k in range(seq)])

    def across(value):
        return [value[0]] + [swap(value[j], parts * j) for j in range(1, GROUPS)]

    def group_swap(value, step):
        apart = [(1, 2), (2, 1)][step]
        return lax.ppermute(value, "seq", [(k, k ^ parts * apart[k % parts % 2]) for k in range(seq)])

    row_steps = depth.bit_length() - 1

    def row_swap(value, step):
        pairs = []
        for k in range(seq):
            distance = 1 << (row_steps - 1 - step if k % parts % 2 else step)
            pairs += [(k * depth + z, k * depth + (z ^ distance)) for z in range(depth)]
        return lax.ppermute(value, ("seq", "rows"), pairs)

    grouped, sends = arrange(where, tokens, segment_ids, valid_tokens)
    mine = across(sends)
    others = [swap(jnp.stack(mine), p) for p in range(1, parts)]
    blocks = jnp.stack(mine + [x[j] for x in others for j in range(GROUPS)])

    qx_far, full_far, att_c, att_d, kx, vx, near, near_valid, tok = far_attention(
        where, blocks, jnp.stack([q_weight, k_weight, v_weight])
    )
    att_far = jnp.stack([swap(att_c, parts * 2), swap(att_d, parts * 3)])
    qx, full, att_a, att_b = near_attention(near, near_valid, kx, vx, qx_far, full_far)
    att_b = swap(att_b, parts)
    slots = jnp.concatenate([att_a[None], att_b[None], grouped])
    vecs = jnp.pad(jnp.stack(after([gain_one, bias_one, gain_two, bias_two], att_a)), ((0, 4), (0, 0)))
    mixed, first_grad, sends, kept = middle(
        where, slots, att_far, cotangent, valid_tokens, vecs, out_weight, ffn_in, jnp.swapaxes(ffn_out, 1, 2)
    )
    grads = across(sends)

    pays = [outer_products(where, parts, p, kept) for p in range(1, parts)]
    moved = [[swap(x, p) for x in pays[p - 1]] for p in range(1, parts)]
    pay = outer_products(where, parts, 0, after(kept, pays))
    gx = prepare(after(grads, pay), full, model // HEADS)
    moved = after(moved, gx)
    low = add_low([pay[0]] + [x[0] for x in moved])
    high = add_low([pay[1]] + [x[1] for x in moved])

    cuts = [1, 2, 2]
    calls = [(head, part) for head, count in enumerate(cuts) for part in range(count)]
    dqs, dks, dvs = [], [], []

    def work(*ready):
        head, part = calls.pop(0)
        dq, dk, dv = backward_attention(
            head,
            part,
            cuts[head],
            qx,
            after(gx, ready),
            kx,
            vx,
            dqs.pop() if part else None,
        )
        dqs.append(dq)
        dks.append(dk)
        dvs.append(dv)
        return dq

    moved = group_swap(high, 0)
    moved = after(moved, work(high, low))
    low, high = add_low([low[0], moved[0]]), add_low([low[1], moved[1]])
    moved = group_swap(high, 1)
    piece = add_low([low, after(moved, work(high, low))]).reshape(depth, -1, 128)
    even, odd = row_distances(depth)
    picks = [own_row ^ jnp.where(own_part % 2 == 1, odd[m], even[m]) for m in range(depth)]
    piece = jnp.stack([lax.dynamic_index_in_dim(piece, z, 0, False) for z in picks])
    for step in range(row_steps):
        count = piece.shape[0] // 2
        low, high = piece[:count], piece[count:]
        moved = row_swap(high, step)
        if len(calls) > 1:
            moved = after(moved, work(high, low))
        piece = add_low([low, moved])
    moved = row_swap(piece, row_steps - 1)
    while calls:
        done = work(piece)
        moved, dqs[-1] = after((moved, dqs[-1]), done)
    piece = jnp.concatenate([piece, moved])
    step = row_steps - 2
    moved = row_swap(piece, step)
    backs, wgrads = project_back(where, parts, tok, (q_weight, k_weight, v_weight), cuts, after(dqs, piece), dks, dvs)
    piece = jnp.concatenate([piece, moved])
    for step in reversed(range(row_steps - 2)):
        piece = jnp.concatenate([piece, row_swap(piece, step)])
    wgrads, backs, piece = after((wgrads, backs, piece[None]), piece)
    swaps = [[swap(x[p], p) for p in range(1, parts)] for x in (wgrads, backs)]
    moved = group_swap(piece, 1)
    quarter, back_sum = add_low([wgrads[0]] + swaps[0]), add_low([backs[0]] + swaps[1])
    back_first = swap(back_sum[1], parts)
    for step in range(row_steps - 1):
        quarter = add_low([quarter, row_swap(quarter, step)])
    piece = jnp.concatenate([piece, moved])
    quarter, back_sum, back_first, piece = after((quarter, back_sum, back_first, piece), quarter)
    moved = group_swap(piece, 0)
    quarter = add_low([quarter, row_swap(quarter, row_steps - 1)])
    quarter = jnp.stack([quarter, group_swap(quarter, 1)])
    piece = jnp.concatenate([piece, moved])
    quarter, back_sum, piece = after((quarter, back_sum, piece), quarter)
    slots = [piece] + [swap(piece, p) for p in range(1, parts)]
    back_moved = [back_sum[0], back_first] + [swap(back_sum[j], parts * j) for j in (2, 3)]
    moved = group_swap(quarter, 0)
    grad_out_weight, grad_ffn_in, grad_ffn_out_t, vectors = weight_grads(where, slots, model, wide)
    moved, back_moved = after((moved, back_moved), vectors)
    quarter = jnp.concatenate([quarter, moved])
    thirds = [quarter] + [swap(quarter, p) for p in range(1, parts)]
    grad_tokens, grad_q, grad_k, grad_v = finish(where, back_moved, thirds, first_grad)

    return (
        mixed,
        grad_tokens,
        grad_q,
        grad_k,
        grad_v,
        grad_out_weight,
        vectors[0],
        vectors[1],
        grad_ffn_in,
        jnp.swapaxes(grad_ffn_out_t, 1, 2),
        vectors[2],
        vectors[3],
    )


def solution(mesh):
    tokens = P("rows", "seq", None)
    flags = P("rows", "seq")
    in_specs = (tokens, flags, flags) + (P(),) * 10 + (tokens,)
    out_specs = (tokens, tokens) + (P(),) * 10
    return jax.shard_map(shards, mesh=mesh, in_specs=in_specs, out_specs=out_specs, check_vma=False)
```

```python
import functools

import jax
import jax.numpy as jnp
from jax import lax
from jax.experimental import pallas as pl
from jax.experimental.pallas import tpu as pltpu
from jax.sharding import PartitionSpec as P

HEADS = 12
GROUPS = 4
PENALTY = 2.0**30
VMEM_BYTES = 36 * 2**20
SMALL_VMEM = 20 * 2**20
ATT_BASE = 9
bf16 = jnp.bfloat16
f32 = jnp.float32


def dot(a, b, dims):
    return lax.dot_general(a, b, (dims, ((), ())), preferred_element_type=f32)


NN = ((1,), (0,))
TN = ((0,), (0,))
NT = ((1,), (1,))


def whole(shape):
    return pl.BlockSpec(shape, lambda *_: (0,) * len(shape), pipeline_mode=pl.Buffered(1))


def pieces(row):
    high = row.astype(bf16)
    rest = row - high.astype(f32)
    middle = rest.astype(bf16)
    low = (rest - middle.astype(f32)).astype(bf16)
    count = row.shape[-1]
    index = lax.broadcasted_iota(jnp.int32, (16, count), 0)
    out = jnp.where(index == 0, high.astype(f32), 0.0)
    out = jnp.where(index == 1, middle.astype(f32), out)
    out = jnp.where(index == 2, low.astype(f32), out)
    return out.astype(bf16)


def minus_rows(count):
    index = lax.broadcasted_iota(jnp.int32, (16, count), 0)
    return jnp.where(index < 3, -1.0, 0.0).astype(bf16)


def attention_vmem(keys):
    return 2**20 * (ATT_BASE + 2 * keys // 1024)


def after(value, *others):
    return lax.optimization_barrier((value, others))[0]


CHEAP = pl.CostEstimate(flops=1, bytes_accessed=1, transcendentals=0)


def arrange_kernel(where_ref, tok_ref, code_ref, grouped_ref, *sends):
    _, width, _ = grouped_ref.shape
    flipped = tok_ref[0].astype(f32).T.astype(bf16)
    for g in range(GROUPS):
        grouped_ref[g] = flipped[g * width : (g + 1) * width]
    for j, send in enumerate(sends):
        send[:width] = grouped_ref[jnp.bitwise_xor(where_ref[0], j)]
        send[width:] = code_ref[...]


def arrange(where, tokens, segment_ids, valid_tokens):
    _, toks, model = tokens.shape
    width = model // GROUPS
    index = lax.broadcasted_iota(jnp.int32, (16, toks), 0)
    codes = jnp.where(index == 0, segment_ids, jnp.where(valid_tokens == 1, segment_ids, -1))
    args = (tokens, codes.astype(bf16))
    outs = [jax.ShapeDtypeStruct((GROUPS, width, toks), bf16)] + [
        jax.ShapeDtypeStruct((width + 16, toks), bf16)
    ] * GROUPS
    grouped, *sends = pl.pallas_call(
        arrange_kernel,
        name="arrange",
        grid_spec=pltpu.PrefetchScalarGridSpec(
            num_scalar_prefetch=1,
            grid=(1,),
            in_specs=[whole(a.shape) for a in args],
            out_specs=[whole(o.shape) for o in outs],
        ),
        out_shape=outs,
        cost_estimate=CHEAP,
        compiler_params=pltpu.CompilerParams(vmem_limit_bytes=SMALL_VMEM),
    )(where, *args)
    return grouped, sends


def attend(head, size, qs, kx_ref, vx_ref, own, valids, qx_ref, full_ref, atts, total_ref, peak_ref):
    toks = atts[0].shape[1]
    tile, keys = 2 * toks, kx_ref.shape[2]
    ext = size + 16

    own_keys = kx_ref[head, :size, own : own + tile]
    self_score = jnp.sum(qs[head, :size].astype(f32) * own_keys.astype(f32), axis=0, keepdims=True)
    qx_ref[0, :ext] = qs[head]
    qx_ref[0, ext:] = pieces(self_score)

    step = 256

    def scores(first):
        return dot(kx_ref[head, :, first : first + step], qx_ref[0], TN)

    total = None
    upcoming = [scores(0), scores(step)]
    for first in range(0, keys, step):
        now = upcoming.pop(0)
        if first + 2 * step < keys:
            upcoming.append(scores(first + 2 * step))
        mixed = dot(vx_ref[head, :, first : first + step], jnp.exp(now).astype(bf16), NN)
        total = mixed if total is None else total + mixed
    total_ref[...] = total
    peak_ref[...] = self_score
    in_range = jnp.max(-total[size : size + 1]) < 2.0**100

    @pl.when(jnp.logical_not(in_range))
    def _():
        total_ref[...] = jnp.zeros_like(total_ref)
        peak_ref[...] = jnp.full_like(peak_ref, -4.0 * PENALTY)

        def again(index, carry):
            span = pl.ds(pl.multiple_of(index * step, step), step)
            now = dot(kx_ref[head, :ext, span], qs[head, :ext], TN)
            peak = jnp.maximum(peak_ref[...], jnp.max(now, axis=0, keepdims=True))
            mixed = dot(vx_ref[head, :, span], jnp.exp(now - peak).astype(bf16), NN)
            total_ref[...] = total_ref[...] * jnp.exp(peak_ref[...] - peak) + mixed
            peak_ref[...] = peak
            return carry

        lax.fori_loop(0, keys // step, again, 0)

    row_sum = -total_ref[size : size + 1]
    log_total = peak_ref[...] + jnp.log(row_sum)
    attended = jnp.where(valids, total_ref[:size] / row_sum, 0.0)
    full_ref[...] = attended
    for half in range(2):
        atts[half][...] = attended[:, half * toks : (half + 1) * toks].astype(bf16)
    qx_ref[0, ext:] = pieces(jnp.where(valids, log_total, PENALTY))


def far_kernel(parts, width, heads, where_ref, *refs):
    blocks, w_ref, qx_ref, full_ref, att_a, att_b, kx_ref, vx_ref, near_ref, valid_ref, tok_ref = refs[:11]
    far, wt, total_ref, peak_ref, far_valid = refs[11:]
    head = pl.program_id(0)
    size = width // heads
    toks = blocks.shape[2]
    tile, ext = 2 * toks, size + 16

    @pl.when(head == 0)
    def _():
        code_index = lax.broadcasted_iota(jnp.int32, (16, tile), 0).astype(f32)
        for which in range(3):
            scale = size**-0.5 if which == 0 else 1.0
            wt[which * width : (which + 1) * width, :] = (w_ref[which, 0].astype(f32) * scale).T.astype(bf16)
        for p in range(parts):
            for j in range(0, GROUPS, 2):
                b = p * GROUPS + j
                span = slice(b * toks, (b + 2) * toks)
                both = jnp.concatenate([blocks[b], blocks[b + 1]], axis=1)
                tok_ref[:, span] = both[:width]
                first = 0 if p == 0 else width
                made = dot(wt[first:], both[:width], NN).astype(bf16)
                codes = both[width:].astype(f32)
                mask = jnp.where(code_index == codes[1:2], 0.0, -PENALTY).astype(bf16)
                for h in range(heads):
                    keys = width - first + h * size
                    kx_ref[h, :size, span] = made[keys : keys + size]
                    kx_ref[h, size:ext, span] = mask
                    kx_ref[h, ext:, span] = minus_rows(tile)
                    vx_ref[h, :size, span] = made[keys + width : keys + width + size]
                    vx_ref[h, size:, span] = minus_rows(tile)
                if p == 0:
                    target, flags = (near_ref, valid_ref) if j == 0 else (far, far_valid)
                    hot = jnp.where(code_index == codes[0:1], 1.0, 0.0).astype(bf16)
                    flags[...] = jnp.broadcast_to(codes[1:2], (8, tile))
                    for h in range(heads):
                        target[h, :size] = made[h * size : (h + 1) * size]
                        target[h, size:] = hot

    valids = far_valid[0:1, :] >= 0.0
    attend(head, size, far, kx_ref, vx_ref, tile, valids, qx_ref, full_ref, (att_a, att_b), total_ref, peak_ref)


def near_kernel(size, *refs):
    near_ref, valid_ref, kx_ref, vx_ref, qx_far, full_far, qx_ref, full_ref, att_a, att_b, total_ref, peak_ref = refs
    tile = qx_far.shape[2]
    valids = valid_ref[0:1, :] >= 0.0
    qx_ref[0, :, tile:] = qx_far[0]
    full_ref[:, tile:] = full_far[...]
    attend(
        pl.program_id(0),
        size,
        near_ref,
        kx_ref,
        vx_ref,
        0,
        valids,
        qx_ref.at[:, :, :tile],
        full_ref.at[:, :tile],
        (att_a, att_b),
        total_ref,
        peak_ref,
    )


def attention_outs(heads, size, toks, tiles):
    width, count = heads * size, 2 * toks * tiles
    specs = [
        pl.BlockSpec((1, size + 32, count), lambda h, *_: (h, 0, 0)),
        pl.BlockSpec((size, count), lambda h, *_: (h, 0)),
        pl.BlockSpec((size, toks), lambda h, *_: (h, 0)),
        pl.BlockSpec((size, toks), lambda h, *_: (h, 0)),
    ]
    shapes = [
        jax.ShapeDtypeStruct((heads, size + 32, count), bf16),
        jax.ShapeDtypeStruct((width, count), f32),
        jax.ShapeDtypeStruct((width, toks), bf16),
        jax.ShapeDtypeStruct((width, toks), bf16),
    ]
    scratch = [pltpu.VMEM((size + 16, 2 * toks), f32), pltpu.VMEM((1, 2 * toks), f32)]
    return specs, shapes, scratch


def far_attention(where, blocks, weights):
    count, _, toks = blocks.shape
    parts = count // GROUPS
    width = weights.shape[2]
    heads = HEADS // GROUPS
    size = width // heads
    tile, keys = 2 * toks, count * toks
    specs, shapes, scratch = attention_outs(heads, size, toks, 1)
    shared = [
        jax.ShapeDtypeStruct((heads, size + 32, keys), bf16),
        jax.ShapeDtypeStruct((heads, size + 16, keys), bf16),
        jax.ShapeDtypeStruct((heads, size + 16, tile), bf16),
        jax.ShapeDtypeStruct((8, tile), f32),
        pltpu.HBM((width, keys), bf16),
    ]
    return pl.pallas_call(
        functools.partial(far_kernel, parts, width, heads),
        name="attention_far",
        grid_spec=pltpu.PrefetchScalarGridSpec(
            num_scalar_prefetch=1,
            grid=(heads,),
            in_specs=[whole(blocks.shape), pl.BlockSpec((3, 1, width, width), lambda h, w: (0, w[0], 0, 0))],
            out_specs=specs + [whole(x.shape) for x in shared],
            scratch_shapes=[pltpu.VMEM((heads, size + 16, tile), bf16), pltpu.VMEM((3 * width, width), bf16)]
            + scratch
            + [pltpu.VMEM((8, tile), f32)],
        ),
        out_shape=shapes + shared,
        cost_estimate=CHEAP,
        compiler_params=pltpu.CompilerParams(vmem_limit_bytes=attention_vmem(keys)),
    )(where, blocks, weights)


def near_attention(near, valid, kx, vx, qx, full):
    heads, ext, tile = near.shape
    size = ext - 16
    far_specs, _, _ = attention_outs(heads, size, tile // 2, 1)
    specs, shapes, scratch = attention_outs(heads, size, tile // 2, 2)
    return pl.pallas_call(
        functools.partial(near_kernel, size),
        name="attention_near",
        grid=(heads,),
        in_specs=[whole(x.shape) for x in (near, valid, kx, vx)] + far_specs[:2],
        out_specs=specs,
        scratch_shapes=scratch,
        out_shape=shapes,
        cost_estimate=CHEAP,
        compiler_params=pltpu.CompilerParams(vmem_limit_bytes=attention_vmem(kx.shape[2])),
    )(near, valid, kx, vx, qx, full)


def prepare_kernel(size, *refs):
    grads, full_ref, gx_ref = refs[:GROUPS], refs[GROUPS], refs[GROUPS + 1]
    toks = grads[0].shape[1]
    for head in range(gx_ref.shape[0]):
        rows = slice(head * size, (head + 1) * size)
        for j in range(GROUPS):
            span = slice(j * toks, (j + 1) * toks)
            grad = grads[j][rows, :]
            gx_ref[head, :size, span] = grad
            gx_ref[head, size:, span] = pieces(
                jnp.sum(grad.astype(f32) * full_ref[rows, span], axis=0, keepdims=True)
            )


def prepare(grads, full, size):
    width, count = full.shape
    out = jax.ShapeDtypeStruct((width // size, size + 16, count), bf16)
    return pl.pallas_call(
        functools.partial(prepare_kernel, size),
        name="prepare_backward",
        grid=(1,),
        in_specs=[whole(x.shape) for x in (*grads, full)],
        out_specs=whole(out.shape),
        out_shape=out,
        cost_estimate=pl.CostEstimate(flops=20 * 10**9, bytes_accessed=1, transcendentals=0),
        compiler_params=pltpu.CompilerParams(vmem_limit_bytes=SMALL_VMEM),
    )(*grads, full)


def backward_kernel(size, step, tile, ends, qx_ref, gx_ref, kx_ref, vx_ref, *refs):
    first, last = ends
    (dq_ref, dk_ref, dv_ref), total = refs[-4:-1] if last else refs[-3:], refs[-1] if last else refs[-3]
    total[...] = jnp.zeros_like(total) if first else refs[0][...]

    def keys(index, carry):
        kspan = pl.ds(pl.multiple_of(index * step, step), step)
        dk = dv = None
        for start in range(0, qx_ref.shape[2], tile):
            qspan = slice(start, start + tile)
            probs = jnp.exp(dot(qx_ref[0, :, qspan], kx_ref[0, :, kspan], TN))
            slopes = dot(gx_ref[0, :, qspan], vx_ref[0, :, kspan], TN)
            probs_low = probs.astype(bf16)
            grad_scores = (probs * slopes).astype(bf16)
            dv_new = dot(gx_ref[0, :size, qspan], probs_low, NN)
            dk_new = dot(qx_ref[0, :size, qspan], grad_scores, NN)
            total[:, qspan] += dot(kx_ref[0, :size, kspan], grad_scores, NT)
            dv = dv_new if dv is None else dv + dv_new
            dk = dk_new if dk is None else dk + dk_new
        dv_ref[:, kspan] = dv.astype(bf16)
        dk_ref[:, kspan] = dk.astype(bf16)
        return carry

    lax.fori_loop(0, kx_ref.shape[2] // step, keys, 0)
    if last:
        dq_ref[...] = (total[...] * size**-0.5).astype(bf16)


def backward_attention(head, part, cuts, qx, gx, kx, vx, dq=None):
    size, count = vx.shape[1] - 16, qx.shape[2]
    keys = vx.shape[2] // cuts
    first, last = part == 0, part == cuts - 1
    dq_shape, sum_shape = (size, count), (size, keys)
    return pl.pallas_call(
        functools.partial(backward_kernel, size, count // 2, count // 3, (first, last)),
        name="attention_backward",
        grid=(1,),
        in_specs=[
            pl.BlockSpec((1, size + 32, count), lambda i: (head, 0, 0)),
            pl.BlockSpec((1, size + 16, count), lambda i: (head, 0, 0)),
            pl.BlockSpec((1, size + 32, keys), lambda i: (head, 0, part)),
            pl.BlockSpec((1, size + 16, keys), lambda i: (head, 0, part)),
        ]
        + [whole(dq_shape)] * (not first),
        out_specs=[whole(dq_shape), whole(sum_shape), whole(sum_shape)],
        scratch_shapes=[pltpu.VMEM(dq_shape, f32)] * last,
        out_shape=[
            jax.ShapeDtypeStruct(dq_shape, bf16 if last else f32),
            jax.ShapeDtypeStruct(sum_shape, bf16),
            jax.ShapeDtypeStruct(sum_shape, bf16),
        ],
        cost_estimate=CHEAP,
        compiler_params=pltpu.CompilerParams(vmem_limit_bytes=attention_vmem(vx.shape[2])),
    )(qx, gx, kx, vx, *([] if first else [dq]))


def project_kernel(parts, heads, cuts, where_ref, *refs):
    tok_ref, wq_ref, wk_ref, wv_ref = refs[:4]
    refs = refs[4:]
    dq = jnp.concatenate([ref[...] for ref in refs[:heads]])
    piles, refs = refs[heads : heads + 2 * sum(cuts)], refs[heads + 2 * sum(cuts) :]
    starts = [sum(cuts[:h]) for h in range(heads + 1)]
    dk, dv = (
        jnp.concatenate(
            [jnp.concatenate([ref[...] for ref in pile[x:y]], axis=1) for x, y in zip(starts, starts[1:])]
        )
        for pile in (piles[: sum(cuts)], piles[sum(cuts) :])
    )
    backs, wgrads, scratch = refs[:parts], refs[parts : 2 * parts], refs[2 * parts]
    width, keys = tok_ref.shape
    count = keys // parts
    toks = count // GROUPS

    scratch[0] = dot(tok_ref[:, :count], dq, NT).astype(bf16)
    scratch[1] = dot(tok_ref[...], dk, NT).astype(bf16)
    scratch[2] = dot(tok_ref[...], dv, NT).astype(bf16)
    for p in reversed(range(parts)):
        span = slice(p * count, (p + 1) * count)
        back = dot(wk_ref[0], dk[:, span], NN) + dot(wv_ref[0], dv[:, span], NN)
        if p == 0:
            back += dot(wq_ref[0], dq, NN)
        for j in range(GROUPS):
            backs[p][j] = back[:, j * toks : (j + 1) * toks].astype(bf16)
    chunk = width // parts
    for p in range(parts):
        rows = pl.ds(pl.multiple_of(jnp.bitwise_xor(where_ref[1], p) * chunk, chunk), chunk)
        wgrads[p][...] = scratch[:, rows, :]


def project_back(where, parts, tok, weights, cuts, dqs, dks, dvs):
    width, keys = tok.shape
    toks = keys // parts // GROUPS
    heads = len(dqs)
    flat = [*dqs, *dks, *dvs]
    weight_spec = pl.BlockSpec((1, width, width), lambda i, w: (w[0], 0, 0))
    outs = [jax.ShapeDtypeStruct((GROUPS, width, toks), bf16)] * parts + [
        jax.ShapeDtypeStruct((3, width // parts, width), bf16)
    ] * parts
    results = pl.pallas_call(
        functools.partial(project_kernel, parts, heads, cuts),
        name="project_back",
        grid_spec=pltpu.PrefetchScalarGridSpec(
            num_scalar_prefetch=1,
            grid=(1,),
            in_specs=[whole(tok.shape)] + [weight_spec] * 3 + [whole(x.shape) for x in flat],
            out_specs=[whole(o.shape) for o in outs],
            scratch_shapes=[pltpu.VMEM((3, width, width), bf16)],
        ),
        out_shape=outs,
        cost_estimate=CHEAP,
        compiler_params=pltpu.CompilerParams(vmem_limit_bytes=attention_vmem(keys)),
    )(where, tok, *weights, *flat)
    return results[:parts], results[parts:]


def norm_parts(values):
    mean = jnp.mean(values, axis=0, keepdims=True)
    center = values - mean
    spread = jnp.mean(center * center, axis=0, keepdims=True)
    scale = lax.rsqrt(spread + 1e-06)
    return center * scale, scale


def norm_back(normal, scale, grad):
    mean = jnp.mean(grad, axis=0, keepdims=True)
    cross = jnp.mean(grad * normal, axis=0, keepdims=True)
    return (grad - mean - normal * cross) * scale


def middle_kernel(where_ref, *refs):
    slot_ref, far_ref, cot_ref, valid_ref, vec_ref, w_ref, fi_ref, fo_ref = refs[:8]
    refs = refs[8:]
    mixed_ref, first_grad_ref = refs[:2]
    sends = refs[2 : 2 + GROUPS]
    att, narrow_ref, wide_ref, first_low_ref, vec_out_ref = refs[2 + GROUPS : 7 + GROUPS]
    first_ref, slope_ref, second_ref, gfirst_ref, grad_att = refs[7 + GROUPS :]
    _, width, toks = slot_ref.shape
    model = width * GROUPS
    own_group = where_ref[0]
    vecs = vec_ref[...].T
    gain_one, bias_one = vecs[:, 0:1], vecs[:, 1:2]
    gain_two, bias_two = vecs[:, 2:3], vecs[:, 3:4]

    for j in range(GROUPS):
        start = pl.multiple_of(jnp.bitwise_xor(own_group, j) * width, width)
        att[pl.ds(start, width), :] = slot_ref[j] if j < 2 else far_ref[j - 2]
    tok = jnp.concatenate([slot_ref[2 + g] for g in range(GROUPS)])
    first_pre = tok.astype(f32) + dot(w_ref[...], att[...], TN)
    normal_one, scale_one = norm_parts(first_pre)
    first_ref[...] = normal_one
    first = normal_one * gain_one + bias_one
    narrow_ref[0] = first.astype(bf16)
    for g in range(GROUPS):
        mine = slice(g * width, (g + 1) * width)
        pre = dot(fi_ref[g], narrow_ref[0, mine, :], TN)
        phi = 0.5 * (1.0 + lax.erf(pre * 0.5**0.5))
        density = jnp.exp(-0.5 * pre * pre) * 0.3989422804014327
        wide_ref[1, g] = (pre * phi).astype(bf16)
        slope_ref[g] = phi + pre * density
        second_ref[mine, :] = (first_ref[mine, :] * gain_one[mine] + bias_one[mine]) + dot(fo_ref[g], wide_ref[1, g], NN)
    normal_two, scale_two = norm_parts(second_ref[...])
    mixed_ref[0] = (normal_two * gain_two + bias_two).T
    cot = cot_ref[0].T
    grad_gain_two = jnp.sum(cot * normal_two, axis=1, keepdims=True)
    grad_bias_two = jnp.sum(cot, axis=1, keepdims=True)
    grad_second = norm_back(normal_two, scale_two, cot * gain_two)
    second_ref[...] = grad_second
    grad_low = grad_second.astype(bf16)
    narrow_ref[1] = grad_low
    for g in range(GROUPS):
        mine = slice(g * width, (g + 1) * width)
        ghp = (dot(fo_ref[g], grad_low[mine, :], TN) * slope_ref[g]).astype(bf16)
        wide_ref[0, g] = ghp
        gfirst_ref[mine, :] = second_ref[mine, :] + dot(fi_ref[g], ghp, NN)
    grad_first = gfirst_ref[...]
    normal_one = first_ref[...]
    grad_gain_one = jnp.sum(grad_first * normal_one, axis=1, keepdims=True)
    grad_bias_one = jnp.sum(grad_first, axis=1, keepdims=True)
    first_grad = norm_back(normal_one, scale_one, grad_first * gain_one)
    first_grad_ref[...] = first_grad
    first_low = first_grad.astype(bf16)
    first_low_ref[...] = first_low
    grad_att[...] = jnp.where(valid_ref[...] == 1, dot(w_ref[...], first_low, NN), 0.0).astype(bf16)
    for j in range(GROUPS):
        start = pl.multiple_of(jnp.bitwise_xor(own_group, j) * width, width)
        sends[j][...] = grad_att[pl.ds(start, width), :]

    lane = lax.broadcasted_iota(jnp.int32, (model, 128), 1)
    vectors = jnp.where(lane == 0, grad_gain_one, 0.0)
    vectors = jnp.where(lane == 1, grad_bias_one, vectors)
    vectors = jnp.where(lane == 2, grad_gain_two, vectors)
    vectors = jnp.where(lane == 3, grad_bias_two, vectors)
    vec_out_ref[...] = vectors.astype(bf16)


def middle(where, slots, far, cotangent, valid, vecs, out_weight, ffn_in, ffn_out_t):
    _, width, toks = slots.shape
    model = width * GROUPS
    wide = ffn_in.shape[2]
    args = (slots, far, cotangent, valid, vecs, out_weight, ffn_in, ffn_out_t)
    outs = (
        [jax.ShapeDtypeStruct((1, toks, model), f32), pltpu.HBM((model, toks), f32)]
        + [jax.ShapeDtypeStruct((width, toks), bf16)] * GROUPS
        + [
            jax.ShapeDtypeStruct((model, toks), bf16),
            jax.ShapeDtypeStruct((2, model, toks), bf16),
            jax.ShapeDtypeStruct((2, GROUPS, wide, toks), bf16),
            jax.ShapeDtypeStruct((model, toks), bf16),
            jax.ShapeDtypeStruct((model, 128), bf16),
        ]
    )
    results = pl.pallas_call(
        middle_kernel,
        name="middle",
        grid_spec=pltpu.PrefetchScalarGridSpec(
            num_scalar_prefetch=1,
            grid=(1,),
            in_specs=[whole(a.shape) for a in args],
            out_specs=[whole(o.shape) for o in outs],
            scratch_shapes=[
                pltpu.VMEM((model, toks), f32),
                pltpu.VMEM((GROUPS, wide, toks), f32),
                pltpu.VMEM((model, toks), f32),
                pltpu.VMEM((model, toks), f32),
                pltpu.VMEM((model, toks), bf16),
            ],
        ),
        out_shape=outs,
        cost_estimate=CHEAP,
        compiler_params=pltpu.CompilerParams(vmem_limit_bytes=VMEM_BYTES),
    )(where, *args)
    return results[0], results[1], results[2 : 2 + GROUPS], results[2 + GROUPS :]


def swapped(slot, odd):
    return jnp.where(odd, slot, (slot % 2) * 2 + slot // 2)


def outer_kernel(parts, slot, where_ref, att, narrow_ref, wide_ref, first_low_ref, vec_ref, near_ref, far_ref, scratch):
    model = att.shape[0]
    width = model // GROUPS
    wide = wide_ref.shape[2]
    half = parts // 2
    own_group, part = where_ref[0], jnp.bitwise_xor(where_ref[1], slot)
    ffn_rows, out_rows = width // half, model // (parts * GROUPS)
    array, piece = part // half, part % half
    tiles, wide_tiles = model // 128, wide // 128

    out_start = pl.multiple_of(part * (model // parts), model // parts)
    scratch[...] = dot(att[pl.ds(out_start, model // parts), :], first_low_ref[...], NT).astype(bf16)
    base = wide_tiles * ffn_rows
    for m in range(GROUPS):
        target, index = (near_ref, far_ref)[m // 2], m % 2
        group = jnp.bitwise_xor(own_group, swapped(m, part % 2 == 1))
        start = pl.multiple_of(group * width + piece * ffn_rows, ffn_rows)
        made = dot(narrow_ref[array, pl.ds(start, ffn_rows), :], wide_ref[array, group], NT).astype(bf16)
        for t in range(wide_tiles):
            target[index, t * ffn_rows : (t + 1) * ffn_rows] = made[:, t * 128 : (t + 1) * 128]
        rows = pl.ds(pl.multiple_of(group * out_rows, out_rows), out_rows)
        for t in range(tiles):
            span = slice(base + t * out_rows, base + (t + 1) * out_rows)
            target[index, span] = scratch[rows, t * 128 : (t + 1) * 128]
        rows = pl.ds(pl.multiple_of(out_start + group * out_rows, out_rows), out_rows)
        target[index, base + tiles * out_rows :] = vec_ref[rows, :]


def outer_products(where, parts, slot, kept):
    att, narrow, wide_pair, _, _ = kept
    model = att.shape[0]
    wide = wide_pair.shape[2]
    rows = (wide // 128) * (model // GROUPS // (parts // 2)) + (model // 128 + 1) * (model // (parts * GROUPS))
    outs = [jax.ShapeDtypeStruct((2, rows, 128), bf16)] * 2
    return pl.pallas_call(
        functools.partial(outer_kernel, parts, slot),
        name="outer_products",
        grid_spec=pltpu.PrefetchScalarGridSpec(
            num_scalar_prefetch=1,
            grid=(1,),
            in_specs=[whole(a.shape) for a in kept],
            out_specs=[whole(o.shape) for o in outs],
            scratch_shapes=[pltpu.VMEM((model // parts, model), bf16)],
        ),
        out_shape=outs,
        cost_estimate=CHEAP,
        compiler_params=pltpu.CompilerParams(vmem_limit_bytes=SMALL_VMEM),
    )(where, *kept)


def row_distances(depth):
    steps = depth.bit_length() - 1
    even = [sum(((m >> (steps - 1 - i)) & 1) << i for i in range(steps)) for m in range(depth)]
    return even, list(range(depth))


def weight_grad_kernel(parts, depth, model, wide, where_ref, *refs):
    slots = refs[:parts]
    out_ref, in_ref, ffn_out_ref, vec_ref, scratch, vec_scratch = refs[parts:]
    step = pl.program_id(0)
    group = jnp.bitwise_xor(step, where_ref[0])
    piece = slots[0].shape[2]
    width = model // GROUPS
    half = parts // 2
    ffn_rows, out_rows = width // half, model // (parts * GROUPS)
    tiles, wide_tiles = model // 128, wide // 128
    even, odd = row_distances(depth)
    for p in range(parts):
        part = jnp.bitwise_xor(where_ref[1], p)
        for z in range(depth):
            distance = jnp.where(part % 2 == 1, odd[z], even[z])
            scratch[part, jnp.bitwise_xor(where_ref[2], distance)] = slots[p][0, z].astype(f32)

    def rows(part, first, count):
        last = first + count
        cuts = [first] + [c for c in range(0, depth * piece, piece) if first < c < last] + [last]
        return jnp.concatenate(
            [scratch[part, x // piece, x % piece : x % piece + y - x, :] for x, y in zip(cuts, cuts[1:])]
        )

    base = wide_tiles * ffn_rows
    for part in range(parts):
        target = in_ref if part < half else ffn_out_ref
        mine = slice((part % half) * ffn_rows, (part % half + 1) * ffn_rows)
        for t in range(wide_tiles):
            target[0, mine, t * 128 : (t + 1) * 128] = rows(part, t * ffn_rows, ffn_rows)
        for t in range(tiles):
            out_ref[part, 0, :, t * 128 : (t + 1) * 128] = rows(part, base + t * out_rows, out_rows)
        start = pl.multiple_of(part * (model // parts) + group * out_rows, out_rows)
        vec_scratch[pl.ds(start, out_rows), :] = rows(part, base + tiles * out_rows, out_rows)

    @pl.when(step == GROUPS - 1)
    def _():
        vec_ref[...] = vec_scratch[...].T[:8]


def weight_grads(where, slots, model, wide):
    parts = len(slots)
    _, depth, piece, _ = slots[0].shape
    width = model // GROUPS
    out_rows = model // (parts * GROUPS)

    def slot_spec(p):
        def place(j, w):
            return (swapped(j, jnp.bitwise_xor(w[1], p) % 2 == 1), 0, 0, 0)

        return pl.BlockSpec((1, depth, piece, 128), place)

    out, ffn_in, ffn_out_t, vectors = pl.pallas_call(
        functools.partial(weight_grad_kernel, parts, depth, model, wide),
        name="weight_grads",
        grid_spec=pltpu.PrefetchScalarGridSpec(
            num_scalar_prefetch=1,
            grid=(GROUPS,),
            in_specs=[slot_spec(p) for p in range(parts)],
            out_specs=[
                pl.BlockSpec((parts, 1, out_rows, model), lambda j, w: (0, jnp.bitwise_xor(j, w[0]), 0, 0)),
                pl.BlockSpec((1, width, wide), lambda j, w: (jnp.bitwise_xor(j, w[0]), 0, 0)),
                pl.BlockSpec((1, width, wide), lambda j, w: (jnp.bitwise_xor(j, w[0]), 0, 0)),
                pl.BlockSpec((8, model), lambda j, w: (0, 0)),
            ],
            scratch_shapes=[pltpu.VMEM((parts, depth, piece, 128), f32), pltpu.VMEM((model, 128), f32)],
        ),
        out_shape=[
            jax.ShapeDtypeStruct((parts, GROUPS, out_rows, model), f32),
            jax.ShapeDtypeStruct((GROUPS, width, wide), f32),
            jax.ShapeDtypeStruct((GROUPS, width, wide), f32),
            jax.ShapeDtypeStruct((8, model), f32),
        ],
        cost_estimate=CHEAP,
        compiler_params=pltpu.CompilerParams(vmem_limit_bytes=SMALL_VMEM),
    )(where, *slots)
    return out.reshape(model, model), ffn_in, ffn_out_t, vectors


def join_kernel(where_ref, *refs):
    slots, (first_grad_ref, out_ref) = refs[:GROUPS], refs[GROUPS:]
    width = slots[0].shape[0]
    for j in range(GROUPS):
        mine = pl.ds(pl.multiple_of(jnp.bitwise_xor(where_ref[0], j) * width, width), width)
        out_ref[mine, :] = first_grad_ref[mine, :] + slots[j][...].astype(f32)


def join(where, slots, first_grad):
    args = (*slots, first_grad)
    return pl.pallas_call(
        join_kernel,
        name="join",
        grid_spec=pltpu.PrefetchScalarGridSpec(
            num_scalar_prefetch=1,
            grid=(1,),
            in_specs=[whole(a.shape) for a in args],
            out_specs=whole(first_grad.shape),
        ),
        out_shape=jax.ShapeDtypeStruct(first_grad.shape, f32),
        cost_estimate=pl.CostEstimate(flops=2 * 10**9, bytes_accessed=1, transcendentals=0),
        compiler_params=pltpu.CompilerParams(vmem_limit_bytes=SMALL_VMEM),
    )(where, *args)


def finish_kernel(parts, where_ref, *refs):
    total_ref, thirds, (out_ref, *outs) = refs[0], refs[1 : 1 + parts], refs[1 + parts :]
    out_ref[0] = total_ref[...].T
    for p in range(parts):
        chunk = thirds[p].shape[2]
        part = jnp.bitwise_xor(where_ref[1], p)
        rows = pl.ds(pl.multiple_of(part * chunk, chunk), chunk)
        for m in range(GROUPS):
            group = jnp.bitwise_xor(where_ref[0], swapped(m, part % 2 == 1))
            for which in range(3):
                outs[which][group, rows, :] = thirds[p][m, which].astype(f32)


def finish(where, total, thirds):
    model, toks = total.shape
    width = model // GROUPS
    args = (total, *thirds)
    outs = [jax.ShapeDtypeStruct((1, toks, model), f32)] + [
        jax.ShapeDtypeStruct((GROUPS, width, width), f32)
    ] * 3
    return pl.pallas_call(
        functools.partial(finish_kernel, len(thirds)),
        name="finish",
        grid_spec=pltpu.PrefetchScalarGridSpec(
            num_scalar_prefetch=1,
            grid=(1,),
            in_specs=[whole(a.shape) for a in args],
            out_specs=[whole(o.shape) for o in outs],
        ),
        out_shape=outs,
        cost_estimate=CHEAP,
        compiler_params=pltpu.CompilerParams(vmem_limit_bytes=SMALL_VMEM),
    )(where, *args)


def add_low(terms):
    total = terms[0].astype(f32)
    for term in terms[1:]:
        total = total + term.astype(f32)
    return total.astype(bf16)


def shards(
    tokens,
    segment_ids,
    valid_tokens,
    q_weight,
    k_weight,
    v_weight,
    out_weight,
    gain_one,
    bias_one,
    ffn_in,
    ffn_out,
    gain_two,
    bias_two,
    cotangent,
):
    seq = lax.axis_size("seq")
    depth = lax.axis_size("rows")
    parts = seq // GROUPS
    _, toks, model = tokens.shape
    width = model // GROUPS
    wide = ffn_in.shape[2]
    place = lax.axis_index("seq")
    own_group, own_part = place // parts, place % parts
    own_row = lax.axis_index("rows")
    where = jnp.stack([own_group, own_part, own_row]).astype(jnp.int32)

    def swap(value, distance):
        return lax.ppermute(value, "seq", [(k, k ^ distance) for k in range(seq)])

    def across(value):
        return [value[0]] + [swap(value[j], parts * j) for j in range(1, GROUPS)]

    def group_swap(value, step):
        apart = [(1, 2), (2, 1)][step]
        return lax.ppermute(value, "seq", [(k, k ^ parts * apart[k % parts % 2]) for k in range(seq)])

    row_steps = depth.bit_length() - 1

    def row_swap(value, step):
        pairs = []
        for k in range(seq):
            distance = 1 << (row_steps - 1 - step if k % parts % 2 else step)
            pairs += [(k * depth + z, k * depth + (z ^ distance)) for z in range(depth)]
        return lax.ppermute(value, ("seq", "rows"), pairs)

    grouped, sends = arrange(where, tokens, segment_ids, valid_tokens)
    mine = across(sends)
    others = [swap(jnp.stack(mine), p) for p in range(1, parts)]
    blocks = jnp.stack(mine + [x[j] for x in others for j in range(GROUPS)])

    qx_far, full_far, att_c, att_d, kx, vx, near, near_valid, tok = far_attention(
        where, blocks, jnp.stack([q_weight, k_weight, v_weight])
    )
    att_far = jnp.stack([swap(att_c, parts * 2), swap(att_d, parts * 3)])
    qx, full, att_a, att_b = near_attention(near, near_valid, kx, vx, qx_far, full_far)
    att_b = swap(att_b, parts)
    slots = jnp.concatenate([att_a[None], att_b[None], grouped])
    vecs = jnp.pad(jnp.stack(after([gain_one, bias_one, gain_two, bias_two], att_a)), ((0, 4), (0, 0)))
    mixed, first_grad, sends, kept = middle(
        where, slots, att_far, cotangent, valid_tokens, vecs, out_weight, ffn_in, jnp.swapaxes(ffn_out, 1, 2)
    )
    grads = across(sends)

    pays = [outer_products(where, parts, p, kept) for p in range(1, parts)]
    moved = [[swap(x, p) for x in pays[p - 1]] for p in range(1, parts)]
    pay = outer_products(where, parts, 0, after(kept, pays))
    gx = prepare(after(grads, pay), full, model // HEADS)
    moved = after(moved, gx)
    low = add_low([pay[0]] + [x[0] for x in moved])
    high = add_low([pay[1]] + [x[1] for x in moved])

    cuts = [1, 2, 2]
    calls = [(head, part) for head, count in enumerate(cuts) for part in range(count)]
    dqs, dks, dvs = [], [], []

    def work(*ready):
        head, part = calls.pop(0)
        dq, dk, dv = backward_attention(
            head,
            part,
            cuts[head],
            qx,
            after(gx, ready),
            kx,
            vx,
            dqs.pop() if part else None,
        )
        dqs.append(dq)
        dks.append(dk)
        dvs.append(dv)
        return dq

    moved = group_swap(high, 0)
    moved = after(moved, work(high, low))
    low, high = add_low([low[0], moved[0]]), add_low([low[1], moved[1]])
    moved = group_swap(high, 1)
    piece = add_low([low, after(moved, work(high, low))]).reshape(depth, -1, 128)
    even, odd = row_distances(depth)
    picks = [own_row ^ jnp.where(own_part % 2 == 1, odd[m], even[m]) for m in range(depth)]
    piece = jnp.stack([lax.dynamic_index_in_dim(piece, z, 0, False) for z in picks])
    for step in range(row_steps):
        count = piece.shape[0] // 2
        low, high = piece[:count], piece[count:]
        moved = row_swap(high, step)
        if len(calls) > 1:
            moved = after(moved, work(high, low))
        piece = add_low([low, moved])
    moved = row_swap(piece, row_steps - 1)
    while calls:
        done = work(piece)
        moved, dqs[-1] = after((moved, dqs[-1]), done)
    piece = jnp.concatenate([piece, moved])
    step = row_steps - 2
    moved = row_swap(piece, step)
    backs, wgrads = project_back(where, parts, tok, (q_weight, k_weight, v_weight), cuts, after(dqs, piece), dks, dvs)
    piece = jnp.concatenate([piece, moved])
    for step in reversed(range(row_steps - 2)):
        piece = jnp.concatenate([piece, row_swap(piece, step)])
    wgrads, backs, piece = after((wgrads, backs, piece[None]), piece)
    swaps = [[swap(x[p], p) for p in range(1, parts)] for x in (wgrads, backs)]
    moved = group_swap(piece, 1)
    quarter, back_sum = add_low([wgrads[0]] + swaps[0]), add_low([backs[0]] + swaps[1])
    back_first = swap(back_sum[1], parts)
    for step in range(row_steps - 1):
        quarter = add_low([quarter, row_swap(quarter, step)])
    piece = jnp.concatenate([piece, moved])
    quarter, back_sum, back_first, piece = after((quarter, back_sum, back_first, piece), quarter)
    moved = group_swap(piece, 0)
    quarter = add_low([quarter, row_swap(quarter, row_steps - 1)])
    quarter = jnp.stack([quarter, group_swap(quarter, 1)])
    piece = jnp.concatenate([piece, moved])
    quarter, back_sum, piece = after((quarter, back_sum, piece), quarter)
    slots = [piece] + [swap(piece, p) for p in range(1, parts)]
    back_moved = [back_sum[0], back_first] + [swap(back_sum[j], parts * j) for j in (2, 3)]
    moved = group_swap(quarter, 0)
    grad_out_weight, grad_ffn_in, grad_ffn_out_t, vectors = weight_grads(where, slots, model, wide)
    quarter = jnp.concatenate([quarter, after(moved, vectors)])
    total = join(where, after(back_moved, vectors), first_grad)
    thirds = [quarter] + [swap(quarter, p) for p in range(1, parts)]
    grad_tokens, grad_q, grad_k, grad_v = finish(where, total, thirds)

    return (
        mixed,
        grad_tokens,
        grad_q,
        grad_k,
        grad_v,
        grad_out_weight,
        vectors[0],
        vectors[1],
        grad_ffn_in,
        jnp.swapaxes(grad_ffn_out_t, 1, 2),
        vectors[2],
        vectors[3],
    )


def solution(mesh):
    tokens = P("rows", "seq", None)
    flags = P("rows", "seq")
    in_specs = (tokens, flags, flags) + (P(),) * 10 + (tokens,)
    out_specs = (tokens, tokens) + (P(),) * 10
    return jax.shard_map(shards, mesh=mesh, in_specs=in_specs, out_specs=out_specs, check_vma=False)
```

```python
import functools

import jax
import jax.numpy as jnp
from jax import lax
from jax.experimental import pallas as pl
from jax.experimental.pallas import tpu as pltpu
from jax.sharding import PartitionSpec as P

HEADS = 12
GROUPS = 4
PENALTY = 2.0**30
VMEM_BYTES = 36 * 2**20
SMALL_VMEM = 20 * 2**20
ATT_BASE = 9
bf16 = jnp.bfloat16
f32 = jnp.float32


def dot(a, b, dims):
    return lax.dot_general(a, b, (dims, ((), ())), preferred_element_type=f32)


NN = ((1,), (0,))
TN = ((0,), (0,))
NT = ((1,), (1,))


def whole(shape):
    return pl.BlockSpec(shape, lambda *_: (0,) * len(shape), pipeline_mode=pl.Buffered(1))


def pieces(row):
    high = row.astype(bf16)
    rest = row - high.astype(f32)
    middle = rest.astype(bf16)
    low = (rest - middle.astype(f32)).astype(bf16)
    count = row.shape[-1]
    index = lax.broadcasted_iota(jnp.int32, (16, count), 0)
    out = jnp.where(index == 0, high.astype(f32), 0.0)
    out = jnp.where(index == 1, middle.astype(f32), out)
    out = jnp.where(index == 2, low.astype(f32), out)
    return out.astype(bf16)


def minus_rows(count):
    index = lax.broadcasted_iota(jnp.int32, (16, count), 0)
    return jnp.where(index < 3, -1.0, 0.0).astype(bf16)


def attention_vmem(keys):
    return 2**20 * (ATT_BASE + 2 * keys // 1024)


def after(value, *others):
    return lax.optimization_barrier((value, others))[0]


CHEAP = pl.CostEstimate(flops=1, bytes_accessed=1, transcendentals=0)


def arrange_kernel(where_ref, tok_ref, code_ref, grouped_ref, *sends):
    _, width, _ = grouped_ref.shape
    flipped = tok_ref[0].astype(f32).T.astype(bf16)
    for g in range(GROUPS):
        grouped_ref[g] = flipped[g * width : (g + 1) * width]
    for j, send in enumerate(sends):
        send[:width] = grouped_ref[jnp.bitwise_xor(where_ref[0], j)]
        send[width:] = code_ref[...]


def arrange(where, tokens, segment_ids, valid_tokens):
    _, toks, model = tokens.shape
    width = model // GROUPS
    index = lax.broadcasted_iota(jnp.int32, (16, toks), 0)
    codes = jnp.where(index == 0, segment_ids, jnp.where(valid_tokens == 1, segment_ids, -1))
    args = (tokens, codes.astype(bf16))
    outs = [jax.ShapeDtypeStruct((GROUPS, width, toks), bf16)] + [
        jax.ShapeDtypeStruct((width + 16, toks), bf16)
    ] * GROUPS
    grouped, *sends = pl.pallas_call(
        arrange_kernel,
        name="arrange",
        grid_spec=pltpu.PrefetchScalarGridSpec(
            num_scalar_prefetch=1,
            grid=(1,),
            in_specs=[whole(a.shape) for a in args],
            out_specs=[whole(o.shape) for o in outs],
        ),
        out_shape=outs,
        cost_estimate=CHEAP,
        compiler_params=pltpu.CompilerParams(vmem_limit_bytes=SMALL_VMEM),
    )(where, *args)
    return grouped, sends


def attend(head, size, qs, kx_ref, vx_ref, own, valids, qx_ref, full_ref, atts, total_ref, peak_ref):
    toks = atts[0].shape[1]
    tile, keys = 2 * toks, kx_ref.shape[2]
    ext = size + 16

    own_keys = kx_ref[head, :size, own : own + tile]
    self_score = jnp.sum(qs[head, :size].astype(f32) * own_keys.astype(f32), axis=0, keepdims=True)
    qx_ref[0, :ext] = qs[head]
    qx_ref[0, ext:] = pieces(self_score)

    step = 256

    def scores(first):
        return dot(kx_ref[head, :, first : first + step], qx_ref[0], TN)

    total = None
    upcoming = [scores(0), scores(step)]
    for first in range(0, keys, step):
        now = upcoming.pop(0)
        if first + 2 * step < keys:
            upcoming.append(scores(first + 2 * step))
        mixed = dot(vx_ref[head, :, first : first + step], jnp.exp(now).astype(bf16), NN)
        total = mixed if total is None else total + mixed
    total_ref[...] = total
    peak_ref[...] = self_score
    in_range = jnp.max(-total[size : size + 1]) < 2.0**100

    @pl.when(jnp.logical_not(in_range))
    def _():
        total_ref[...] = jnp.zeros_like(total_ref)
        peak_ref[...] = jnp.full_like(peak_ref, -4.0 * PENALTY)

        def again(index, carry):
            span = pl.ds(pl.multiple_of(index * step, step), step)
            now = dot(kx_ref[head, :ext, span], qs[head, :ext], TN)
            peak = jnp.maximum(peak_ref[...], jnp.max(now, axis=0, keepdims=True))
            mixed = dot(vx_ref[head, :, span], jnp.exp(now - peak).astype(bf16), NN)
            total_ref[...] = total_ref[...] * jnp.exp(peak_ref[...] - peak) + mixed
            peak_ref[...] = peak
            return carry

        lax.fori_loop(0, keys // step, again, 0)

    row_sum = -total_ref[size : size + 1]
    log_total = peak_ref[...] + jnp.log(row_sum)
    attended = jnp.where(valids, total_ref[:size] / row_sum, 0.0)
    full_ref[...] = attended
    for half in range(2):
        atts[half][...] = attended[:, half * toks : (half + 1) * toks].astype(bf16)
    qx_ref[0, ext:] = pieces(jnp.where(valids, log_total, PENALTY))


def far_kernel(parts, width, heads, where_ref, *refs):
    blocks, w_ref, qx_ref, full_ref, att_a, att_b, kx_ref, vx_ref, near_ref, valid_ref, tok_ref = refs[:11]
    far, wt, total_ref, peak_ref, far_valid = refs[11:]
    head = pl.program_id(0)
    size = width // heads
    toks = blocks.shape[2]
    tile, ext = 2 * toks, size + 16

    @pl.when(head == 0)
    def _():
        code_index = lax.broadcasted_iota(jnp.int32, (16, tile), 0).astype(f32)
        for which in range(3):
            scale = size**-0.5 if which == 0 else 1.0
            wt[which * width : (which + 1) * width, :] = (w_ref[which, 0].astype(f32) * scale).T.astype(bf16)
        for p in range(parts):
            for j in range(0, GROUPS, 2):
                b = p * GROUPS + j
                span = slice(b * toks, (b + 2) * toks)
                both = jnp.concatenate([blocks[b], blocks[b + 1]], axis=1)
                tok_ref[:, span] = both[:width]
                first = 0 if p == 0 else width
                made = dot(wt[first:], both[:width], NN).astype(bf16)
                codes = both[width:].astype(f32)
                mask = jnp.where(code_index == codes[1:2], 0.0, -PENALTY).astype(bf16)
                for h in range(heads):
                    keys = width - first + h * size
                    kx_ref[h, :size, span] = made[keys : keys + size]
                    kx_ref[h, size:ext, span] = mask
                    kx_ref[h, ext:, span] = minus_rows(tile)
                    vx_ref[h, :size, span] = made[keys + width : keys + width + size]
                    vx_ref[h, size:, span] = minus_rows(tile)
                if p == 0:
                    target, flags = (near_ref, valid_ref) if j == 0 else (far, far_valid)
                    hot = jnp.where(code_index == codes[0:1], 1.0, 0.0).astype(bf16)
                    flags[...] = jnp.broadcast_to(codes[1:2], (8, tile))
                    for h in range(heads):
                        target[h, :size] = made[h * size : (h + 1) * size]
                        target[h, size:] = hot

    valids = far_valid[0:1, :] >= 0.0
    attend(head, size, far, kx_ref, vx_ref, tile, valids, qx_ref, full_ref, (att_a, att_b), total_ref, peak_ref)


def near_kernel(size, *refs):
    near_ref, valid_ref, kx_ref, vx_ref, qx_far, full_far, qx_ref, full_ref, att_a, att_b, total_ref, peak_ref = refs
    tile = qx_far.shape[2]
    valids = valid_ref[0:1, :] >= 0.0
    qx_ref[0, :, tile:] = qx_far[0]
    full_ref[:, tile:] = full_far[...]
    attend(
        pl.program_id(0),
        size,
        near_ref,
        kx_ref,
        vx_ref,
        0,
        valids,
        qx_ref.at[:, :, :tile],
        full_ref.at[:, :tile],
        (att_a, att_b),
        total_ref,
        peak_ref,
    )


def attention_outs(heads, size, toks, tiles):
    width, count = heads * size, 2 * toks * tiles
    specs = [
        pl.BlockSpec((1, size + 32, count), lambda h, *_: (h, 0, 0)),
        pl.BlockSpec((size, count), lambda h, *_: (h, 0)),
        pl.BlockSpec((size, toks), lambda h, *_: (h, 0)),
        pl.BlockSpec((size, toks), lambda h, *_: (h, 0)),
    ]
    shapes = [
        jax.ShapeDtypeStruct((heads, size + 32, count), bf16),
        jax.ShapeDtypeStruct((width, count), f32),
        jax.ShapeDtypeStruct((width, toks), bf16),
        jax.ShapeDtypeStruct((width, toks), bf16),
    ]
    scratch = [pltpu.VMEM((size + 16, 2 * toks), f32), pltpu.VMEM((1, 2 * toks), f32)]
    return specs, shapes, scratch


def far_attention(where, blocks, weights):
    count, _, toks = blocks.shape
    parts = count // GROUPS
    width = weights.shape[2]
    heads = HEADS // GROUPS
    size = width // heads
    tile, keys = 2 * toks, count * toks
    specs, shapes, scratch = attention_outs(heads, size, toks, 1)
    shared = [
        jax.ShapeDtypeStruct((heads, size + 32, keys), bf16),
        jax.ShapeDtypeStruct((heads, size + 16, keys), bf16),
        jax.ShapeDtypeStruct((heads, size + 16, tile), bf16),
        jax.ShapeDtypeStruct((8, tile), f32),
        pltpu.HBM((width, keys), bf16),
    ]
    return pl.pallas_call(
        functools.partial(far_kernel, parts, width, heads),
        name="attention_far",
        grid_spec=pltpu.PrefetchScalarGridSpec(
            num_scalar_prefetch=1,
            grid=(heads,),
            in_specs=[whole(blocks.shape), pl.BlockSpec((3, 1, width, width), lambda h, w: (0, w[0], 0, 0))],
            out_specs=specs + [whole(x.shape) for x in shared],
            scratch_shapes=[pltpu.VMEM((heads, size + 16, tile), bf16), pltpu.VMEM((3 * width, width), bf16)]
            + scratch
            + [pltpu.VMEM((8, tile), f32)],
        ),
        out_shape=shapes + shared,
        cost_estimate=CHEAP,
        compiler_params=pltpu.CompilerParams(vmem_limit_bytes=attention_vmem(keys)),
    )(where, blocks, weights)


def near_attention(near, valid, kx, vx, qx, full):
    heads, ext, tile = near.shape
    size = ext - 16
    far_specs, _, _ = attention_outs(heads, size, tile // 2, 1)
    specs, shapes, scratch = attention_outs(heads, size, tile // 2, 2)
    return pl.pallas_call(
        functools.partial(near_kernel, size),
        name="attention_near",
        grid=(heads,),
        in_specs=[whole(x.shape) for x in (near, valid, kx, vx)] + far_specs[:2],
        out_specs=specs,
        scratch_shapes=scratch,
        out_shape=shapes,
        cost_estimate=pl.CostEstimate(flops=2 * 10**9, bytes_accessed=10**6, transcendentals=0),
        compiler_params=pltpu.CompilerParams(vmem_limit_bytes=attention_vmem(kx.shape[2])),
    )(near, valid, kx, vx, qx, full)


def prepare_kernel(size, *refs):
    grads, full_ref, gx_ref = refs[:GROUPS], refs[GROUPS], refs[GROUPS + 1]
    toks = grads[0].shape[1]
    for head in range(gx_ref.shape[0]):
        rows = slice(head * size, (head + 1) * size)
        for j in range(GROUPS):
            span = slice(j * toks, (j + 1) * toks)
            grad = grads[j][rows, :]
            gx_ref[head, :size, span] = grad
            gx_ref[head, size:, span] = pieces(
                jnp.sum(grad.astype(f32) * full_ref[rows, span], axis=0, keepdims=True)
            )


def prepare(grads, full, size):
    width, count = full.shape
    out = jax.ShapeDtypeStruct((width // size, size + 16, count), bf16)
    return pl.pallas_call(
        functools.partial(prepare_kernel, size),
        name="prepare_backward",
        grid=(1,),
        in_specs=[whole(x.shape) for x in (*grads, full)],
        out_specs=whole(out.shape),
        out_shape=out,
        cost_estimate=pl.CostEstimate(flops=20 * 10**9, bytes_accessed=1, transcendentals=0),
        compiler_params=pltpu.CompilerParams(vmem_limit_bytes=SMALL_VMEM),
    )(*grads, full)


def backward_kernel(size, step, tile, ends, qx_ref, gx_ref, kx_ref, vx_ref, *refs):
    first, last = ends
    (dq_ref, dk_ref, dv_ref), total = refs[-4:-1] if last else refs[-3:], refs[-1] if last else refs[-3]
    total[...] = jnp.zeros_like(total) if first else refs[0][...]

    def keys(index, carry):
        kspan = pl.ds(pl.multiple_of(index * step, step), step)
        dk = dv = None
        for start in range(0, qx_ref.shape[2], tile):
            qspan = slice(start, start + tile)
            probs = jnp.exp(dot(qx_ref[0, :, qspan], kx_ref[0, :, kspan], TN))
            slopes = dot(gx_ref[0, :, qspan], vx_ref[0, :, kspan], TN)
            probs_low = probs.astype(bf16)
            grad_scores = (probs * slopes).astype(bf16)
            dv_new = dot(gx_ref[0, :size, qspan], probs_low, NN)
            dk_new = dot(qx_ref[0, :size, qspan], grad_scores, NN)
            total[:, qspan] += dot(kx_ref[0, :size, kspan], grad_scores, NT)
            dv = dv_new if dv is None else dv + dv_new
            dk = dk_new if dk is None else dk + dk_new
        dv_ref[:, kspan] = dv.astype(bf16)
        dk_ref[:, kspan] = dk.astype(bf16)
        return carry

    lax.fori_loop(0, kx_ref.shape[2] // step, keys, 0)
    if last:
        dq_ref[...] = (total[...] * size**-0.5).astype(bf16)


def backward_attention(head, part, cuts, qx, gx, kx, vx, dq=None):
    size, count = vx.shape[1] - 16, qx.shape[2]
    keys = vx.shape[2] // cuts
    first, last = part == 0, part == cuts - 1
    dq_shape, sum_shape = (size, count), (size, keys)
    return pl.pallas_call(
        functools.partial(backward_kernel, size, count // 2, count // 3, (first, last)),
        name="attention_backward",
        grid=(1,),
        in_specs=[
            pl.BlockSpec((1, size + 32, count), lambda i: (head, 0, 0)),
            pl.BlockSpec((1, size + 16, count), lambda i: (head, 0, 0)),
            pl.BlockSpec((1, size + 32, keys), lambda i: (head, 0, part)),
            pl.BlockSpec((1, size + 16, keys), lambda i: (head, 0, part)),
        ]
        + [whole(dq_shape)] * (not first),
        out_specs=[whole(dq_shape), whole(sum_shape), whole(sum_shape)],
        scratch_shapes=[pltpu.VMEM(dq_shape, f32)] * last,
        out_shape=[
            jax.ShapeDtypeStruct(dq_shape, bf16 if last else f32),
            jax.ShapeDtypeStruct(sum_shape, bf16),
            jax.ShapeDtypeStruct(sum_shape, bf16),
        ],
        cost_estimate=CHEAP,
        compiler_params=pltpu.CompilerParams(vmem_limit_bytes=attention_vmem(vx.shape[2])),
    )(qx, gx, kx, vx, *([] if first else [dq]))


def project_kernel(parts, heads, cuts, where_ref, *refs):
    tok_ref, wq_ref, wk_ref, wv_ref = refs[:4]
    refs = refs[4:]
    dq = jnp.concatenate([ref[...] for ref in refs[:heads]])
    piles, refs = refs[heads : heads + 2 * sum(cuts)], refs[heads + 2 * sum(cuts) :]
    starts = [sum(cuts[:h]) for h in range(heads + 1)]
    dk, dv = (
        jnp.concatenate(
            [jnp.concatenate([ref[...] for ref in pile[x:y]], axis=1) for x, y in zip(starts, starts[1:])]
        )
        for pile in (piles[: sum(cuts)], piles[sum(cuts) :])
    )
    backs, wgrads, scratch = refs[:parts], refs[parts : 2 * parts], refs[2 * parts]
    width, keys = tok_ref.shape
    count = keys // parts
    toks = count // GROUPS

    scratch[0] = dot(tok_ref[:, :count], dq, NT).astype(bf16)
    scratch[1] = dot(tok_ref[...], dk, NT).astype(bf16)
    scratch[2] = dot(tok_ref[...], dv, NT).astype(bf16)
    for p in reversed(range(parts)):
        span = slice(p * count, (p + 1) * count)
        back = dot(wk_ref[0], dk[:, span], NN) + dot(wv_ref[0], dv[:, span], NN)
        if p == 0:
            back += dot(wq_ref[0], dq, NN)
        for j in range(GROUPS):
            backs[p][j] = back[:, j * toks : (j + 1) * toks].astype(bf16)
    chunk = width // parts
    for p in range(parts):
        rows = pl.ds(pl.multiple_of(jnp.bitwise_xor(where_ref[1], p) * chunk, chunk), chunk)
        wgrads[p][...] = scratch[:, rows, :]


def project_back(where, parts, tok, weights, cuts, dqs, dks, dvs):
    width, keys = tok.shape
    toks = keys // parts // GROUPS
    heads = len(dqs)
    flat = [*dqs, *dks, *dvs]
    weight_spec = pl.BlockSpec((1, width, width), lambda i, w: (w[0], 0, 0))
    outs = [jax.ShapeDtypeStruct((GROUPS, width, toks), bf16)] * parts + [
        jax.ShapeDtypeStruct((3, width // parts, width), bf16)
    ] * parts
    results = pl.pallas_call(
        functools.partial(project_kernel, parts, heads, cuts),
        name="project_back",
        grid_spec=pltpu.PrefetchScalarGridSpec(
            num_scalar_prefetch=1,
            grid=(1,),
            in_specs=[whole(tok.shape)] + [weight_spec] * 3 + [whole(x.shape) for x in flat],
            out_specs=[whole(o.shape) for o in outs],
            scratch_shapes=[pltpu.VMEM((3, width, width), bf16)],
        ),
        out_shape=outs,
        cost_estimate=CHEAP,
        compiler_params=pltpu.CompilerParams(vmem_limit_bytes=attention_vmem(keys)),
    )(where, tok, *weights, *flat)
    return results[:parts], results[parts:]


def norm_parts(values):
    mean = jnp.mean(values, axis=0, keepdims=True)
    center = values - mean
    spread = jnp.mean(center * center, axis=0, keepdims=True)
    scale = lax.rsqrt(spread + 1e-06)
    return center * scale, scale


def norm_back(normal, scale, grad):
    mean = jnp.mean(grad, axis=0, keepdims=True)
    cross = jnp.mean(grad * normal, axis=0, keepdims=True)
    return (grad - mean - normal * cross) * scale


def middle_kernel(where_ref, *refs):
    slot_ref, far_ref, cot_ref, valid_ref, vec_ref, w_ref, fi_ref, fo_ref = refs[:8]
    refs = refs[8:]
    mixed_ref, first_grad_ref = refs[:2]
    sends = refs[2 : 2 + GROUPS]
    att, narrow_ref, wide_ref, first_low_ref, vec_out_ref = refs[2 + GROUPS : 7 + GROUPS]
    first_ref, slope_ref, second_ref, gfirst_ref, grad_att = refs[7 + GROUPS :]
    _, width, toks = slot_ref.shape
    model = width * GROUPS
    own_group = where_ref[0]
    vecs = vec_ref[...].T
    gain_one, bias_one = vecs[:, 0:1], vecs[:, 1:2]
    gain_two, bias_two = vecs[:, 2:3], vecs[:, 3:4]

    for j in range(GROUPS):
        start = pl.multiple_of(jnp.bitwise_xor(own_group, j) * width, width)
        att[pl.ds(start, width), :] = slot_ref[j] if j < 2 else far_ref[j - 2]
    tok = jnp.concatenate([slot_ref[2 + g] for g in range(GROUPS)])
    first_pre = tok.astype(f32) + dot(w_ref[...], att[...], TN)
    normal_one, scale_one = norm_parts(first_pre)
    first_ref[...] = normal_one
    first = normal_one * gain_one + bias_one
    narrow_ref[0] = first.astype(bf16)
    for g in range(GROUPS):
        mine = slice(g * width, (g + 1) * width)
        pre = dot(fi_ref[g], narrow_ref[0, mine, :], TN)
        phi = 0.5 * (1.0 + lax.erf(pre * 0.5**0.5))
        density = jnp.exp(-0.5 * pre * pre) * 0.3989422804014327
        wide_ref[1, g] = (pre * phi).astype(bf16)
        slope_ref[g] = phi + pre * density
        second_ref[mine, :] = (first_ref[mine, :] * gain_one[mine] + bias_one[mine]) + dot(fo_ref[g], wide_ref[1, g], NN)
    normal_two, scale_two = norm_parts(second_ref[...])
    mixed_ref[0] = (normal_two * gain_two + bias_two).T
    cot = cot_ref[0].T
    grad_gain_two = jnp.sum(cot * normal_two, axis=1, keepdims=True)
    grad_bias_two = jnp.sum(cot, axis=1, keepdims=True)
    grad_second = norm_back(normal_two, scale_two, cot * gain_two)
    second_ref[...] = grad_second
    grad_low = grad_second.astype(bf16)
    narrow_ref[1] = grad_low
    for g in range(GROUPS):
        mine = slice(g * width, (g + 1) * width)
        ghp = (dot(fo_ref[g], grad_low[mine, :], TN) * slope_ref[g]).astype(bf16)
        wide_ref[0, g] = ghp
        gfirst_ref[mine, :] = second_ref[mine, :] + dot(fi_ref[g], ghp, NN)
    grad_first = gfirst_ref[...]
    normal_one = first_ref[...]
    grad_gain_one = jnp.sum(grad_first * normal_one, axis=1, keepdims=True)
    grad_bias_one = jnp.sum(grad_first, axis=1, keepdims=True)
    first_grad = norm_back(normal_one, scale_one, grad_first * gain_one)
    first_grad_ref[...] = first_grad
    first_low = first_grad.astype(bf16)
    first_low_ref[...] = first_low
    grad_att[...] = jnp.where(valid_ref[...] == 1, dot(w_ref[...], first_low, NN), 0.0).astype(bf16)
    for j in range(GROUPS):
        start = pl.multiple_of(jnp.bitwise_xor(own_group, j) * width, width)
        sends[j][...] = grad_att[pl.ds(start, width), :]

    lane = lax.broadcasted_iota(jnp.int32, (model, 128), 1)
    vectors = jnp.where(lane == 0, grad_gain_one, 0.0)
    vectors = jnp.where(lane == 1, grad_bias_one, vectors)
    vectors = jnp.where(lane == 2, grad_gain_two, vectors)
    vectors = jnp.where(lane == 3, grad_bias_two, vectors)
    vec_out_ref[...] = vectors.astype(bf16)


def middle(where, slots, far, cotangent, valid, vecs, out_weight, ffn_in, ffn_out_t):
    _, width, toks = slots.shape
    model = width * GROUPS
    wide = ffn_in.shape[2]
    args = (slots, far, cotangent, valid, vecs, out_weight, ffn_in, ffn_out_t)
    outs = (
        [jax.ShapeDtypeStruct((1, toks, model), f32), pltpu.HBM((model, toks), f32)]
        + [jax.ShapeDtypeStruct((width, toks), bf16)] * GROUPS
        + [
            jax.ShapeDtypeStruct((model, toks), bf16),
            jax.ShapeDtypeStruct((2, model, toks), bf16),
            jax.ShapeDtypeStruct((2, GROUPS, wide, toks), bf16),
            jax.ShapeDtypeStruct((model, toks), bf16),
            jax.ShapeDtypeStruct((model, 128), bf16),
        ]
    )
    results = pl.pallas_call(
        middle_kernel,
        name="middle",
        grid_spec=pltpu.PrefetchScalarGridSpec(
            num_scalar_prefetch=1,
            grid=(1,),
            in_specs=[whole(a.shape) for a in args],
            out_specs=[whole(o.shape) for o in outs],
            scratch_shapes=[
                pltpu.VMEM((model, toks), f32),
                pltpu.VMEM((GROUPS, wide, toks), f32),
                pltpu.VMEM((model, toks), f32),
                pltpu.VMEM((model, toks), f32),
                pltpu.VMEM((model, toks), bf16),
            ],
        ),
        out_shape=outs,
        cost_estimate=CHEAP,
        compiler_params=pltpu.CompilerParams(vmem_limit_bytes=VMEM_BYTES),
    )(where, *args)
    return results[0], results[1], results[2 : 2 + GROUPS], results[2 + GROUPS :]


def swapped(slot, odd):
    return jnp.where(odd, slot, (slot % 2) * 2 + slot // 2)


def outer_kernel(parts, slot, where_ref, att, narrow_ref, wide_ref, first_low_ref, vec_ref, near_ref, far_ref, scratch):
    model = att.shape[0]
    width = model // GROUPS
    wide = wide_ref.shape[2]
    half = parts // 2
    own_group, part = where_ref[0], jnp.bitwise_xor(where_ref[1], slot)
    ffn_rows, out_rows = width // half, model // (parts * GROUPS)
    array, piece = part // half, part % half
    tiles, wide_tiles = model // 128, wide // 128

    out_start = pl.multiple_of(part * (model // parts), model // parts)
    scratch[...] = dot(att[pl.ds(out_start, model // parts), :], first_low_ref[...], NT).astype(bf16)
    base = wide_tiles * ffn_rows
    for m in range(GROUPS):
        target, index = (near_ref, far_ref)[m // 2], m % 2
        group = jnp.bitwise_xor(own_group, swapped(m, part % 2 == 1))
        start = pl.multiple_of(group * width + piece * ffn_rows, ffn_rows)
        made = dot(narrow_ref[array, pl.ds(start, ffn_rows), :], wide_ref[array, group], NT).astype(bf16)
        for t in range(wide_tiles):
            target[index, t * ffn_rows : (t + 1) * ffn_rows] = made[:, t * 128 : (t + 1) * 128]
        rows = pl.ds(pl.multiple_of(group * out_rows, out_rows), out_rows)
        for t in range(tiles):
            span = slice(base + t * out_rows, base + (t + 1) * out_rows)
            target[index, span] = scratch[rows, t * 128 : (t + 1) * 128]
        rows = pl.ds(pl.multiple_of(out_start + group * out_rows, out_rows), out_rows)
        target[index, base + tiles * out_rows :] = vec_ref[rows, :]


def outer_products(where, parts, slot, kept):
    att, narrow, wide_pair, _, _ = kept
    model = att.shape[0]
    wide = wide_pair.shape[2]
    rows = (wide // 128) * (model // GROUPS // (parts // 2)) + (model // 128 + 1) * (model // (parts * GROUPS))
    outs = [jax.ShapeDtypeStruct((2, rows, 128), bf16)] * 2
    return pl.pallas_call(
        functools.partial(outer_kernel, parts, slot),
        name="outer_products",
        grid_spec=pltpu.PrefetchScalarGridSpec(
            num_scalar_prefetch=1,
            grid=(1,),
            in_specs=[whole(a.shape) for a in kept],
            out_specs=[whole(o.shape) for o in outs],
            scratch_shapes=[pltpu.VMEM((model // parts, model), bf16)],
        ),
        out_shape=outs,
        cost_estimate=CHEAP,
        compiler_params=pltpu.CompilerParams(vmem_limit_bytes=SMALL_VMEM),
    )(where, *kept)


def row_distances(depth):
    steps = depth.bit_length() - 1
    even = [sum(((m >> (steps - 1 - i)) & 1) << i for i in range(steps)) for m in range(depth)]
    return even, list(range(depth))


def weight_grad_kernel(parts, depth, model, wide, where_ref, *refs):
    slots = refs[:parts]
    out_ref, in_ref, ffn_out_ref, vec_ref, scratch, vec_scratch = refs[parts:]
    step = pl.program_id(0)
    group = jnp.bitwise_xor(step, where_ref[0])
    piece = slots[0].shape[2]
    width = model // GROUPS
    half = parts // 2
    ffn_rows, out_rows = width // half, model // (parts * GROUPS)
    tiles, wide_tiles = model // 128, wide // 128
    even, odd = row_distances(depth)
    for p in range(parts):
        part = jnp.bitwise_xor(where_ref[1], p)
        for z in range(depth):
            distance = jnp.where(part % 2 == 1, odd[z], even[z])
            scratch[part, jnp.bitwise_xor(where_ref[2], distance)] = slots[p][0, z].astype(f32)

    def rows(part, first, count):
        last = first + count
        cuts = [first] + [c for c in range(0, depth * piece, piece) if first < c < last] + [last]
        return jnp.concatenate(
            [scratch[part, x // piece, x % piece : x % piece + y - x, :] for x, y in zip(cuts, cuts[1:])]
        )

    base = wide_tiles * ffn_rows
    for part in range(parts):
        target = in_ref if part < half else ffn_out_ref
        mine = slice((part % half) * ffn_rows, (part % half + 1) * ffn_rows)
        for t in range(wide_tiles):
            target[0, mine, t * 128 : (t + 1) * 128] = rows(part, t * ffn_rows, ffn_rows)
        for t in range(tiles):
            out_ref[part, 0, :, t * 128 : (t + 1) * 128] = rows(part, base + t * out_rows, out_rows)
        start = pl.multiple_of(part * (model // parts) + group * out_rows, out_rows)
        vec_scratch[pl.ds(start, out_rows), :] = rows(part, base + tiles * out_rows, out_rows)

    @pl.when(step == GROUPS - 1)
    def _():
        vec_ref[...] = vec_scratch[...].T[:8]


def weight_grads(where, slots, model, wide):
    parts = len(slots)
    _, depth, piece, _ = slots[0].shape
    width = model // GROUPS
    out_rows = model // (parts * GROUPS)

    def slot_spec(p):
        def place(j, w):
            return (swapped(j, jnp.bitwise_xor(w[1], p) % 2 == 1), 0, 0, 0)

        return pl.BlockSpec((1, depth, piece, 128), place)

    out, ffn_in, ffn_out_t, vectors = pl.pallas_call(
        functools.partial(weight_grad_kernel, parts, depth, model, wide),
        name="weight_grads",
        grid_spec=pltpu.PrefetchScalarGridSpec(
            num_scalar_prefetch=1,
            grid=(GROUPS,),
            in_specs=[slot_spec(p) for p in range(parts)],
            out_specs=[
                pl.BlockSpec((parts, 1, out_rows, model), lambda j, w: (0, jnp.bitwise_xor(j, w[0]), 0, 0)),
                pl.BlockSpec((1, width, wide), lambda j, w: (jnp.bitwise_xor(j, w[0]), 0, 0)),
                pl.BlockSpec((1, width, wide), lambda j, w: (jnp.bitwise_xor(j, w[0]), 0, 0)),
                pl.BlockSpec((8, model), lambda j, w: (0, 0)),
            ],
            scratch_shapes=[pltpu.VMEM((parts, depth, piece, 128), f32), pltpu.VMEM((model, 128), f32)],
        ),
        out_shape=[
            jax.ShapeDtypeStruct((parts, GROUPS, out_rows, model), f32),
            jax.ShapeDtypeStruct((GROUPS, width, wide), f32),
            jax.ShapeDtypeStruct((GROUPS, width, wide), f32),
            jax.ShapeDtypeStruct((8, model), f32),
        ],
        cost_estimate=CHEAP,
        compiler_params=pltpu.CompilerParams(vmem_limit_bytes=SMALL_VMEM),
    )(where, *slots)
    return out.reshape(model, model), ffn_in, ffn_out_t, vectors


def join_kernel(where_ref, *refs):
    slots, (first_grad_ref, out_ref) = refs[:GROUPS], refs[GROUPS:]
    width = slots[0].shape[0]
    for j in range(GROUPS):
        mine = pl.ds(pl.multiple_of(jnp.bitwise_xor(where_ref[0], j) * width, width), width)
        out_ref[mine, :] = first_grad_ref[mine, :] + slots[j][...].astype(f32)


def join(where, slots, first_grad):
    args = (*slots, first_grad)
    return pl.pallas_call(
        join_kernel,
        name="join",
        grid_spec=pltpu.PrefetchScalarGridSpec(
            num_scalar_prefetch=1,
            grid=(1,),
            in_specs=[whole(a.shape) for a in args],
            out_specs=whole(first_grad.shape),
        ),
        out_shape=jax.ShapeDtypeStruct(first_grad.shape, f32),
        cost_estimate=pl.CostEstimate(flops=2 * 10**9, bytes_accessed=1, transcendentals=0),
        compiler_params=pltpu.CompilerParams(vmem_limit_bytes=SMALL_VMEM),
    )(where, *args)


def finish_kernel(parts, where_ref, *refs):
    total_ref, thirds, (out_ref, *outs) = refs[0], refs[1 : 1 + parts], refs[1 + parts :]
    out_ref[0] = total_ref[...].T
    for p in range(parts):
        chunk = thirds[p].shape[2]
        part = jnp.bitwise_xor(where_ref[1], p)
        rows = pl.ds(pl.multiple_of(part * chunk, chunk), chunk)
        for m in range(GROUPS):
            group = jnp.bitwise_xor(where_ref[0], swapped(m, part % 2 == 1))
            for which in range(3):
                outs[which][group, rows, :] = thirds[p][m, which].astype(f32)


def finish(where, total, thirds):
    model, toks = total.shape
    width = model // GROUPS
    args = (total, *thirds)
    outs = [jax.ShapeDtypeStruct((1, toks, model), f32)] + [
        jax.ShapeDtypeStruct((GROUPS, width, width), f32)
    ] * 3
    return pl.pallas_call(
        functools.partial(finish_kernel, len(thirds)),
        name="finish",
        grid_spec=pltpu.PrefetchScalarGridSpec(
            num_scalar_prefetch=1,
            grid=(1,),
            in_specs=[whole(a.shape) for a in args],
            out_specs=[whole(o.shape) for o in outs],
        ),
        out_shape=outs,
        cost_estimate=CHEAP,
        compiler_params=pltpu.CompilerParams(vmem_limit_bytes=SMALL_VMEM),
    )(where, *args)


def add_low(terms):
    total = terms[0].astype(f32)
    for term in terms[1:]:
        total = total + term.astype(f32)
    return total.astype(bf16)


def shards(
    tokens,
    segment_ids,
    valid_tokens,
    q_weight,
    k_weight,
    v_weight,
    out_weight,
    gain_one,
    bias_one,
    ffn_in,
    ffn_out,
    gain_two,
    bias_two,
    cotangent,
):
    seq = lax.axis_size("seq")
    depth = lax.axis_size("rows")
    parts = seq // GROUPS
    _, toks, model = tokens.shape
    width = model // GROUPS
    wide = ffn_in.shape[2]
    place = lax.axis_index("seq")
    own_group, own_part = place // parts, place % parts
    own_row = lax.axis_index("rows")
    where = jnp.stack([own_group, own_part, own_row]).astype(jnp.int32)

    def swap(value, distance):
        return lax.ppermute(value, "seq", [(k, k ^ distance) for k in range(seq)])

    def across(value):
        return [value[0]] + [swap(value[j], parts * j) for j in range(1, GROUPS)]

    def group_swap(value, step):
        apart = [(1, 2), (2, 1)][step]
        return lax.ppermute(value, "seq", [(k, k ^ parts * apart[k % parts % 2]) for k in range(seq)])

    row_steps = depth.bit_length() - 1

    def row_swap(value, step):
        pairs = []
        for k in range(seq):
            distance = 1 << (row_steps - 1 - step if k % parts % 2 else step)
            pairs += [(k * depth + z, k * depth + (z ^ distance)) for z in range(depth)]
        return lax.ppermute(value, ("seq", "rows"), pairs)

    grouped, sends = arrange(where, tokens, segment_ids, valid_tokens)
    mine = across(sends)
    others = [swap(jnp.stack(mine), p) for p in range(1, parts)]
    blocks = jnp.stack(mine + [x[j] for x in others for j in range(GROUPS)])

    qx_far, full_far, att_c, att_d, kx, vx, near, near_valid, tok = far_attention(
        where, blocks, jnp.stack([q_weight, k_weight, v_weight])
    )
    att_far = jnp.stack([swap(att_c, parts * 2), swap(att_d, parts * 3)])
    qx, full, att_a, att_b = near_attention(near, near_valid, kx, vx, qx_far, full_far)
    att_b = swap(att_b, parts)
    slots = jnp.concatenate([att_a[None], att_b[None], grouped])
    vecs = jnp.pad(jnp.stack(after([gain_one, bias_one, gain_two, bias_two], att_a)), ((0, 4), (0, 0)))
    mixed, first_grad, sends, kept = middle(
        where, slots, att_far, cotangent, valid_tokens, vecs, out_weight, ffn_in, jnp.swapaxes(ffn_out, 1, 2)
    )
    grads = across(sends)

    pays = [outer_products(where, parts, p, kept) for p in range(1, parts)]
    moved = [[swap(x, p) for x in pays[p - 1]] for p in range(1, parts)]
    pay = outer_products(where, parts, 0, after(kept, pays))
    gx = prepare(after(grads, pay), full, model // HEADS)
    moved = after(moved, gx)
    low = add_low([pay[0]] + [x[0] for x in moved])
    high = add_low([pay[1]] + [x[1] for x in moved])

    cuts = [1, 2, 2]
    calls = [(head, part) for head, count in enumerate(cuts) for part in range(count)]
    dqs, dks, dvs = [], [], []

    def work(*ready):
        head, part = calls.pop(0)
        dq, dk, dv = backward_attention(
            head,
            part,
            cuts[head],
            qx,
            after(gx, ready),
            kx,
            vx,
            dqs.pop() if part else None,
        )
        dqs.append(dq)
        dks.append(dk)
        dvs.append(dv)
        return dq

    moved = group_swap(high, 0)
    moved = after(moved, work(high, low))
    low, high = add_low([low[0], moved[0]]), add_low([low[1], moved[1]])
    moved = group_swap(high, 1)
    piece = add_low([low, after(moved, work(high, low))]).reshape(depth, -1, 128)
    even, odd = row_distances(depth)
    picks = [own_row ^ jnp.where(own_part % 2 == 1, odd[m], even[m]) for m in range(depth)]
    piece = jnp.stack([lax.dynamic_index_in_dim(piece, z, 0, False) for z in picks])
    for step in range(row_steps):
        count = piece.shape[0] // 2
        low, high = piece[:count], piece[count:]
        moved = row_swap(high, step)
        if len(calls) > 1:
            moved = after(moved, work(high, low))
        piece = add_low([low, moved])
    moved = row_swap(piece, row_steps - 1)
    while calls:
        done = work(piece)
        moved, dqs[-1] = after((moved, dqs[-1]), done)
    piece = jnp.concatenate([piece, moved])
    step = row_steps - 2
    moved = row_swap(piece, step)
    backs, wgrads = project_back(where, parts, tok, (q_weight, k_weight, v_weight), cuts, after(dqs, piece), dks, dvs)
    piece = jnp.concatenate([piece, moved])
    for step in reversed(range(row_steps - 2)):
        piece = jnp.concatenate([piece, row_swap(piece, step)])
    wgrads, backs, piece = after((wgrads, backs, piece[None]), piece)
    swaps = [[swap(x[p], p) for p in range(1, parts)] for x in (wgrads, backs)]
    moved = group_swap(piece, 1)
    quarter, back_sum = add_low([wgrads[0]] + swaps[0]), add_low([backs[0]] + swaps[1])
    back_first = swap(back_sum[3], parts * 3)
    for step in range(row_steps - 1):
        quarter = add_low([quarter, row_swap(quarter, step)])
    piece = jnp.concatenate([piece, moved])
    quarter, back_sum, back_first, piece = after((quarter, back_sum, back_first, piece), quarter)
    moved = group_swap(piece, 0)
    quarter = add_low([quarter, row_swap(quarter, row_steps - 1)])
    quarter = jnp.stack([quarter, group_swap(quarter, 1)])
    piece = jnp.concatenate([piece, moved])
    quarter, back_sum, piece = after((quarter, back_sum, piece), quarter)
    slots = [piece] + [swap(piece, p) for p in range(1, parts)]
    back_moved = [back_sum[0]] + [swap(back_sum[j], parts * j) for j in (1, 2)] + [back_first]
    moved = group_swap(quarter, 0)
    grad_out_weight, grad_ffn_in, grad_ffn_out_t, vectors = weight_grads(where, slots, model, wide)
    quarter = jnp.concatenate([quarter, after(moved, vectors)])
    total = join(where, after(back_moved, vectors), first_grad)
    thirds = [quarter] + [swap(quarter, p) for p in range(1, parts)]
    grad_tokens, grad_q, grad_k, grad_v = finish(where, total, thirds)

    return (
        mixed,
        grad_tokens,
        grad_q,
        grad_k,
        grad_v,
        grad_out_weight,
        vectors[0],
        vectors[1],
        grad_ffn_in,
        jnp.swapaxes(grad_ffn_out_t, 1, 2),
        vectors[2],
        vectors[3],
    )


def solution(mesh):
    tokens = P("rows", "seq", None)
    flags = P("rows", "seq")
    in_specs = (tokens, flags, flags) + (P(),) * 10 + (tokens,)
    out_specs = (tokens, tokens) + (P(),) * 10
    return jax.shard_map(shards, mesh=mesh, in_specs=in_specs, out_specs=out_specs, check_vma=False)
```
